32 devices in a mesh: seq: 8 (over z, y), tensor: 2 (over core), dp: 2 (over x).
Axes of the slice: x: 2, y: 2, z: 4, core: 2. Of those that a mesh axis runs over, the one named last changes fastest.
Arguments:
- inputs: bfloat16 [2, 6144, 1536], P('dp', 'seq', 'tensor'), may hold values from -6 to 6
- lengths: int32 [2], P('dp'), may hold values from 1536 to 6144, as said below
- cotangent: bfloat16 [2, 6144, 1536], P('dp', 'seq', 'tensor'), may hold values from -6 to 6
- w_value: bfloat16 [1536, 1536], P(None, 'tensor'), may hold values from -0.15625 to 0.15625
- w_gate: bfloat16 [1536, 1536], P(None, 'tensor'), may hold values from -0.15625 to 0.15625
- kernel: bfloat16 [31, 1536], P(None, 'tensor'), may hold values from -1 to 1
- w_out: bfloat16 [1536, 1536], P('tensor'), may hold values from -0.15625 to 0.15625
Outputs:
- output: bfloat16 [2, 6144, 1536], P('dp', 'seq', 'tensor')
- input_gradient: bfloat16 [2, 6144, 1536], P('dp', 'seq', 'tensor')
- value_grad: float32 [1536, 1536], P(('seq', 'dp'), 'tensor')
- gate_grad: float32 [1536, 1536], P(('seq', 'dp'), 'tensor')
- kernel_grad: float32 [31, 1536], P(None, 'tensor')
- out_grad: float32 [1536, 1536], P('tensor', ('seq', 'dp'))
The draws below stay inside these ranges and needn't reach their ends.
Inputs may be any that keep to these rules, and one draw needn't show every extreme that they name: `lengths`: in every draw some utterance has all 6144 frames valid.
All inputs are finite; a program needn't handle non-finite values.
Results may differ from the reference program's by a relative error of at most 0.009.
Values may be sent and summed in bfloat16 or wider, within the bound.
No kernel may reach another device: no remote copies, remote signals or barrier semaphores. Data moves between devices by JAX's collectives and lax.ppermute only.
A program may use at most 128 MiB of HBM per device.

```python
import jax
import jax.numpy as jnp
from jax import lax

D = 1536
KERNEL = 31
LENGTH = 6144
UTTS = 2


def draw_lengths(key, part):
    first, second = jax.random.split(jax.random.fold_in(key, 17))
    drawn = jax.random.randint(first, (UTTS,), LENGTH // 4, LENGTH + 1, dtype=jnp.int32)
    chosen = jax.random.randint(second, (), 0, UTTS, dtype=jnp.int32)
    return jnp.where(jnp.arange(UTTS, dtype=jnp.int32) == chosen, jnp.int32(LENGTH), drawn)


def raised(values, rng, source, target, parts, factor):
    owner, partner = [(jnp.arange(values.shape[position]) // (values.shape[position] // parts)).reshape([-1 if axis == position else 1 for axis in range(values.ndim)]) for position in (source, target)]
    chosen = jax.random.permutation(rng, parts)[partner]
    strong = (owner == chosen) | (owner == (partner + parts // 2) % parts)
    return jnp.where(strong, factor * values, values)


def shard_levels(own_key, shape, cuts, least, top_value):
    def one(position, parts):
        heights = jax.random.uniform(jax.random.fold_in(jax.random.fold_in(own_key, 6), position), (parts,), jnp.float32, least / len(cuts), top_value / len(cuts))
        return jnp.repeat(jnp.exp(heights), shape[position] // parts).reshape((-1,) + (1,) * (len(shape) - position - 1))

    gain = one(*cuts[0])
    for cut in cuts[1:]:
        gain = gain * one(*cut)
    return gain


def noise(own_key, dims, deviation, limit, shards=(), held_as=jnp.bfloat16):
    values = deviation * jax.random.normal(own_key, dims, jnp.float32)
    if shards:
        values = values * shard_levels(own_key, dims, shards, -0.22, 0.18)
    return jnp.clip(values, -limit, limit).astype(held_as)


def bell_draw_with(own_key, extent, width, limit, shards, heavy, kind=jnp.bfloat16):
    result = width * jax.random.normal(own_key, extent, jnp.float32)
    if shards:
        result = result * shard_levels(own_key, extent, shards, -0.22, 0.18)
    return jnp.clip(raised(result, jax.random.fold_in(own_key, 3), *heavy), -limit, limit).astype(kind)


def setup_inputs(seed: int = 0) -> dict:
    streams_of = jax.random.split(jax.random.key(seed), 8)
    inputs = bell_draw_with(streams_of[0], (UTTS, LENGTH, D), 1.0, 6.0, ((0, 2), (1, 8), (2, 2)), (1, 2, 8, 2.0))
    lengths = draw_lengths(jax.random.fold_in(streams_of[7], 71), 0)
    cotangent = bell_draw_with(streams_of[2], (UTTS, LENGTH, D), 1.0, 6.0, ((0, 2), (1, 8), (2, 2)), (1, 2, 8, 2.0))
    w_value = noise(streams_of[3], (D, D), D ** -0.5, 0.15625, ((1, 2),))
    w_gate = noise(streams_of[4], (D, D), D ** -0.5, 0.15625, ((1, 2),))
    kernel = noise(streams_of[5], (KERNEL, D), KERNEL ** -0.5, 1.0, ((1, 2),))
    w_out = noise(streams_of[6], (D, D), D ** -0.5, 0.15625, ((0, 2),))
    return dict(inputs=inputs, lengths=lengths, cotangent=cotangent, w_value=w_value, w_gate=w_gate, kernel=kernel, w_out=w_out)


epsilon = 1e-05

def layer_normalizer(values):
    center = values - lax.optimization_barrier(jnp.mean(values, axis=-1, keepdims=True))
    inverse = lax.rsqrt(lax.optimization_barrier(jnp.mean(center * center, axis=-1, keepdims=True)) + epsilon)
    return (center * inverse, inverse)

def utterance(frame_total, length, cotangent, w_value, w_gate, kernel, w_out):
    count = frame_total.shape[0]
    half = (KERNEL - 1) // 2
    valid = (jnp.arange(count, dtype=jnp.int32) < length).astype(jnp.float32)[:, None]
    taps = kernel.astype(jnp.float32)
    centered_scaled, inverse_deviation_one = layer_normalizer(frame_total.astype(jnp.float32))
    normalized_rows = centered_scaled.astype(jnp.bfloat16)
    values = jnp.dot(normalized_rows, w_value, preferred_element_type=jnp.float32)
    gates = jnp.dot(normalized_rows, w_gate, preferred_element_type=jnp.float32)
    sigma = jax.nn.sigmoid(gates)
    hidden = (values * sigma * valid).astype(jnp.bfloat16)
    padded = jnp.pad(hidden, ((half, half), (0, 0))).astype(jnp.float32)
    conv = jnp.zeros((count, hidden.shape[1]), jnp.float32)
    for offset in range(KERNEL):
        conv = conv + padded[offset:offset + count] * taps[offset]
    zhat, rstd_two = layer_normalizer(conv)
    swish_gate = jax.nn.sigmoid(zhat)
    swished = (zhat * swish_gate).astype(jnp.bfloat16)
    output = (frame_total.astype(jnp.float32) + jnp.dot(swished, w_out, preferred_element_type=jnp.float32)).astype(jnp.bfloat16)
    out_grad = jnp.dot(swished.T, cotangent, preferred_element_type=jnp.float32)
    dswish = jnp.dot(cotangent, w_out.T, preferred_element_type=jnp.float32)
    dswish = dswish * (swish_gate + zhat * swish_gate * (1.0 - swish_gate))
    dconv = rstd_two * (dswish - lax.optimization_barrier(jnp.mean(dswish, axis=-1, keepdims=True)) - zhat * lax.optimization_barrier(jnp.mean(dswish * zhat, axis=-1, keepdims=True)))
    dconv = dconv.astype(jnp.bfloat16)
    slope = dconv.astype(jnp.float32)
    kernel_grad = jnp.stack([lax.optimization_barrier(jnp.sum(padded[offset:offset + count] * slope, axis=0)) for offset in range(KERNEL)])
    slope_pad = jnp.pad(slope, ((half, half), (0, 0)))
    dhidden = jnp.zeros((count, hidden.shape[1]), jnp.float32)
    for offset in range(KERNEL):
        dhidden = dhidden + slope_pad[2 * half - offset:2 * half - offset + count] * taps[offset]
    dhidden = dhidden * valid
    dvalues = (dhidden * sigma).astype(jnp.bfloat16)
    dgates = (dhidden * values * sigma * (1.0 - sigma)).astype(jnp.bfloat16)
    value_grad = jnp.dot(normalized_rows.T, dvalues, preferred_element_type=jnp.float32)
    gate_grad = jnp.dot(normalized_rows.T, dgates, preferred_element_type=jnp.float32)
    normalized_grad = jnp.dot(dvalues, w_value.T, preferred_element_type=jnp.float32) + jnp.dot(dgates, w_gate.T, preferred_element_type=jnp.float32)
    input_gradient = cotangent.astype(jnp.float32) + inverse_deviation_one * (normalized_grad - lax.optimization_barrier(jnp.mean(normalized_grad, axis=-1, keepdims=True)) - centered_scaled * lax.optimization_barrier(jnp.mean(normalized_grad * centered_scaled, axis=-1, keepdims=True)))
    return (output, input_gradient.astype(jnp.bfloat16), value_grad, gate_grad, kernel_grad, out_grad)

def reference(inputs, lengths, cotangent, w_value, w_gate, kernel, w_out):

    def single(packed):
        return utterance(packed[0], packed[1], packed[2], w_value, w_gate, kernel, w_out)
    output, input_gradient, value_grad, gate_grad, kernel_grad, out_grad = lax.map(single, (inputs, lengths, cotangent))
    return (output, input_gradient, lax.optimization_barrier(jnp.sum(value_grad, axis=0)), lax.optimization_barrier(jnp.sum(gate_grad, axis=0)), lax.optimization_barrier(jnp.sum(kernel_grad, axis=0)), lax.optimization_barrier(jnp.sum(out_grad, axis=0)))
```

```python
import jax
import jax.numpy as jnp
from jax import lax
from jax.sharding import PartitionSpec as P

epsilon = 1e-05


def swap(value, axis, bit=0):
    size = lax.axis_size(axis)
    return lax.ppermute(value, axis, [(i, i ^ (1 << bit)) for i in range(size)])


def bits_of(axis):
    return [(axis, b) for b in range(lax.axis_size(axis).bit_length() - 1)]


def pair_sum(value):
    return value + swap(value, "tensor")


def both_halves(own, other, dim):
    first = lax.axis_index("tensor") == 0
    return jnp.where(
        first,
        jnp.concatenate([own, other], axis=dim),
        jnp.concatenate([other, own], axis=dim),
    )


def padded_2(shard, width):
    peers, length = (lax.axis_size("seq"), shard.shape[0])
    up = [(i, (i + 1) % peers) for i in range(peers - 1)]
    down = [(j, i) for i, j in up]
    before = lax.ppermute(shard[length - width :], "seq", up)
    after = lax.ppermute(shard[:width], "seq", down)
    return jnp.concatenate([before, shard, after], axis=0)


def layer_normalizer(values):
    center = values - jnp.mean(values, axis=-1, keepdims=True)
    inverse = lax.rsqrt(jnp.mean(center * center, axis=-1, keepdims=True) + epsilon)
    return (center * inverse, inverse)


class Halver:
    def __init__(self, terms):
        self.bits = bits_of("seq")[::-1] + bits_of("dp")[::-1]
        blocks = 1 << len(self.bits)
        rows = terms.shape[0] // blocks
        self.value = terms.reshape((2,) * len(self.bits) + (rows, terms.shape[1]))

    def step(self, bit):
        dim = self.bits.index(bit)
        mine = (lax.axis_index(bit[0]) >> bit[1]) & 1
        send = lax.dynamic_index_in_dim(self.value, 1 - mine, dim, keepdims=False)
        keep = lax.dynamic_index_in_dim(self.value, mine, dim, keepdims=False)
        shape = send.shape
        got = swap(send.reshape(-1, shape[-1]), *bit).reshape(shape)
        self.value = keep.astype(jnp.float32) + got.astype(jnp.float32)
        self.bits = self.bits[:dim] + self.bits[dim + 1 :]
        if self.bits:
            self.value = self.value.astype(jnp.bfloat16)


def scatter_sum(terms):
    thirds = [Halver(t) for t in jnp.split(terms, 3, axis=1)]
    every = bits_of("dp") + bits_of("seq")
    turning, rest = every[:3], every[3:]
    for phase in range(len(turning)):
        for i, third in enumerate(thirds):
            third.step(turning[(i + phase) % len(turning)])
    merged = thirds[0]
    merged.value = jnp.concatenate([t.value for t in thirds], axis=-1)
    for bit in rest:
        merged.step(bit)
    return merged.value


def shards(inputs, lengths, cotangent, w_value, w_gate, kernel, w_out):
    frame_total = inputs[0]
    count = frame_total.shape[0]
    channel_total = frame_total.shape[1]
    channel_width = channel_total * lax.axis_size("tensor")
    taps_count = kernel.shape[0]
    half = (taps_count - 1) // 2
    tensor_position = lax.axis_index("tensor")
    first_frame = lax.axis_index("seq") * count
    positions = first_frame + jnp.arange(count, dtype=jnp.int32)
    valid = (positions < lengths[0]).astype(jnp.float32)[:, None]
    taps = kernel.astype(jnp.float32)
    upstream = cotangent[0]
    complete_rows = both_halves(frame_total, swap(frame_total, "tensor"), 1)
    upstream_whole = both_halves(upstream, swap(upstream, "tensor"), 1)
    centered_scaled, inverse_deviation_one = layer_normalizer(complete_rows.astype(jnp.float32))
    normalized_rows = centered_scaled.astype(jnp.bfloat16)
    values = jnp.dot(normalized_rows, w_value, preferred_element_type=jnp.float32)
    gates = jnp.dot(normalized_rows, w_gate, preferred_element_type=jnp.float32)
    sigma = jax.nn.sigmoid(gates)
    hidden = (values * sigma * valid).astype(jnp.bfloat16)
    padded = padded_2(hidden, half).astype(jnp.float32)
    conv = jnp.zeros((count, channel_total), jnp.float32)
    for offset in range(taps_count):
        conv = conv + padded[offset : offset + count] * taps[offset]
    conv_sums = pair_sum(jnp.stack([jnp.sum(conv, axis=-1), jnp.sum(conv * conv, axis=-1)]))
    conv_mean = (conv_sums[0] / channel_width)[:, None]
    conv_var = (conv_sums[1] / channel_width)[:, None] - conv_mean * conv_mean
    rstd_two = lax.rsqrt(conv_var + epsilon)
    zhat = (conv - conv_mean) * rstd_two
    swish_gate = jax.nn.sigmoid(zhat)
    swished = (zhat * swish_gate).astype(jnp.bfloat16)
    out_term = jnp.dot(upstream_whole.T, swished, preferred_element_type=jnp.float32)
    out_grad = scatter_sum(out_term.astype(jnp.bfloat16)).T
    partial_out = jnp.dot(swished, w_out, preferred_element_type=jnp.float32).astype(jnp.bfloat16)

    def pair_scatter(partial):
        mine = lax.dynamic_slice_in_dim(
            partial, tensor_position * channel_total, channel_total, 1
        )
        theirs = lax.dynamic_slice_in_dim(
            partial, (1 - tensor_position) * channel_total, channel_total, 1
        )
        return mine.astype(jnp.float32) + swap(theirs, "tensor").astype(jnp.float32)

    output = (frame_total.astype(jnp.float32) + pair_scatter(partial_out)).astype(jnp.bfloat16)
    dswish = jnp.dot(upstream_whole, w_out.T, preferred_element_type=jnp.float32)
    dswish = dswish * (swish_gate + zhat * swish_gate * (1.0 - swish_gate))
    slopes = pair_sum(jnp.stack([jnp.sum(dswish, axis=-1), jnp.sum(dswish * zhat, axis=-1)]))
    dconv = rstd_two * (
        dswish
        - (slopes[0] / channel_width)[:, None]
        - zhat * (slopes[1] / channel_width)[:, None]
    )
    dconv = dconv.astype(jnp.bfloat16)
    slope = dconv.astype(jnp.float32)
    slope_pad = padded_2(dconv, half).astype(jnp.float32)
    dhidden = jnp.zeros((count, channel_total), jnp.float32)
    for offset in range(taps_count):
        dhidden = dhidden + slope_pad[2 * half - offset : 2 * half - offset + count] * taps[offset]
    dhidden = dhidden * valid
    dvalues = (dhidden * sigma).astype(jnp.bfloat16)
    dgates = (dhidden * values * sigma * (1.0 - sigma)).astype(jnp.bfloat16)
    value_term = jnp.dot(normalized_rows.T, dvalues, preferred_element_type=jnp.float32)
    gate_term = jnp.dot(normalized_rows.T, dgates, preferred_element_type=jnp.float32)
    grads = scatter_sum(
        jnp.concatenate(
            [
                t[:, c : c + channel_total // 3]
                for c in range(0, channel_total, channel_total // 3)
                for t in (value_term.astype(jnp.bfloat16), gate_term.astype(jnp.bfloat16))
            ],
            axis=1,
        )
    )
    width = channel_total // 3
    value_grad = jnp.concatenate([grads[:, i * width : (i + 1) * width] for i in (0, 2, 4)], axis=1)
    gate_grad = jnp.concatenate([grads[:, i * width : (i + 1) * width] for i in (1, 3, 5)], axis=1)
    kernel_grad = jnp.stack(
        [jnp.sum(padded[offset : offset + count] * slope, axis=0) for offset in range(taps_count)]
    )
    for bit in bits_of("dp") + bits_of("seq"):
        kernel_grad = kernel_grad + swap(kernel_grad, *bit)
    dnormed_part = jnp.dot(dvalues, w_value.T, preferred_element_type=jnp.float32) + jnp.dot(
        dgates, w_gate.T, preferred_element_type=jnp.float32
    )
    normalized_grad = pair_scatter(dnormed_part.astype(jnp.bfloat16))
    local_centered_scaled = lax.dynamic_slice_in_dim(
        centered_scaled, tensor_position * channel_total, channel_total, 1
    )
    input_sums = pair_sum(
        jnp.stack(
            [
                jnp.sum(normalized_grad, axis=-1),
                jnp.sum(normalized_grad * local_centered_scaled, axis=-1),
            ]
        )
    )
    input_gradient = upstream.astype(jnp.float32) + inverse_deviation_one * (
        normalized_grad
        - (input_sums[0] / channel_width)[:, None]
        - local_centered_scaled * (input_sums[1] / channel_width)[:, None]
    )
    input_gradient = input_gradient.astype(jnp.bfloat16)
    return (output[None], input_gradient[None], value_grad, gate_grad, kernel_grad, out_grad)


def solution(mesh):
    return jax.shard_map(
        shards,
        mesh=mesh,
        in_specs=(
            P("dp", "seq", "tensor"),
            P("dp"),
            P("dp", "seq", "tensor"),
            P(None, "tensor"),
            P(None, "tensor"),
            P(None, "tensor"),
            P("tensor", None),
        ),
        out_specs=(
            P("dp", "seq", "tensor"),
            P("dp", "seq", "tensor"),
            P(("seq", "dp"), "tensor"),
            P(("seq", "dp"), "tensor"),
            P(None, "tensor"),
            P("tensor", ("seq", "dp")),
        ),
        check_vma=False,
    )
```

```python
import functools

import jax
import jax.numpy as jnp
from jax import lax
from jax.experimental import pallas as pl
from jax.experimental.pallas import tpu as pltpu
from jax.sharding import PartitionSpec as P

epsilon = 1e-05
f32, bf16 = jnp.float32, jnp.bfloat16
LANES = 128
WIDE, NEAR = 32, 16
NT = (((1,), (1,)), ((), ()))
PARAMS = dict(vmem_limit_bytes=48 << 20)


def swap(value, axis, bit=0):
    size = lax.axis_size(axis)
    return lax.ppermute(value, axis, [(i, i ^ (1 << bit)) for i in range(size)])


def bits_of(axis):
    return [(axis, b) for b in range(lax.axis_size(axis).bit_length() - 1)]


class Halver:
    def __init__(self, terms):
        self.bits = bits_of("seq")[::-1] + bits_of("dp")[::-1]
        blocks = 1 << len(self.bits)
        rows = terms.shape[0] // blocks
        self.value = terms.reshape((2,) * len(self.bits) + (rows, terms.shape[1]))

    def step(self, bit):
        dim = self.bits.index(bit)
        mine = (lax.axis_index(bit[0]) >> bit[1]) & 1
        send = lax.dynamic_index_in_dim(self.value, 1 - mine, dim, keepdims=False)
        keep = lax.dynamic_index_in_dim(self.value, mine, dim, keepdims=False)
        shape = send.shape
        got = swap(send.reshape(-1, shape[-1]), *bit).reshape(shape)
        self.value = keep.astype(f32) + got.astype(f32)
        self.bits = self.bits[:dim] + self.bits[dim + 1 :]
        if self.bits:
            self.value = self.value.astype(bf16)


def scatter_sum(terms):
    thirds = [Halver(t) for t in terms]
    every = bits_of("dp") + bits_of("seq")
    turning, rest = every[:3], every[3:]
    for phase in range(len(turning)):
        for i, third in enumerate(thirds):
            third.step(turning[(i + phase) % len(turning)])
    merged = thirds[0]
    merged.value = jnp.concatenate([t.value for t in thirds], axis=-1)
    for bit in rest:
        merged.step(bit)
    return merged.value


def row_mask(info, first, rows, limit):
    place = info[0] + first + lax.broadcasted_iota(jnp.int32, (rows, 1), 0)
    return ((place >= 0) & (place < limit)).astype(f32)


def front_kernel(info, own, other, halo_own, halo_other, wv, wg, norm, rstd, hid, sig, slope, edge):
    half = own.shape[1]
    count = own.shape[0]
    mine = pl.multiple_of(info[3] * half, half)
    theirs = pl.multiple_of((1 - info[3]) * half, half)

    def normalize(a, b):
        a, b = a.astype(f32), b.astype(f32)
        width = 2 * half
        mean = (jnp.sum(a, 1, keepdims=True) + jnp.sum(b, 1, keepdims=True)) / width
        a, b = a - mean, b - mean
        var = (jnp.sum(a * a, 1, keepdims=True) + jnp.sum(b * b, 1, keepdims=True)) / width
        inverse = lax.rsqrt(var + epsilon)
        return (a * inverse).astype(bf16), (b * inverse).astype(bf16), inverse

    @pl.when(pl.program_id(0) == 0)
    def _():
        def body(i, _):
            rows = pl.ds(pl.multiple_of(i * 32, 32), 32)
            a, b, inverse = normalize(own[rows, :], other[rows, :])
            norm[rows, pl.ds(mine, half)] = a
            norm[rows, pl.ds(theirs, half)] = b
            rstd[rows, :] = jnp.broadcast_to(inverse, (32, LANES))
            return 0

        lax.fori_loop(0, count // 32, body, 0)
        for to, at in ((0, 0), (WIDE, WIDE + NEAR)):
            a, b, _ = normalize(halo_own[at : at + WIDE, :], halo_other[at : at + WIDE, :])
            edge[to : to + WIDE, pl.ds(mine, half)] = a
            edge[to : to + WIDE, pl.ds(theirs, half)] = b

    def gated(rows):
        value = jnp.dot(rows, wv[...], preferred_element_type=f32)
        gate = jnp.dot(rows, wg[...], preferred_element_type=f32)
        return value, jax.nn.sigmoid(gate)

    step = count // 4
    for c in range(0, count, step):
        value, s = gated(norm[c : c + step, :])
        keep = row_mask(info, c, step, info[1])
        vs = value * s * keep
        hid[WIDE + c : WIDE + c + step, :] = vs.astype(bf16)
        sig[c : c + step, :] = s * keep
        slope[c : c + step, :] = vs * (1.0 - s)
    value, s = gated(edge[...])
    vs = value * s
    hid[:WIDE, :] = (vs[:WIDE] * row_mask(info, -WIDE, WIDE, info[1])).astype(bf16)
    hid[WIDE + count :, :] = (vs[WIDE:] * row_mask(info, count, WIDE, info[1])).astype(bf16)


def whole(shape):
    return pl.BlockSpec(shape, lambda n: (0,) * len(shape))


def cost(flops, nbytes, trans=0):
    return pl.CostEstimate(flops=flops, bytes_accessed=nbytes, transcendentals=trans)


SMEM = pl.BlockSpec(memory_space=pltpu.SMEM)


def front(info, own, other, halo_own, halo_other, w_value, w_gate):
    count, half = own.shape
    width, channels = w_value.shape
    tile = channels // 3
    columns = lambda rows: pl.BlockSpec((rows, tile), lambda n: (0, n))
    return pl.pallas_call(
        front_kernel,
        grid=(channels // tile,),
        in_specs=[SMEM]
        + [whole(a.shape) for a in (own, other, halo_own, halo_other)]
        + [columns(width), columns(width)],
        out_specs=[
            whole((count, width)),
            whole((count, LANES)),
            columns(count + 2 * WIDE),
            columns(count),
            columns(count),
        ],
        out_shape=[
            jax.ShapeDtypeStruct((count, width), bf16),
            jax.ShapeDtypeStruct((count, LANES), f32),
            jax.ShapeDtypeStruct((count + 2 * WIDE, channels), bf16),
            jax.ShapeDtypeStruct((count, channels), f32),
            jax.ShapeDtypeStruct((count, channels), f32),
        ],
        scratch_shapes=[pltpu.VMEM((2 * WIDE, width), bf16)],
        compiler_params=pltpu.CompilerParams(**PARAMS),
        cost_estimate=cost(4 * count * width * channels, 20 << 20, count * channels),
        name="front",
    )(info, own, other, halo_own, halo_other, w_value, w_gate)


def upstream_kernel(info, own, other, halo_own, halo_other, w_out, full, out, edge):
    count, half = own.shape
    mine = pl.multiple_of(info[3] * half, half)
    theirs = pl.multiple_of((1 - info[3]) * half, half)

    @pl.when(pl.program_id(0) == 0)
    def _():
        for a, b, at in ((own, halo_own, mine), (other, halo_other, theirs)):
            full[:, pl.ds(at, half)] = a[...]
            edge[:NEAR, pl.ds(at, half)] = b[WIDE : WIDE + NEAR, :]
            edge[NEAR:, pl.ds(at, half)] = b[2 * WIDE + NEAR :, :]

    step = count // 4
    for c in range(0, count, step):
        out[NEAR + c : NEAR + c + step, :] = lax.dot_general(
            full[c : c + step, :], w_out[...], NT, preferred_element_type=f32
        )
    ends = lax.dot_general(edge[...], w_out[...], NT, preferred_element_type=f32)
    out[:NEAR, :] = ends[:NEAR]
    out[NEAR + count :, :] = ends[NEAR:]


def upstream(info, own, other, halo_own, halo_other, w_out):
    count, half = own.shape
    channels, width = w_out.shape
    tile = channels // 3
    return pl.pallas_call(
        upstream_kernel,
        grid=(channels // tile,),
        in_specs=[SMEM]
        + [whole(a.shape) for a in (own, other, halo_own, halo_other)]
        + [pl.BlockSpec((tile, width), lambda n: (n, 0))],
        out_specs=[
            whole((count, width)),
            pl.BlockSpec((count + 2 * NEAR, tile), lambda n: (0, n)),
        ],
        out_shape=[
            jax.ShapeDtypeStruct((count, width), bf16),
            jax.ShapeDtypeStruct((count + 2 * NEAR, channels), f32),
        ],
        scratch_shapes=[pltpu.VMEM((2 * NEAR, width), bf16)],
        compiler_params=pltpu.CompilerParams(**PARAMS),
        cost_estimate=cost(2 * count * width * channels, 10 << 20),
        name="upstream",
    )(info, own, other, halo_own, halo_other, w_out)


def tap_sums(source, base, groups, taps):
    sums = [None] * groups
    for residue in range(8):
        mine = list(range(residue, len(taps), 8))
        shifted = [
            source[pl.ds(base + 8 * i + residue, 8), :] for i in range(groups + len(mine) - 1)
        ]
        for i, k in enumerate(mine):
            for g in range(groups):
                term = shifted[g + i] * taps[k]
                sums[g] = term if sums[g] is None else sums[g] + term
    return sums


def tap_rows(taps, reverse=False):
    values = taps[...].astype(f32)
    order = range(taps.shape[0])
    return [
        jnp.broadcast_to(values[k : k + 1, :], (8, LANES))
        for k in (reversed(order) if reverse else order)
    ]


def paired(first, second):
    lane = lax.broadcasted_iota(jnp.int32, (first.shape[0], LANES), 1)
    return jnp.where(
        lane < LANES // 2,
        jnp.sum(first, axis=1, keepdims=True),
        jnp.sum(second, axis=1, keepdims=True),
    )


def conv_kernel(hid, taps, conv, stats, scratch, total, square):
    n = pl.program_id(0)
    rows = conv.shape[0]
    skip = WIDE - NEAR - (taps.shape[0] - 1) // 2
    scratch[: hid.shape[0], :] = hid[...].astype(f32)
    weights = tap_rows(taps)
    groups = 20

    @pl.when(n == 0)
    def _():
        total[...] = jnp.zeros_like(total)
        square[...] = jnp.zeros_like(square)

    def body(i, _):
        base = pl.multiple_of(i * 8 * groups, 8)
        for g, value in enumerate(tap_sums(scratch, base + skip, groups, weights)):
            at = pl.ds(base + 8 * g, 8)
            conv[at, :] = value
            total[at, :] += value
            square[at, :] += value * value
        return 0

    lax.fori_loop(0, rows // (8 * groups), body, 0)

    @pl.when(n == pl.num_programs(0) - 1)
    def _():
        stats[...] = paired(total[...], square[...])


def depthwise(hid, taps):
    rows, channels = hid.shape
    kept = rows - 2 * (WIDE - NEAR)
    columns = lambda r: pl.BlockSpec((r, LANES), lambda n: (0, n))
    return pl.pallas_call(
        conv_kernel,
        grid=(channels // LANES,),
        in_specs=[columns(rows), columns(taps.shape[0])],
        out_specs=[columns(kept), whole((kept, LANES))],
        out_shape=[
            jax.ShapeDtypeStruct((kept, channels), f32),
            jax.ShapeDtypeStruct((kept, LANES), f32),
        ],
        scratch_shapes=[
            pltpu.VMEM((rows + 16, LANES), f32),
            pltpu.VMEM((kept, LANES), f32),
            pltpu.VMEM((kept, LANES), f32),
        ],
        compiler_params=pltpu.CompilerParams(**PARAMS),
        cost_estimate=cost(62 * kept * channels, 4 << 20),
        name="depthwise",
    )(hid, taps)


def moments(first, second, width):
    mean = (first[:, :1] + second[:, :1]) / width
    half = LANES // 2
    square = (first[:, half : half + 1] + second[:, half : half + 1]) / width
    return mean, lax.rsqrt(square - mean * mean + epsilon)


def swish_kernel(conv, pull, own, other, swished, dswish, stats):
    mean, inverse = moments(own, other, 2 * conv.shape[1])
    zhat = (conv[...] - mean) * inverse
    s = jax.nn.sigmoid(zhat)
    zs = zhat * s
    swished[...] = zs.astype(bf16)
    d = pull[...] * (s + zs * (1.0 - s))
    dswish[...] = d
    stats[...] = paired(d, d * zhat)


def swish(conv, pull, own, other):
    rows, channels = conv.shape
    step = 160
    block = lambda c: pl.BlockSpec((step, c), lambda n: (n, 0))
    return pl.pallas_call(
        swish_kernel,
        grid=(rows // step,),
        in_specs=[block(channels), block(channels), block(LANES), block(LANES)],
        out_specs=[block(channels), block(channels), block(LANES)],
        out_shape=[
            jax.ShapeDtypeStruct((rows, channels), bf16),
            jax.ShapeDtypeStruct((rows, channels), f32),
            jax.ShapeDtypeStruct((rows, LANES), f32),
        ],
        compiler_params=pltpu.CompilerParams(**PARAMS),
        cost_estimate=cost(20 * rows * channels, 9 << 20, rows * channels),
        name="swish",
    )(conv, pull, own, other)


def back_kernel(info, dswish, conv, own, other, own2, other2, taps, sig, slope, dconv, dvg, scratch, coef, *, width):
    rows = dswish.shape[0]
    count = sig.shape[0]
    channels = width // 2

    @pl.when(pl.program_id(0) == 0)
    def _():
        mean, inverse = moments(own, other, width)
        half = LANES // 2
        shift = (own2[:, :1] + other2[:, :1]) / width
        cross = (own2[:, half : half + 1] + other2[:, half : half + 1]) / width
        keep = row_mask(info, -NEAR, rows, info[2])
        inverse = inverse * keep
        tilt = inverse * inverse * cross
        coef[0] = jnp.broadcast_to(inverse, (rows, LANES))
        coef[1] = jnp.broadcast_to(tilt, (rows, LANES))
        coef[2] = jnp.broadcast_to(tilt * mean - inverse * shift, (rows, LANES))

    d = (coef[0] * dswish[...] - coef[1] * conv[...] + coef[2]).astype(bf16)
    dconv[...] = d
    scratch[:rows, :] = d.astype(f32)
    weights = tap_rows(taps, reverse=True)
    groups = 16
    skip = NEAR - (taps.shape[0] - 1) // 2

    def body(i, _):
        base = pl.multiple_of(i * 8 * groups, 16)
        sums = tap_sums(scratch, base + skip, groups, weights)
        for g in range(0, groups, 2):
            at = pl.ds(base + 8 * g, 16)
            dh = jnp.concatenate(sums[g : g + 2], axis=0)
            dvg[0, at, :] = (dh * sig[at, :]).astype(bf16)
            dvg[1, at, :] = (dh * slope[at, :]).astype(bf16)
        return 0

    lax.fori_loop(0, count // (8 * groups), body, 0)


def back(info, third, dswish, conv, stats, stats2, taps, sig, slope):
    rows, channels = dswish.shape
    count = sig.shape[0]
    tiles = channels // LANES // 3
    columns = lambda r: pl.BlockSpec((r, LANES), lambda n: (0, third * tiles + n))
    local = lambda r: pl.BlockSpec((r, LANES), lambda n: (0, n))
    return pl.pallas_call(
        functools.partial(back_kernel, width=2 * channels),
        grid=(tiles,),
        in_specs=[SMEM, columns(rows), columns(rows)]
        + [whole((rows, LANES))] * 4
        + [columns(taps.shape[0]), columns(count), columns(count)],
        out_specs=[local(rows), pl.BlockSpec((2, count, LANES), lambda n: (0, 0, n))],
        out_shape=[
            jax.ShapeDtypeStruct((rows, tiles * LANES), bf16),
            jax.ShapeDtypeStruct((2, count, tiles * LANES), bf16),
        ],
        scratch_shapes=[
            pltpu.VMEM((rows + 16, LANES), f32),
            pltpu.VMEM((3, rows, LANES), f32),
        ],
        compiler_params=pltpu.CompilerParams(**PARAMS),
        cost_estimate=cost(70 * count * tiles * LANES, 5 << 20),
        name="back",
    )(info, dswish, conv, *stats, *stats2, taps, sig, slope)


def taps_kernel(dconv, hid, out, scratch, total):
    count = dconv.shape[0] - 2 * NEAR
    taps = out.shape[0]
    half = (taps - 1) // 2
    scratch[: dconv.shape[0], :] = dconv[...].astype(f32)
    total[...] = jnp.zeros_like(total)
    groups = 16

    def body(i, _):
        base = pl.multiple_of(i * 8 * groups, 16)
        h = []
        for g in range(0, groups, 2):
            both = hid[pl.ds(WIDE + base + 8 * g, 16), :].astype(f32)
            h += [both[:8], both[8:]]
        for residue in range(8):
            mine = list(range(residue, taps, 8))
            shifted = [
                scratch[pl.ds(base + NEAR - half + 8 * g + residue, 8), :]
                for g in range(groups + len(mine) - 1)
            ]
            for j, m in enumerate(mine):
                term = shifted[j] * h[0]
                for g in range(1, groups):
                    term = term + shifted[g + j] * h[g]
                total[taps - 1 - m] += term
        return 0

    lax.fori_loop(0, count // (8 * groups), body, 0)
    out[...] = jnp.sum(total[...], axis=1)


def taps_gradient(third, dconv, hid, taps):
    rows, channels = dconv.shape
    tiles = channels // LANES
    local = lambda r: pl.BlockSpec((r, LANES), lambda n: (0, n))
    return pl.pallas_call(
        taps_kernel,
        grid=(tiles,),
        in_specs=[
            local(rows),
            pl.BlockSpec((hid.shape[0], LANES), lambda n: (0, third * tiles + n)),
        ],
        out_specs=local(taps),
        out_shape=jax.ShapeDtypeStruct((taps, channels), f32),
        scratch_shapes=[
            pltpu.VMEM((rows + 16, LANES), f32),
            pltpu.VMEM((taps, 8, LANES), f32),
        ],
        compiler_params=pltpu.CompilerParams(**PARAMS),
        cost_estimate=cost(62 * rows * channels, 1 << 20),
        name="taps",
    )(dconv, hid)


def shards(inputs, lengths, cotangent, w_value, w_gate, kernel, w_out):
    x, ct = inputs[0], cotangent[0]
    count, channels = x.shape
    width = channels * lax.axis_size("tensor")
    core = lax.axis_index("tensor")
    peers = lax.axis_size("seq")
    info = jnp.stack(
        [lax.axis_index("seq") * count, lengths[0], jnp.int32(peers * count), core]
    ).astype(jnp.int32)

    up = [(i, i + 1) for i in range(peers - 1)]
    down = [(j, i) for i, j in up]
    before = lax.ppermute(jnp.concatenate([x[-WIDE:], ct[-NEAR:]]), "seq", up)
    after = lax.ppermute(jnp.concatenate([x[:WIDE], ct[:NEAR]]), "seq", down)
    halo = jnp.concatenate([before, after])
    x_other, ct_other, halo_other = swap(x, "tensor"), swap(ct, "tensor"), swap(halo, "tensor")

    ct_full, pull = upstream(info, ct, ct_other, halo, halo_other, w_out)
    norm, rstd, hid, sig, slope = front(info, x, x_other, halo, halo_other, w_value, w_gate)
    conv, stats = depthwise(hid, kernel)
    stats_other = swap(stats, "tensor")
    swished, dswish, stats2 = swish(conv, pull, stats, stats_other)
    stats2_other = swap(stats2, "tensor")
    swished = swished[NEAR : NEAR + count]

    third = channels // 3
    out_term = jnp.dot(ct_full.T, swished, preferred_element_type=f32).astype(bf16)
    out_grad = scatter_sum(jnp.split(out_term, 3, axis=1)).T

    dconvs, dvgs, terms = [], [], []
    for i in range(3):
        dconv, dvg = back(
            info, i, dswish, conv, (stats, stats_other), (stats2, stats2_other), kernel, sig, slope
        )
        dconvs.append(dconv)
        dvgs.append(dvg)
        terms.append(
            jnp.concatenate(
                [jnp.dot(norm.T, dvg[j], preferred_element_type=f32).astype(bf16) for j in (0, 1)],
                axis=1,
            )
        )
    grads = scatter_sum(terms)
    value_grad, gate_grad = (
        jnp.concatenate([grads[:, (2 * i + j) * third :][:, :third] for i in range(3)], axis=1)
        for j in (0, 1)
    )
    kernel_grad = jnp.concatenate(
        [taps_gradient(i, dconvs[i], hid, kernel.shape[0]) for i in range(3)], axis=1
    )
    for bit in bits_of("dp") + bits_of("seq"):
        kernel_grad = kernel_grad + swap(kernel_grad, *bit)

    def pair_scatter(product):
        theirs = product((1 - core) * channels).astype(bf16)
        got = swap(theirs, "tensor").astype(f32)
        return product(core * channels) + got

    def out_part(at):
        w = lax.dynamic_slice_in_dim(w_out, at, channels, 1)
        return jnp.dot(swished, w, preferred_element_type=f32)

    dvalues, dgates = (jnp.concatenate([dvg[j] for dvg in dvgs], axis=1) for j in (0, 1))

    def norm_part(at):
        wv = lax.dynamic_slice_in_dim(w_value, at, channels, 0)
        wg = lax.dynamic_slice_in_dim(w_gate, at, channels, 0)
        return jnp.dot(dvalues, wv.T, preferred_element_type=f32) + jnp.dot(
            dgates, wg.T, preferred_element_type=f32
        )

    output = (x.astype(f32) + pair_scatter(out_part)).astype(bf16)
    dnorm = pair_scatter(norm_part)
    xhat = lax.dynamic_slice_in_dim(norm, core * channels, channels, 1).astype(f32)
    sums = jnp.stack([jnp.sum(dnorm, axis=-1), jnp.sum(dnorm * xhat, axis=-1)])
    sums = (sums + swap(sums, "tensor")) / width
    input_gradient = ct.astype(f32) + rstd[:, :1] * (
        dnorm - sums[0][:, None] - xhat * sums[1][:, None]
    )
    return (
        output[None],
        input_gradient.astype(bf16)[None],
        value_grad,
        gate_grad,
        kernel_grad,
        out_grad,
    )


def solution(mesh):
    return jax.shard_map(
        shards,
        mesh=mesh,
        in_specs=(
            P("dp", "seq", "tensor"),
            P("dp"),
            P("dp", "seq", "tensor"),
            P(None, "tensor"),
            P(None, "tensor"),
            P(None, "tensor"),
            P("tensor", None),
        ),
        out_specs=(
            P("dp", "seq", "tensor"),
            P("dp", "seq", "tensor"),
            P(("seq", "dp"), "tensor"),
            P(("seq", "dp"), "tensor"),
            P(None, "tensor"),
            P("tensor", ("seq", "dp")),
        ),
        check_vma=False,
    )
```

```python
import functools

import jax
import jax.numpy as jnp
from jax import lax
from jax.experimental import pallas as pl
from jax.experimental.pallas import tpu as pltpu
from jax.sharding import PartitionSpec as P

epsilon = 1e-05
f32, bf16 = jnp.float32, jnp.bfloat16
LANES = 128
WIDE, NEAR = 32, 16
NN = (((1,), (0,)), ((), ()))
NT = (((1,), (1,)), ((), ()))
TN = (((0,), (0,)), ((), ()))
VMEM = pl.BlockSpec(memory_space=pltpu.VMEM)
SMEM = pl.BlockSpec(memory_space=pltpu.SMEM)
ANY = pl.BlockSpec(memory_space=pl.ANY)


def dot(a, b, dims=NN):
    return lax.dot_general(a, b, dims, preferred_element_type=f32)


def run(kernel, info, args, outs, scratch=(), after=(), limit=16):
    def body(*refs):
        lead = 1 + len(args)
        kernel(*refs[:lead], *refs[lead + len(after) :])

    return pl.pallas_call(
        body,
        in_specs=[SMEM] + [VMEM] * len(args) + [ANY] * len(after),
        out_specs=[VMEM] * len(outs),
        out_shape=[pltpu.VMEM(shape, dtype) for shape, dtype in outs],
        scratch_shapes=list(scratch),
        compiler_params=pltpu.CompilerParams(vmem_limit_bytes=limit << 20),
        cost_estimate=pl.CostEstimate(flops=COST, bytes_accessed=COST, transcendentals=0),
        name=kernel.__name__ if hasattr(kernel, "__name__") else kernel.func.__name__,
    )(info, *[pltpu.with_memory_space_constraint(a, pltpu.VMEM) for a in args], *after)


COST = 1 << 12


def swap(value, axis, bit=0):
    size = lax.axis_size(axis)
    return lax.ppermute(value, axis, [(i, i ^ (1 << bit)) for i in range(size)])


def bits_of(axis):
    return [(axis, b) for b in range(lax.axis_size(axis).bit_length() - 1)]


def every_bit():
    return bits_of("dp") + bits_of("seq")


class Halver:
    def __init__(self, keep, send, bit, rows):
        self.bits = every_bit()[::-1]
        self.rows = rows
        self.merge(keep, send, bit)

    def merge(self, keep, send, bit):
        got = swap(send, *bit)
        value = keep.astype(f32) + got.astype(f32)
        self.bits.remove(bit)
        if self.bits:
            value = value.astype(bf16)
        self.value = value.reshape((2,) * len(self.bits) + (self.rows, value.shape[-1]))

    def step(self, bit):
        dim = self.bits.index(bit)
        mine = (lax.axis_index(bit[0]) >> bit[1]) & 1
        columns = self.value.shape[-1]
        send = lax.dynamic_index_in_dim(self.value, 1 - mine, dim, keepdims=False)
        keep = lax.dynamic_index_in_dim(self.value, mine, dim, keepdims=False)
        self.merge(keep.reshape(-1, columns), send.reshape(-1, columns), bit)


def scatter_sum(halves, rows):
    every = every_bit()
    turning, rest = every[:3], every[3:]
    thirds = [Halver(*half, turning[i], rows) for i, half in enumerate(halves)]
    for phase in range(1, len(turning)):
        for i, third in enumerate(thirds):
            third.step(turning[(i + phase) % len(turning)])
    merged = thirds[0]
    merged.value = jnp.concatenate([t.value for t in thirds], axis=-1)
    for bit in rest:
        merged.step(bit)
    return merged.value


def store_halves(info, bit, start, value, keep, send, rows):
    for mine in (0, 1):

        @pl.when(info[4 + bit] == mine)
        def _():
            for r in range(0, value.shape[0], rows):
                block = (start + r) // rows
                to = ((block >> (bit + 1)) << bit) | (block & ((1 << bit) - 1))
                target = keep if (block >> bit) & 1 == mine else send
                target[to * rows : (to + 1) * rows, :] = value[r : r + rows, :]


def row_mask(info, first, rows, limit):
    place = info[0] + first + lax.broadcasted_iota(jnp.int32, (rows, 1), 0)
    return ((place >= 0) & (place < limit)).astype(f32)


def halves_at(info, half):
    return (
        pl.multiple_of(info[3] * half, half),
        pl.multiple_of((1 - info[3]) * half, half),
    )


def upstream(info, own, other, w_out, full, pull):
    count, half = own.shape
    mine, theirs = halves_at(info, half)
    full[:, pl.ds(mine, half)] = own[...]
    full[:, pl.ds(theirs, half)] = other[...]
    step = count // 2
    for c in range(0, count, step):
        pull[c : c + step, :] = dot(full[c : c + step, :], w_out[...], NT)


def front(info, own, other, halo_own, halo_other, wv, wg, w_out, norm, rstd, hid, sig, slope, ends, edge):
    count, half = own.shape
    channels = wv.shape[1]
    mine, theirs = halves_at(info, half)

    def normalize(to, a, b):
        a, b = a.astype(f32), b.astype(f32)
        width = 2 * half
        mean = (jnp.sum(a, 1, keepdims=True) + jnp.sum(b, 1, keepdims=True)) / width
        a, b = a - mean, b - mean
        var = jnp.sum(a * a, 1, keepdims=True) + jnp.sum(b * b, 1, keepdims=True)
        inverse = lax.rsqrt(var / width + epsilon)
        norm[to, pl.ds(mine, half)] = (a * inverse).astype(bf16)
        norm[to, pl.ds(theirs, half)] = (b * inverse).astype(bf16)
        return inverse

    chunk = 64

    def body(i, _):
        at = pl.multiple_of(i * chunk, chunk)
        inverse = normalize(
            pl.ds(pl.multiple_of(WIDE + at, WIDE), chunk),
            own[pl.ds(at, chunk), :],
            other[pl.ds(at, chunk), :],
        )
        rstd[pl.ds(at, chunk), :] = jnp.broadcast_to(inverse, (chunk, LANES))
        return 0

    lax.fori_loop(0, count // chunk, body, 0)
    for to, at in ((0, 0), (WIDE + count, WIDE + NEAR)):
        normalize(pl.ds(to, WIDE), halo_own[at : at + WIDE, :], halo_other[at : at + WIDE, :])
    for a, at in ((halo_own, mine), (halo_other, theirs)):
        edge[:NEAR, pl.ds(at, half)] = a[WIDE : WIDE + NEAR, :]
        edge[NEAR:, pl.ds(at, half)] = a[2 * WIDE + NEAR :, :]
    ends[...] = dot(edge[...], w_out[...], NT)

    tile = channels // 3
    rows = count + 2 * WIDE
    step = rows // 2
    for n in range(0, channels, tile):
        cols = slice(n, n + tile)
        for c in range(0, rows, step):
            value = dot(norm[c : c + step, :], wv[:, cols])
            s = jax.nn.sigmoid(dot(norm[c : c + step, :], wg[:, cols]))
            keep = row_mask(info, c - WIDE, step, info[1])
            vs = value * s * keep
            hid[c : c + step, cols] = vs.astype(bf16)
            low, high = max(c, WIDE), min(c + step, WIDE + count)
            part = slice(low - c, high - c)
            sig[low - WIDE : high - WIDE, cols] = (s * keep)[part]
            slope[low - WIDE : high - WIDE, cols] = (vs * (1.0 - s))[part]


def tap_sums(source, base, groups, taps):
    sums = [None] * groups
    for residue in range(8):
        mine = list(range(residue, len(taps), 8))
        shifted = [
            source[pl.ds(base + 8 * i + residue, 8), :] for i in range(groups + len(mine) - 1)
        ]
        for i, k in enumerate(mine):
            for g in range(groups):
                term = shifted[g + i] * taps[k]
                sums[g] = term if sums[g] is None else sums[g] + term
    return sums


def tap_rows(taps, cols, reverse=False):
    values = taps[:, cols].astype(f32)
    order = range(taps.shape[0])
    return [
        jnp.broadcast_to(values[k : k + 1, :], (8, LANES))
        for k in (reversed(order) if reverse else order)
    ]


def lane_tile(n):
    return pl.ds(pl.multiple_of(n * LANES, LANES), LANES)


def paired(first, second):
    lane = lax.broadcasted_iota(jnp.int32, (first.shape[0], LANES), 1)
    return jnp.where(
        lane < LANES // 2,
        jnp.sum(first, axis=1, keepdims=True),
        jnp.sum(second, axis=1, keepdims=True),
    )


def depthwise(info, hid, taps, conv, stats, scratch, total, square):
    rows = conv.shape[0]
    skip = WIDE - NEAR - (taps.shape[0] - 1) // 2
    groups = 20
    total[...] = jnp.zeros_like(total)
    square[...] = jnp.zeros_like(square)

    def tile(n, _):
        cols = lane_tile(n)
        scratch[: hid.shape[0], :] = hid[:, cols].astype(f32)
        weights = tap_rows(taps, cols)

        def body(i, _):
            base = pl.multiple_of(i * 8 * groups, 8)
            for g, value in enumerate(tap_sums(scratch, base + skip, groups, weights)):
                at = pl.ds(base + 8 * g, 8)
                conv[at, cols] = value
                total[at, :] += value
                square[at, :] += value * value
            return 0

        lax.fori_loop(0, rows // (8 * groups), body, 0)
        return 0

    lax.fori_loop(0, conv.shape[1] // LANES, tile, 0)
    stats[...] = paired(total[...], square[...])


def moments(first, second, width):
    mean = (first[:, :1] + second[:, :1]) / width
    half = LANES // 2
    square = (first[:, half : half + 1] + second[:, half : half + 1]) / width
    return mean, lax.rsqrt(square - mean * mean + epsilon)


def swish(info, conv, pull, ends, own, other, swished, dswish, stats):
    count, channels = pull.shape

    def part(at, g, rows):
        to = pl.ds(at, rows)
        mean, inverse = moments(own[to, :], other[to, :], 2 * channels)
        zhat = (conv[to, :] - mean) * inverse
        s = jax.nn.sigmoid(zhat)
        zs = zhat * s
        d = g * (s + zs * (1.0 - s))
        dswish[to, :] = d
        stats[to, :] = paired(d, d * zhat)
        return zs.astype(bf16)

    part(0, ends[:NEAR, :], NEAR)
    part(NEAR + count, ends[NEAR:, :], NEAR)
    step = 32

    def body(i, _):
        at = pl.multiple_of(i * step, step)
        rows = pl.ds(at, step)
        swished[rows, :] = part(pl.multiple_of(at + NEAR, NEAR), pull[rows, :], step)
        return 0

    lax.fori_loop(0, count // step, body, 0)


def out_terms(info, full, swished, *halves, rows):
    width = full.shape[1]
    cols = swished.shape[1] // 3
    step = width // 4
    for i in range(3):
        for c in range(0, width, step):
            r = dot(full[:, c : c + step], swished[:, i * cols : (i + 1) * cols], TN)
            store_halves(info, i, c, r.astype(bf16), halves[2 * i], halves[2 * i + 1], rows)


def back(info, dswish, conv, own, other, own2, other2, taps, sig, slope, norm, dconv, dvg, keep, send, scratch, coef, *, third, block):
    rows, channels = dswish.shape
    count = sig.shape[0]
    width = 2 * channels
    mean, inverse = moments(own[...], other[...], width)
    half = LANES // 2
    shift = (own2[:, :1] + other2[:, :1]) / width
    cross = (own2[:, half : half + 1] + other2[:, half : half + 1]) / width
    inverse = inverse * row_mask(info, -NEAR, rows, info[2])
    tilt = inverse * inverse * cross
    coef[0] = jnp.broadcast_to(inverse, (rows, LANES))
    coef[1] = jnp.broadcast_to(tilt, (rows, LANES))
    coef[2] = jnp.broadcast_to(tilt * mean - inverse * shift, (rows, LANES))
    tiles = channels // LANES // 3
    groups = 16
    skip = NEAR - (taps.shape[0] - 1) // 2

    def tile(n, _):
        local = lane_tile(n)
        cols = lane_tile(third * tiles + n)
        d = (coef[0] * dswish[:, cols] - coef[1] * conv[:, cols] + coef[2]).astype(bf16)
        dconv[:, local] = d
        scratch[:rows, :] = d.astype(f32)
        weights = tap_rows(taps, cols, reverse=True)

        def body(i, _):
            base = pl.multiple_of(i * 8 * groups, 16)
            sums = tap_sums(scratch, base + skip, groups, weights)
            for g in range(0, groups, 2):
                at = pl.ds(base + 8 * g, 16)
                dh = jnp.concatenate(sums[g : g + 2], axis=0)
                dvg[at, local] = (dh * sig[at, cols]).astype(bf16)
                dvg[at, lane_tile(tiles + n)] = (dh * slope[at, cols]).astype(bf16)
            return 0

        lax.fori_loop(0, count // (8 * groups), body, 0)
        return 0

    lax.fori_loop(0, tiles, tile, 0)
    step = width // 4
    for c in range(0, width, step):
        r = dot(norm[WIDE : WIDE + count, c : c + step], dvg[...], TN)
        store_halves(info, third, c, r.astype(bf16), keep, send, block)


def taps_sums(info, dconv, hid, out, scratch, total, *, third):
    rows, channels = dconv.shape
    count = rows - 2 * NEAR
    taps = out.shape[0]
    half = (taps - 1) // 2
    groups = 16
    tiles = channels // LANES

    def tile(n, _):
        local = lane_tile(n)
        cols = lane_tile(third * tiles + n)
        scratch[:rows, :] = dconv[:, local].astype(f32)
        total[...] = jnp.zeros_like(total)

        def body(i, _):
            base = pl.multiple_of(i * 8 * groups, 16)
            h = []
            for g in range(0, groups, 2):
                both = hid[pl.ds(pl.multiple_of(WIDE + base + 8 * g, 16), 16), cols].astype(f32)
                h += [both[:8], both[8:]]
            for residue in range(8):
                mine = list(range(residue, taps, 8))
                shifted = [
                    scratch[pl.ds(base + NEAR - half + 8 * g + residue, 8), :]
                    for g in range(groups + len(mine) - 1)
                ]
                for j, m in enumerate(mine):
                    term = shifted[j] * h[0]
                    for g in range(1, groups):
                        term = term + shifted[g + j] * h[g]
                    total[taps - 1 - m] += term
            return 0

        lax.fori_loop(0, count // (8 * groups), body, 0)
        out[:, local] = jnp.sum(total[...], axis=1)
        return 0

    lax.fori_loop(0, tiles, tile, 0)


def out_half(info, swished, w_out, result, *, own):
    half = result.shape[1]
    at = halves_at(info, half)[0 if own else 1]
    step = swished.shape[0] // 2
    for c in range(0, swished.shape[0], step):
        part = dot(swished[c : c + step, :], w_out[:, pl.ds(at, half)])
        result[c : c + step, :] = part.astype(result.dtype)


def norm_half(info, a, b, c, wv, wg, result, *, own):
    count, half = result.shape
    at = halves_at(info, half)[0 if own else 1]
    third = half // 3
    step = count // 2
    for r in range(0, count, step):
        total = None
        for i, dvg in enumerate((a, b, c)):
            cols = slice(i * third, (i + 1) * third)
            for j, w in enumerate((wv, wg)):
                part = dot(
                    dvg[r : r + step, j * third : (j + 1) * third], w[pl.ds(at, half), cols], NT
                )
                total = part if total is None else total + part
        result[r : r + step, :] = total.astype(result.dtype)


def norm_sums(info, mine, got, norm, total, stats):
    count, half = mine.shape
    at = halves_at(info, half)[0]
    step = 32

    def body(i, _):
        rows = pl.ds(pl.multiple_of(i * step, step), step)
        xhat = norm[pl.ds(pl.multiple_of(i * step + WIDE, step), step), pl.ds(at, half)]
        d = mine[rows, :] + got[rows, :].astype(f32)
        total[rows, :] = d
        stats[rows, :] = paired(d, d * xhat.astype(f32))
        return 0

    lax.fori_loop(0, count // step, body, 0)


def shards(inputs, lengths, cotangent, w_value, w_gate, kernel, w_out):
    x, ct = inputs[0], cotangent[0]
    count, channels = x.shape
    width = channels * lax.axis_size("tensor")
    core = lax.axis_index("tensor")
    peers = lax.axis_size("seq")
    every = every_bit()
    block = width >> len(every)
    taps = kernel.shape[0]
    info = jnp.stack(
        [lax.axis_index("seq") * count, lengths[0], jnp.int32(peers * count), core]
        + [(lax.axis_index(a) >> b) & 1 for a, b in every]
    ).astype(jnp.int32)

    up = [(i, i + 1) for i in range(peers - 1)]
    down = [(j, i) for i, j in up]
    x_other, ct_other = swap(x, "tensor"), swap(ct, "tensor")
    before = lax.ppermute(jnp.concatenate([x[-WIDE:], ct[-NEAR:]]), "seq", up)
    after = lax.ppermute(jnp.concatenate([x[:WIDE], ct[:NEAR]]), "seq", down)
    halo = jnp.concatenate([before, after])
    halo_other = swap(halo, "tensor")

    rows, ext = count + 2 * NEAR, count + 2 * WIDE
    full, pull = run(
        upstream, info, [ct, ct_other, w_out], [((count, width), bf16), ((count, channels), f32)]
    )
    norm, rstd, hid, sig, slope, ends = run(
        front,
        info,
        [x, x_other, halo, halo_other, w_value, w_gate, w_out],
        [
            ((ext, width), bf16),
            ((count, LANES), f32),
            ((ext, channels), bf16),
            ((count, channels), f32),
            ((count, channels), f32),
            ((2 * NEAR, channels), f32),
        ],
        scratch=[pltpu.VMEM((2 * NEAR, width), bf16)],
        after=[pull],
    )
    row_sums = ((rows, LANES), f32)
    column = pltpu.VMEM((rows, LANES), f32)
    conv, stats = run(
        depthwise,
        info,
        [hid, kernel],
        [((rows, channels), f32), row_sums],
        scratch=[pltpu.VMEM((ext + 16, LANES), f32), column, column],
    )
    stats_other = swap(stats, "tensor")
    swished, dswish, stats2 = run(
        swish,
        info,
        [conv, pull, ends, stats, stats_other],
        [((count, channels), bf16), ((rows, channels), f32), row_sums],
    )
    stats2_other = swap(stats2, "tensor")

    third = channels // 3
    half_block = (width // 2, third)
    halves = run(
        functools.partial(out_terms, rows=block), info, [full, swished], [(half_block, bf16)] * 6
    )
    out_grad = scatter_sum([(halves[2 * i], halves[2 * i + 1]) for i in range(3)], block).T

    dconvs, dvgs, halves = [], [], []
    last = halves
    for i in range(3):
        dconv, dvg, keep, send = run(
            functools.partial(back, third=i, block=block),
            info,
            [dswish, conv, stats, stats_other, stats2, stats2_other, kernel, sig, slope, norm],
            [
                ((rows, third), bf16),
                ((count, 2 * third), bf16),
                ((width // 2, 2 * third), bf16),
                ((width // 2, 2 * third), bf16),
            ],
            scratch=[pltpu.VMEM((rows + 16, LANES), f32), pltpu.VMEM((3, rows, LANES), f32)],
            after=last,
        )
        last = [send]
        dconvs.append(dconv)
        dvgs.append(dvg)
        halves.append((keep, send))
    grads = scatter_sum(halves, block)
    value_grad, gate_grad = (
        jnp.concatenate([grads[:, (2 * i + j) * third :][:, :third] for i in range(3)], axis=1)
        for j in (0, 1)
    )
    kernel_grad = jnp.concatenate(
        [
            run(
                functools.partial(taps_sums, third=i),
                info,
                [dconvs[i], hid],
                [((taps, third), f32)],
                scratch=[pltpu.VMEM((rows + 16, LANES), f32), pltpu.VMEM((taps, 8, LANES), f32)],
                after=last,
            )[0]
            for i in range(3)
        ],
        axis=1,
    )
    for bit in every:
        kernel_grad = kernel_grad + swap(kernel_grad, *bit)

    theirs, mine = (
        run(
            functools.partial(norm_half, own=own),
            info,
            [*dvgs, w_value, w_gate],
            [((count, channels), f32 if own else bf16)],
            after=last,
        )[0]
        for own in (False, True)
    )
    dnorm, stats3 = run(
        norm_sums,
        info,
        [mine, swap(theirs, "tensor"), norm],
        [((count, channels), f32), ((count, LANES), f32)],
    )
    sums = (stats3 + swap(stats3, "tensor")) / width
    xhat = lax.dynamic_slice(norm, (WIDE, core * channels), (count, channels)).astype(f32)
    input_gradient = ct.astype(f32) + rstd[:, :1] * (
        dnorm - sums[:, :1] - xhat * sums[:, LANES // 2 : LANES // 2 + 1]
    )

    theirs, mine = (
        run(
            functools.partial(out_half, own=own),
            info,
            [swished, w_out],
            [((count, channels), f32 if own else bf16)],
            after=last,
        )[0]
        for own in (False, True)
    )
    output = x.astype(f32) + mine + swap(theirs, "tensor").astype(f32)
    return (
        output.astype(bf16)[None],
        input_gradient.astype(bf16)[None],
        value_grad,
        gate_grad,
        kernel_grad,
        out_grad,
    )


def solution(mesh):
    return jax.shard_map(
        shards,
        mesh=mesh,
        in_specs=(
            P("dp", "seq", "tensor"),
            P("dp"),
            P("dp", "seq", "tensor"),
            P(None, "tensor"),
            P(None, "tensor"),
            P(None, "tensor"),
            P("tensor", None),
        ),
        out_specs=(
            P("dp", "seq", "tensor"),
            P("dp", "seq", "tensor"),
            P(("seq", "dp"), "tensor"),
            P(("seq", "dp"), "tensor"),
            P(None, "tensor"),
            P("tensor", ("seq", "dp")),
        ),
        check_vma=False,
    )
```

```python
import functools

import jax
import jax.numpy as jnp
from jax import lax
from jax.experimental import pallas as pl
from jax.experimental.pallas import tpu as pltpu
from jax.sharding import PartitionSpec as P

epsilon = 1e-05
f32, bf16 = jnp.float32, jnp.bfloat16
LANES = 128
WIDE, NEAR = 32, 16
NN = (((1,), (0,)), ((), ()))
NT = (((1,), (1,)), ((), ()))
TN = (((0,), (0,)), ((), ()))
VMEM = pl.BlockSpec(memory_space=pltpu.VMEM)
SMEM = pl.BlockSpec(memory_space=pltpu.SMEM)
ANY = pl.BlockSpec(memory_space=pl.ANY)
HBM = pl.BlockSpec(memory_space=pltpu.HBM)


def dot(a, b, dims=NN):
    return lax.dot_general(a, b, dims, preferred_element_type=f32)


def run(kernel, info, args, outs, scratch=(), after=(), limit=8, space=VMEM, to=VMEM):
    def body(*refs):
        lead = 1 + len(args)
        rest = refs[lead + len(after) :]
        kernel(*refs[:lead], *rest[: len(outs)], *rest[len(outs) + 1 :])
        rest[len(outs)][...] = jnp.zeros((8, LANES), f32)

    args = [pltpu.with_memory_space_constraint(a, space.memory_space) for a in args]
    *results, mark = pl.pallas_call(
        body,
        in_specs=[SMEM] + [space] * len(args) + [ANY] * len(after),
        out_specs=[to] * len(outs) + [VMEM],
        out_shape=[to.memory_space(shape, dtype) for shape, dtype in outs]
        + [pltpu.VMEM((8, LANES), f32)],
        scratch_shapes=list(scratch),
        compiler_params=pltpu.CompilerParams(vmem_limit_bytes=limit << 20),
        cost_estimate=pl.CostEstimate(flops=COST, bytes_accessed=COST, transcendentals=0),
        name=kernel.__name__ if hasattr(kernel, "__name__") else kernel.func.__name__,
    )(info, *args, *after)
    return *results, mark


COST = 1 << 10


def swap(value, axis, bit=0):
    size = lax.axis_size(axis)
    return lax.ppermute(value, axis, [(i, i ^ (1 << bit)) for i in range(size)])


def bits_of(axis):
    return [(axis, b) for b in range(lax.axis_size(axis).bit_length() - 1)]


def every_bit():
    return bits_of("dp") + bits_of("seq")


def split_rows(info, bit, place, total, rows, keep, send, load):
    run_length = rows << place
    for j in range(total // (2 * run_length)):
        for put, side in ((keep, info[4 + bit]), (send, 1 - info[4 + bit])):
            if run_length % 32:
                low, high = (
                    load(slice((2 * j + i) * run_length, (2 * j + i + 1) * run_length))
                    for i in (0, 1)
                )
                value = jnp.where(side == 0, low, high)
            else:
                at = pl.multiple_of((2 * j + side) * run_length, run_length)
                value = load(pl.ds(at, run_length))
            put(j * run_length, value)


def put_into(target):
    def put(at, value):
        target[at : at + value.shape[0], :] = value

    return put


def put_folded(target, first, half):
    columns = target.shape[1] // 2

    def put(at, value):
        length = value.shape[0]
        for low in range(0, length, min(length, half)):
            part = value[low : low + min(length, half)]
            side, row = divmod(at + low, half)
            to = slice(first + row, first + row + part.shape[0])
            target[to, side * columns : (side + 1) * columns] = part

    return put


def add(a, b):
    return (a.astype(f32) + b.astype(f32)).astype(bf16)


def first_split(info, product, okept, ogot, vkeep, okeep, send, *, third, rows):
    total = product.shape[0]
    split_rows(info, third, third, total, rows, put_into(vkeep), put_into(send), lambda at: product[at, :])
    before = (third + 2) % 3
    place = third - (before < third)
    fold = put_folded(send, total // 2, total // 8)
    load = lambda at: add(okept[at, :], ogot[at, :])
    split_rows(info, third, place, total // 2, rows, put_into(okeep), fold, load)


def unfold(got, first, rows, target):
    half = rows // 2
    columns = target.shape[1]
    target[:half, :] = got[first:, :columns]
    target[half:, :] = got[first:, columns:]


def second_split(info, vkept, okept, got, vkeep, okeep, send, flat, *, third, rows):
    total = vkept.shape[0]
    bit = (third + 1) % 3
    left = [b for b in range(3) if b != third]
    load = lambda at: add(vkept[at, :], got[at, :])
    split_rows(info, bit, left.index(bit), total, rows, put_into(vkeep), put_into(send), load)
    unfold(got, total, total // 2, flat)
    fold = put_folded(send, total // 2, total // 8)
    load = lambda at: add(okept[at, :], flat[at, :])
    split_rows(info, bit, 0, total // 2, rows, put_into(okeep), fold, load)


def third_split(info, vkept, okept, got, vkeep, okeep, send, flat, *, third, rows):
    total = vkept.shape[0]
    load = lambda at: add(vkept[at, :], got[at, :])
    split_rows(info, (third + 2) % 3, 0, total, rows, put_into(vkeep), put_into(send), load)
    unfold(got, total, total // 2, flat)
    okeep[...] = add(okept[...], flat[...])


def last_split(info, vkept, okept, got, keep, send, *, rows):
    total, columns = vkept.shape

    def put(target):
        def to(at, value):
            target[at : at + value.shape[0], : value.shape[1]] = value

        return to

    load = lambda at: add(vkept[at, :], got[at, :])
    split_rows(info, 3, 0, total, rows, put(keep), put(send), load)

    def side(target):
        def to(at, value):
            target[at : at + value.shape[0], columns:] = value

        return to

    split_rows(info, 3, 0, total, rows, side(keep), side(send), lambda at: okept[at, :])


def send_bit(value, bit):
    return swap(value, *every_bit()[bit])


def finish(keep, send, rows):
    value = keep.astype(f32) + send_bit(send, 3).astype(f32)
    for bit in range(4, len(every_bit())):
        axis, place = every_bit()[bit]
        value = value.astype(bf16).reshape(-1, 2, rows, value.shape[1])
        mine = (lax.axis_index(axis) >> place) & 1
        keep, send = (
            lax.dynamic_index_in_dim(value, side, 1, keepdims=False) for side in (mine, 1 - mine)
        )
        shape = (-1, value.shape[-1])
        value = keep.reshape(shape).astype(f32) + send_bit(send.reshape(shape), bit).astype(f32)
    return value


def sigmoid(v):
    return 0.5 + 0.5 * jnp.tanh(0.5 * v)


def row_mask(info, first, rows, limit):
    place = info[0] + first + lax.broadcasted_iota(jnp.int32, (rows, 1), 0)
    return ((place >= 0) & (place < limit)).astype(f32)


def halves_at(info, half):
    return (
        pl.multiple_of(info[3] * half, half),
        pl.multiple_of((1 - info[3]) * half, half),
    )


def prepare(info, *refs):
    count = (len(refs) - 1) // 2
    sem = refs[-1]
    copies = [
        pltpu.make_async_copy(refs[i], refs[count + i], sem.at[i]) for i in range(count)
    ]
    for c in copies:
        c.start()
    for c in copies:
        c.wait()


def pick(info, x, ct, last, first, sem):
    count = x.shape[0]
    copies = [
        pltpu.make_async_copy(source.at[a : a + n], target.at[b : b + n], sem.at[i])
        for i, (source, target, a, b, n) in enumerate(
            (
                (x, last, count - WIDE, 0, WIDE),
                (ct, last, count - NEAR, WIDE, NEAR),
                (x, first, 0, 0, WIDE),
                (ct, first, 0, WIDE, NEAR),
            )
        )
    ]
    for c in copies:
        c.start()
    for c in copies:
        c.wait()


def pack(info, before, after, halo):
    rows = before.shape[0]
    halo[:rows, :] = before[...]
    halo[rows:, :] = after[...]


def upstream(info, own, other, w_out, full, pull):
    count, half = own.shape
    mine, theirs = halves_at(info, half)
    full[:, pl.ds(mine, half)] = own[...]
    full[:, pl.ds(theirs, half)] = other[...]
    step = count // 2
    for c in range(0, count, step):
        pull[c : c + step, :] = dot(full[c : c + step, :], w_out[...], NT).astype(bf16)


def front(info, own, other, halo_own, halo_other, wv, wg, w_out, norm, rstd, hid, sig, slope, ends, edge):
    count, half = own.shape
    channels = wv.shape[1]
    mine, theirs = halves_at(info, half)

    def normalize(to, a, b):
        a, b = a.astype(f32), b.astype(f32)
        width = 2 * half
        mean = (jnp.sum(a, 1, keepdims=True) + jnp.sum(b, 1, keepdims=True)) / width
        a, b = a - mean, b - mean
        var = jnp.sum(a * a, 1, keepdims=True) + jnp.sum(b * b, 1, keepdims=True)
        inverse = lax.rsqrt(var / width + epsilon)
        norm[to, pl.ds(mine, half)] = (a * inverse).astype(bf16)
        norm[to, pl.ds(theirs, half)] = (b * inverse).astype(bf16)
        return inverse

    chunk = 64

    def body(i, _):
        at = pl.multiple_of(i * chunk, chunk)
        inverse = normalize(
            pl.ds(pl.multiple_of(WIDE + at, WIDE), chunk),
            own[pl.ds(at, chunk), :],
            other[pl.ds(at, chunk), :],
        )
        rstd[pl.ds(at, chunk), :] = jnp.broadcast_to(inverse, (chunk, LANES))
        return 0

    lax.fori_loop(0, count // chunk, body, 0, unroll=2)
    for to, at in ((0, 0), (WIDE + count, WIDE + NEAR)):
        normalize(pl.ds(to, WIDE), halo_own[at : at + WIDE, :], halo_other[at : at + WIDE, :])
    for a, at in ((halo_own, mine), (halo_other, theirs)):
        edge[:NEAR, pl.ds(at, half)] = a[WIDE : WIDE + NEAR, :]
        edge[NEAR:, pl.ds(at, half)] = a[2 * WIDE + NEAR :, :]
    ends[...] = dot(edge[...], w_out[...], NT)

    tile = channels // 3
    rows = count + 2 * WIDE
    step = rows // 2
    for n in range(0, channels, tile):
        cols = slice(n, n + tile)
        for c in range(0, rows, step):
            value = dot(norm[c : c + step, :], wv[:, cols])
            s = sigmoid(dot(norm[c : c + step, :], wg[:, cols]))
            keep = row_mask(info, c - WIDE, step, info[1])
            vs = value * s * keep
            hid[c : c + step, cols] = vs.astype(bf16)
            low, high = max(c, WIDE), min(c + step, WIDE + count)
            part = slice(low - c, high - c)
            sig[low - WIDE : high - WIDE, cols] = (s * keep)[part].astype(bf16)
            slope[low - WIDE : high - WIDE, cols] = (vs * (1.0 - s))[part].astype(bf16)


def tap_sums(source, base, groups, taps):
    sums = [None] * groups
    for residue in range(8):
        mine = list(range(residue, len(taps), 8))
        shifted = [
            source[pl.ds(base + 8 * i + residue, 8), :] for i in range(groups + len(mine) - 1)
        ]
        for i, k in enumerate(mine):
            for g in range(groups):
                term = shifted[g + i] * taps[k]
                sums[g] = term if sums[g] is None else sums[g] + term
    return sums


def tap_rows(taps, cols, reverse=False):
    values = taps[:, cols].astype(f32)
    order = range(taps.shape[0])
    return [
        jnp.broadcast_to(values[k : k + 1, :], (8, LANES))
        for k in (reversed(order) if reverse else order)
    ]


def lane_tile(n):
    return pl.ds(pl.multiple_of(n * LANES, LANES), LANES)


def paired(first, second):
    lane = lax.broadcasted_iota(jnp.int32, (first.shape[0], LANES), 1)
    return jnp.where(
        lane < LANES // 2,
        jnp.sum(first, axis=1, keepdims=True),
        jnp.sum(second, axis=1, keepdims=True),
    )


def depthwise(info, hid, taps, conv, stats, scratch, total, square):
    rows = conv.shape[0]
    skip = WIDE - NEAR - (taps.shape[0] - 1) // 2
    groups = 20
    total[...] = jnp.zeros_like(total)
    square[...] = jnp.zeros_like(square)

    def tile(n, _):
        cols = lane_tile(n)
        scratch[: hid.shape[0], :] = hid[:, cols].astype(f32)
        weights = tap_rows(taps, cols)

        def body(i, _):
            base = pl.multiple_of(i * 8 * groups, 8)
            for g, value in enumerate(tap_sums(scratch, base + skip, groups, weights)):
                at = pl.ds(base + 8 * g, 8)
                conv[at, cols] = value
                total[at, :] += value
                square[at, :] += value * value
            return 0

        lax.fori_loop(0, rows // (8 * groups), body, 0)
        return 0

    lax.fori_loop(0, conv.shape[1] // LANES, tile, 0)
    stats[...] = paired(total[...], square[...])


def moments(first, second, width):
    mean = (first[:, :1] + second[:, :1]) / width
    half = LANES // 2
    square = (first[:, half : half + 1] + second[:, half : half + 1]) / width
    return mean, lax.rsqrt(square - mean * mean + epsilon)


def swish(info, conv, pull, ends, own, other, swished, dswish, stats):
    count, channels = pull.shape

    def part(at, g, rows):
        to = pl.ds(at, rows)
        mean, inverse = moments(own[to, :], other[to, :], 2 * channels)
        zhat = (conv[to, :] - mean) * inverse
        s = sigmoid(zhat)
        zs = zhat * s
        d = g * (s + zs * (1.0 - s))
        dswish[to, :] = d
        stats[to, :] = paired(d, d * zhat)
        return zs.astype(bf16)

    part(0, ends[:NEAR, :], NEAR)
    part(NEAR + count, ends[NEAR:, :], NEAR)
    step = 32

    def body(i, _):
        at = pl.multiple_of(i * step, step)
        rows = pl.ds(at, step)
        g = pull[rows, :].astype(f32)
        swished[rows, :] = part(pl.multiple_of(at + NEAR, NEAR), g, step)
        return 0

    lax.fori_loop(0, count // step, body, 0, unroll=2)


def out_terms(info, full, swished, *refs, rows):
    halves, product = refs[:-1], refs[-1]
    width = full.shape[1]
    cols = swished.shape[1] // 3
    step = width // 4
    for c in range(0, width, step):
        product[c : c + step, :] = dot(full[:, c : c + step], swished[...], TN).astype(bf16)
    for i in range(3):
        load = lambda at: product[at, i * cols : (i + 1) * cols]
        keep, send = (put_into(half) for half in halves[2 * i : 2 * i + 2])
        split_rows(info, i, i, width, rows, keep, send, load)


def back(info, dswish, conv, own, other, own2, other2, taps, sig, slope, norm, dconv, dvg, product, scratch, coef, *, third):
    rows, channels = dswish.shape
    count = sig.shape[0]
    width = 2 * channels
    mean, inverse = moments(own[...], other[...], width)
    half = LANES // 2
    shift = (own2[:, :1] + other2[:, :1]) / width
    cross = (own2[:, half : half + 1] + other2[:, half : half + 1]) / width
    inverse = inverse * row_mask(info, -NEAR, rows, info[2])
    tilt = inverse * inverse * cross
    coef[0] = jnp.broadcast_to(inverse, (rows, LANES))
    coef[1] = jnp.broadcast_to(tilt, (rows, LANES))
    coef[2] = jnp.broadcast_to(tilt * mean - inverse * shift, (rows, LANES))
    tiles = channels // LANES // 3
    groups = 16
    skip = NEAR - (taps.shape[0] - 1) // 2

    def tile(n, _):
        local = lane_tile(n)
        cols = lane_tile(third * tiles + n)
        d = (coef[0] * dswish[:, cols] - coef[1] * conv[:, cols] + coef[2]).astype(bf16)
        dconv[:, local] = d
        scratch[:rows, :] = d.astype(f32)
        weights = tap_rows(taps, cols, reverse=True)

        def body(i, _):
            base = pl.multiple_of(i * 8 * groups, 16)
            sums = tap_sums(scratch, base + skip, groups, weights)
            for g in range(0, groups, 2):
                at = pl.ds(base + 8 * g, 16)
                dh = jnp.concatenate(sums[g : g + 2], axis=0)
                dvg[at, local] = (dh * sig[at, cols]).astype(bf16)
                dvg[at, lane_tile(tiles + n)] = (dh * slope[at, cols]).astype(bf16)
            return 0

        lax.fori_loop(0, count // (8 * groups), body, 0)
        return 0

    lax.fori_loop(0, tiles, tile, 0)
    step = width // 4
    for c in range(0, width, step):
        r = dot(norm[WIDE : WIDE + count, c : c + step], dvg[...], TN)
        product[c : c + step, :] = r.astype(bf16)


def taps_sums(info, dconv, hid, out, scratch, total, *, third):
    rows, channels = dconv.shape
    count = rows - 2 * NEAR
    taps = out.shape[0]
    half = (taps - 1) // 2
    groups = 16
    tiles = channels // LANES

    def tile(n, _):
        local = lane_tile(n)
        cols = lane_tile(third * tiles + n)
        scratch[:rows, :] = dconv[:, local].astype(f32)
        total[...] = jnp.zeros_like(total)

        def body(i, _):
            base = pl.multiple_of(i * 8 * groups, 16)
            h = []
            for g in range(0, groups, 2):
                both = hid[pl.ds(pl.multiple_of(WIDE + base + 8 * g, 16), 16), cols].astype(f32)
                h += [both[:8], both[8:]]
            for residue in range(8):
                mine = list(range(residue, taps, 8))
                shifted = [
                    scratch[pl.ds(base + NEAR - half + 8 * g + residue, 8), :]
                    for g in range(groups + len(mine) - 1)
                ]
                for j, m in enumerate(mine):
                    term = shifted[j] * h[0]
                    for g in range(1, groups):
                        term = term + shifted[g + j] * h[g]
                    total[taps - 1 - m] += term
            return 0

        lax.fori_loop(0, count // (8 * groups), body, 0)
        out[:, local] = jnp.sum(total[...], axis=1)
        return 0

    lax.fori_loop(0, tiles, tile, 0)


def add_taps(info, value, got, result):
    result[...] = value[...] + got[...]


def out_half(info, swished, w_out, result, *, own):
    half = result.shape[1]
    at = halves_at(info, half)[0 if own else 1]
    step = swished.shape[0] // 2
    for r in range(0, swished.shape[0], step):
        part = dot(swished[r : r + step, :], w_out[:, pl.ds(at, half)])
        result[r : r + step, :] = part.astype(result.dtype)


def norm_half(info, a, b, c, wv, wg, *results, own):
    half = results[0].shape[1]
    at = halves_at(info, half)[0 if own else 1]
    third = half // 3
    step = a.shape[0] // 2
    for n, result in enumerate(results):
        r = n * step
        total = None
        for i, dvg in enumerate((a, b, c)):
            cols = slice(i * third, (i + 1) * third)
            for j, w in enumerate((wv, wg)):
                part = dot(
                    dvg[r : r + step, j * third : (j + 1) * third], w[pl.ds(at, half), cols], NT
                )
                total = part if total is None else total + part
        result[...] = total.astype(result.dtype)


def norm_sums(info, mine0, mine1, got0, got1, norm, total, stats):
    count, half = total.shape
    at = halves_at(info, half)[0]
    step = 32
    for n, (mine, got) in enumerate(((mine0, got0), (mine1, got1))):
        start = n * count // 2

        def body(i, _):
            here = pl.multiple_of(i * step, step)
            rows, to = pl.ds(here, step), pl.ds(start + here, step)
            xhat = norm[pl.ds(WIDE + start + here, step), pl.ds(at, half)]
            d = mine[rows, :] + got[rows, :].astype(f32)
            total[to, :] = d
            stats[to, :] = paired(d, d * xhat.astype(f32))
            return 0

        lax.fori_loop(0, count // 2 // step, body, 0, unroll=2)


def written(result, buffer, sem, part):
    count, step = buffer.shape[0], buffer.shape[0] // sem.shape[0]
    copies = []
    for i in range(sem.shape[0]):
        rows = slice(i * step, (i + 1) * step)
        buffer[rows, :] = part(i * step, step)
        copies.append(pltpu.make_async_copy(buffer.at[rows], result.at[rows], sem.at[i]))
        copies[-1].start()
    for c in copies:
        c.wait()


def input_rows(info, ct, total, norm, rstd, own, other, result, buffer, sem):
    count, half = total.shape
    at = halves_at(info, half)[0]

    def part(first, step):
        rows = slice(first, first + step)
        xhat = norm[WIDE + first : WIDE + first + step, pl.ds(at, half)].astype(f32)
        sums = (own[rows, :] + other[rows, :]) / (2 * half)
        mean, cross = sums[:, :1], sums[:, LANES // 2 : LANES // 2 + 1]
        gradient = rstd[rows, :1] * (total[rows, :] - mean - xhat * cross)
        return (ct[rows, :].astype(f32) + gradient).astype(bf16)

    written(result, buffer, sem, part)


def output_rows(info, x, mine, got, result, buffer, sem):
    def part(first, step):
        rows = slice(first, first + step)
        return (x[rows, :].astype(f32) + mine[rows, :] + got[rows, :].astype(f32)).astype(bf16)

    written(result, buffer, sem, part)


def shards(inputs, lengths, cotangent, w_value, w_gate, kernel, w_out):
    x, ct = inputs[0], cotangent[0]
    count, channels = x.shape
    width = channels * lax.axis_size("tensor")
    core = lax.axis_index("tensor")
    peers = lax.axis_size("seq")
    every = every_bit()
    block = width >> len(every)
    taps = kernel.shape[0]
    info = jnp.stack(
        [lax.axis_index("seq") * count, lengths[0], jnp.int32(peers * count), core]
        + [(lax.axis_index(a) >> b) & 1 for a, b in every]
    ).astype(jnp.int32)

    up = [(i, i + 1) for i in range(peers - 1)]
    down = [(j, i) for i, j in up]
    x_other, ct_other = swap(x, "tensor"), swap(ct, "tensor")
    last, first, mark = run(
        pick,
        info,
        [x, ct],
        [((WIDE + NEAR, channels), bf16)] * 2,
        scratch=[pltpu.SemaphoreType.DMA((4,))],
        space=HBM,
    )
    before, after = lax.ppermute(last, "seq", up), lax.ppermute(first, "seq", down)
    moved = [x, ct, w_value, w_gate, w_out]
    xv, ctv, wv, wg, wo, mark = run(
        prepare,
        info,
        moved,
        [(a.shape, bf16) for a in moved],
        scratch=[pltpu.SemaphoreType.DMA((len(moved),))],
        after=[mark],
        space=HBM,
    )

    rows, ext = count + 2 * NEAR, count + 2 * WIDE
    full, pull, mark = run(
        upstream, info, [ctv, ct_other, wo], [((count, width), bf16), ((count, channels), bf16)]
    )
    halo, mark = run(
        pack, info, [before, after], [((2 * (WIDE + NEAR), channels), bf16)], after=[mark]
    )
    halo_other = swap(halo, "tensor")
    norm, rstd, hid, sig, slope, ends, _ = run(
        front,
        info,
        [xv, x_other, halo, halo_other, wv, wg, wo],
        [
            ((ext, width), bf16),
            ((count, LANES), f32),
            ((ext, channels), bf16),
            ((count, channels), bf16),
            ((count, channels), bf16),
            ((2 * NEAR, channels), f32),
        ],
        scratch=[pltpu.VMEM((2 * NEAR, width), bf16)],
        after=[mark],
    )
    row_sums = ((rows, LANES), f32)
    column = pltpu.VMEM((rows, LANES), f32)
    conv, stats, _ = run(
        depthwise,
        info,
        [hid, kernel],
        [((rows, channels), f32), row_sums],
        scratch=[pltpu.VMEM((ext + 16, LANES), f32), column, column],
    )
    stats_other = swap(stats, "tensor")
    swished, dswish, stats2, _ = run(
        swish,
        info,
        [conv, pull, ends, stats, stats_other],
        [((count, channels), bf16), ((rows, channels), f32), row_sums],
    )
    stats2_other = swap(stats2, "tensor")

    third = channels // 3
    *out_parts, mark = run(
        functools.partial(out_terms, rows=block),
        info,
        [full, swished],
        [((width // 2, third), bf16)] * 6,
        scratch=[pltpu.VMEM((width, channels), bf16)],
    )
    out_got = [send_bit(out_parts[2 * i + 1], i) for i in range(3)]

    def out_part(own, mark):
        return run(
            functools.partial(out_half, own=own),
            info,
            [swished, wo],
            [((count, channels), f32 if own else bf16)],
            after=[mark],
        )

    dconvs, dvgs, kept, got = [], [], [], []
    for i in range(3):
        dconv, dvg, product, mark = run(
            functools.partial(back, third=i),
            info,
            [dswish, conv, stats, stats_other, stats2, stats2_other, kernel, sig, slope, norm],
            [((rows, third), bf16), ((count, 2 * third), bf16), ((width, 2 * third), bf16)],
            scratch=[pltpu.VMEM((rows + 16, LANES), f32), pltpu.VMEM((3, rows, LANES), f32)],
            after=[mark],
        )
        if i == 0:
            out_theirs, mark = out_part(False, mark)
            out_other = swap(out_theirs, "tensor")
            out_mine, mark = out_part(True, mark)
        previous = (i + 2) % 3
        vkeep, okeep, send, mark = run(
            functools.partial(first_split, third=i, rows=block),
            info,
            [product, out_parts[2 * previous], out_got[previous]],
            [
                ((width // 2, 2 * third), bf16),
                ((width // 4, third), bf16),
                ((width // 2 + width // 8, 2 * third), bf16),
            ],
            after=[mark, *out_got],
        )
        dconvs.append(dconv)
        dvgs.append(dvg)
        kept.append((vkeep, okeep))
        got.append(send_bit(send, i))

    def second(i, mark):
        vkeep, okeep, send, mark = run(
            functools.partial(second_split, third=i, rows=block),
            info,
            [*kept[i], got[i]],
            [
                ((width // 4, 2 * third), bf16),
                ((width // 8, third), bf16),
                ((width // 4 + width // 16, 2 * third), bf16),
            ],
            scratch=[pltpu.VMEM((width // 4, third), bf16)],
            after=[mark],
        )
        kept[i], got[i] = (vkeep, okeep), send_bit(send, (i + 1) % 3)
        return mark

    def third_step(i, mark):
        vkeep, okeep, send, mark = run(
            functools.partial(third_split, third=i, rows=block),
            info,
            [*kept[i], got[i]],
            [
                ((width // 8, 2 * third), bf16),
                ((width // 8, third), bf16),
                ((width // 8, 2 * third), bf16),
            ],
            scratch=[pltpu.VMEM((width // 8, third), bf16)],
            after=[mark],
        )
        kept[i], got[i] = (vkeep, okeep), send_bit(send, (i + 2) % 3)
        return mark

    def last_step(i, mark):
        keep, send, mark = run(
            functools.partial(last_split, rows=block),
            info,
            [*kept[i], got[i]],
            [((width // 16, 3 * third), bf16)] * 2,
            after=[mark],
        )
        return finish(keep, send, block), mark

    def norm_part(own, mark):
        return run(
            functools.partial(norm_half, own=own),
            info,
            [*dvgs, wv, wg],
            [((count // 2, channels), f32 if own else bf16)] * 2,
            after=[mark],
        )

    def taps_part(i, mark):
        return run(
            functools.partial(taps_sums, third=i),
            info,
            [dconvs[i], hid],
            [((taps, third), f32)],
            scratch=[pltpu.VMEM((rows + 16, LANES), f32), pltpu.VMEM((taps, 8, LANES), f32)],
            after=[mark],
        )

    def final(kernel, args, mark):
        return run(
            kernel,
            info,
            args,
            [((count, channels), bf16)],
            scratch=[pltpu.VMEM((count, channels), bf16), pltpu.SemaphoreType.DMA((4,))],
            after=[mark],
            to=HBM,
        )

    def taps_step(bit, value, mark):
        return run(
            add_taps, info, [value, send_bit(value, bit)], [(value.shape, f32)], after=[mark]
        )

    parts = []
    for i in range(3):
        part, mark = taps_part(i, mark)
        parts.append(part)
    kernel_grad = jnp.concatenate(parts, axis=1)
    *theirs, mark = norm_part(False, mark)
    theirs = [swap(t, "tensor") for t in theirs]
    *mine, mark = norm_part(True, mark)
    mark = second(0, mark)
    kernel_grad, mark = taps_step(0, kernel_grad, mark)
    mark = second(1, mark)
    dnorm, stats3, mark = run(
        norm_sums,
        info,
        [*mine, *theirs, norm],
        [((count, channels), f32), ((count, LANES), f32)],
        after=[mark],
    )
    stats3_other = swap(stats3, "tensor")
    output, mark = final(output_rows, [x, out_mine, out_other], mark)
    kernel_grad, mark = taps_step(1, kernel_grad, mark)
    mark = second(2, mark)
    input_gradient, mark = final(
        input_rows, [ct, dnorm, norm, rstd, stats3, stats3_other], mark
    )
    mark = third_step(0, mark)
    kernel_grad, mark = taps_step(2, kernel_grad, mark)
    for i in (1, 2):
        mark = third_step(i, mark)
    for bit in range(3, len(every)):
        kernel_grad, mark = taps_step(bit, kernel_grad, mark)
    totals = []
    for i in range(3):
        total, mark = last_step(i, mark)
        totals.append(total)
    value_grad, gate_grad = (
        jnp.concatenate([t[:, j * third : (j + 1) * third] for t in totals], axis=1)
        for j in (0, 1)
    )
    out_grad = jnp.concatenate([totals[(i + 1) % 3][:, 2 * third :] for i in range(3)], axis=1).T
    return (
        output[None],
        input_gradient[None],
        value_grad,
        gate_grad,
        kernel_grad,
        out_grad,
    )


def solution(mesh):
    return jax.shard_map(
        shards,
        mesh=mesh,
        in_specs=(
            P("dp", "seq", "tensor"),
            P("dp"),
            P("dp", "seq", "tensor"),
            P(None, "tensor"),
            P(None, "tensor"),
            P(None, "tensor"),
            P("tensor", None),
        ),
        out_specs=(
            P("dp", "seq", "tensor"),
            P("dp", "seq", "tensor"),
            P(("seq", "dp"), "tensor"),
            P(("seq", "dp"), "tensor"),
            P(None, "tensor"),
            P("tensor", ("seq", "dp")),
        ),
        check_vma=False,
    )
```

```python
import functools

import jax
import jax.numpy as jnp
from jax import lax
from jax.experimental import pallas as pl
from jax.experimental.pallas import tpu as pltpu
from jax.sharding import PartitionSpec as P

epsilon = 1e-05
f32, bf16 = jnp.float32, jnp.bfloat16
LANES = 128
WIDE, NEAR = 32, 16
NN = (((1,), (0,)), ((), ()))
NT = (((1,), (1,)), ((), ()))
TN = (((0,), (0,)), ((), ()))
VMEM = pl.BlockSpec(memory_space=pltpu.VMEM)
SMEM = pl.BlockSpec(memory_space=pltpu.SMEM)
ANY = pl.BlockSpec(memory_space=pl.ANY)
HBM = pl.BlockSpec(memory_space=pltpu.HBM)


def dot(a, b, dims=NN):
    return lax.dot_general(a, b, dims, preferred_element_type=f32)


def run(kernel, info, args, outs, scratch=(), after=(), limit=8, space=VMEM, to=VMEM, far=()):
    near = len(args)

    def body(*refs):
        lead = 1 + near + len(far)
        rest = refs[lead + len(after) :]
        kernel(*refs[:lead], *rest[: len(outs)], *rest[len(outs) + 1 :])
        rest[len(outs)][...] = jnp.zeros((8, LANES), f32)

    args = [pltpu.with_memory_space_constraint(a, space.memory_space) for a in args]
    args += [pltpu.with_memory_space_constraint(a, pltpu.HBM) for a in far]
    *results, mark = pl.pallas_call(
        body,
        in_specs=[SMEM] + [space] * near + [HBM] * len(far) + [ANY] * len(after),
        out_specs=[to] * len(outs) + [VMEM],
        out_shape=[to.memory_space(shape, dtype) for shape, dtype in outs]
        + [pltpu.VMEM((8, LANES), f32)],
        scratch_shapes=list(scratch),
        compiler_params=pltpu.CompilerParams(vmem_limit_bytes=limit << 20),
        cost_estimate=pl.CostEstimate(flops=COST, bytes_accessed=COST, transcendentals=0),
        name=kernel.__name__ if hasattr(kernel, "__name__") else kernel.func.__name__,
    )(info, *args, *after)
    return *results, mark


COST = 1 << 10


def swap(value, axis, bit=0):
    size = lax.axis_size(axis)
    return lax.ppermute(value, axis, [(i, i ^ (1 << bit)) for i in range(size)])


def bits_of(axis):
    return [(axis, b) for b in range(lax.axis_size(axis).bit_length() - 1)]


def every_bit():
    return bits_of("dp") + bits_of("seq")


def split_rows(info, bit, place, total, rows, keep, send, load):
    run_length = rows << place
    for j in range(total // (2 * run_length)):
        for put, side in ((keep, info[4 + bit]), (send, 1 - info[4 + bit])):
            if run_length % 32:
                low, high = (
                    load(slice((2 * j + i) * run_length, (2 * j + i + 1) * run_length))
                    for i in (0, 1)
                )
                value = jnp.where(side == 0, low, high)
            else:
                at = pl.multiple_of((2 * j + side) * run_length, run_length)
                value = load(pl.ds(at, run_length))
            put(j * run_length, value)


def put_into(target):
    def put(at, value):
        target[at : at + value.shape[0], :] = value

    return put


def put_folded(target, first, half):
    columns = target.shape[1] // 2

    def put(at, value):
        length = value.shape[0]
        for low in range(0, length, min(length, half)):
            part = value[low : low + min(length, half)]
            side, row = divmod(at + low, half)
            to = slice(first + row, first + row + part.shape[0])
            target[to, side * columns : (side + 1) * columns] = part

    return put


def add(a, b):
    return (a.astype(f32) + b.astype(f32)).astype(bf16)


def first_split(info, product, okept, ogot, vkeep, okeep, send, *, third, rows):
    total = product.shape[0]
    split_rows(info, third, third, total, rows, put_into(vkeep), put_into(send), lambda at: product[at, :])
    before = (third + 2) % 3
    place = third - (before < third)
    fold = put_folded(send, total // 2, total // 8)
    load = lambda at: add(okept[at, :], ogot[at, :])
    split_rows(info, third, place, total // 2, rows, put_into(okeep), fold, load)


def unfold(got, first, rows, target):
    half = rows // 2
    columns = target.shape[1]
    target[:half, :] = got[first : first + half, :columns]
    target[half:, :] = got[first : first + half, columns:]


def ride(taps, send):
    rows, columns = taps.shape[0], send.shape[1]
    value = taps[...].astype(bf16)
    first = send.shape[0] - rows - rows // 2
    send[first : first + rows, :] = value[:, :columns]
    send[first + rows :, : columns // 2] = value[: rows // 2, columns:]
    send[first + rows :, columns // 2 :] = value[rows // 2 :, columns:]


def alight(taps, got, result):
    rows, columns = taps.shape[0], got.shape[1]
    first = got.shape[0] - rows - rows // 2
    value = taps[...].astype(bf16).astype(f32)
    half = rows // 2
    result[:, :columns] = value[:, :columns] + got[first : first + rows, :].astype(f32)
    result[:half, columns:] = value[:half, columns:] + got[
        first + rows :, : columns // 2
    ].astype(f32)
    result[half:, columns:] = value[half:, columns:] + got[
        first + rows :, columns // 2 :
    ].astype(f32)


def second_split(info, vkept, okept, got, *refs, third, rows):
    *taps, vkeep, okeep, send, flat = refs
    if taps:
        ride(taps[0], send)
    total = vkept.shape[0]
    bit = (third + 1) % 3
    left = [b for b in range(3) if b != third]
    load = lambda at: add(vkept[at, :], got[at, :])
    split_rows(info, bit, left.index(bit), total, rows, put_into(vkeep), put_into(send), load)
    unfold(got, total, total // 2, flat)
    fold = put_folded(send, total // 2, total // 8)
    load = lambda at: add(okept[at, :], flat[at, :])
    split_rows(info, bit, 0, total // 2, rows, put_into(okeep), fold, load)


def third_split(info, vkept, okept, got, *refs, third, rows):
    if third == 1:
        taps, vkeep, okeep, send, sums, flat = refs
        alight(taps, got, sums)
    elif third == 2:
        sums, vkeep, okeep, send, flat = refs
        ride(sums, send)
    else:
        vkeep, okeep, send, flat = refs
    total = vkept.shape[0]
    load = lambda at: add(vkept[at, :], got[at, :])
    split_rows(info, (third + 2) % 3, 0, total, rows, put_into(vkeep), put_into(send), load)
    unfold(got, total, total // 2, flat)
    okeep[...] = add(okept[...], flat[...])


def last_split(info, vkept, okept, got, *refs, rows):
    keep, send = refs[len(refs) // 4 :][:2]
    total, columns = vkept.shape
    if len(refs) > 2:
        alight(refs[0], got, refs[3])
        keep[total // 2 :, :] = refs[3][...].astype(bf16)
        send[total // 2 :, :] = refs[3][...].astype(bf16)

    def put(target):
        def to(at, value):
            target[at : at + value.shape[0], : value.shape[1]] = value

        return to

    load = lambda at: add(vkept[at, :], got[at, :])
    split_rows(info, 3, 0, total, rows, put(keep), put(send), load)

    def side(target):
        def to(at, value):
            target[at : at + value.shape[0], columns:] = value

        return to

    split_rows(info, 3, 0, total, rows, side(keep), side(send), lambda at: okept[at, :])


def send_bit(value, bit):
    return swap(value, *every_bit()[bit])


def finish(keep, send, rows, riding):
    value = keep.astype(f32) + send_bit(send, 3).astype(f32)
    value, behind = value[: value.shape[0] - riding], value[value.shape[0] - riding :]
    for bit in range(4, len(every_bit())):
        axis, place = every_bit()[bit]
        value = value.astype(bf16).reshape(-1, 2, rows, value.shape[1])
        mine = (lax.axis_index(axis) >> place) & 1
        keep, send = (
            lax.dynamic_index_in_dim(value, side, 1, keepdims=False) for side in (mine, 1 - mine)
        )
        shape = (-1, value.shape[-1])
        value = keep.reshape(shape).astype(f32) + send_bit(send.reshape(shape), bit).astype(f32)
    return value, behind


def sigmoid(v):
    return 0.5 + 0.5 * jnp.tanh(0.5 * v)


def row_mask(info, first, rows, limit):
    place = info[0] + first + lax.broadcasted_iota(jnp.int32, (rows, 1), 0)
    return ((place >= 0) & (place < limit)).astype(f32)


def halves_at(info, half):
    return (
        pl.multiple_of(info[3] * half, half),
        pl.multiple_of((1 - info[3]) * half, half),
    )


def start_all(pairs, sem):
    copies = [pltpu.make_async_copy(a, b, sem.at[i]) for i, (a, b) in enumerate(pairs)]
    for c in copies:
        c.start()
    return copies


def prepare(info, ct, w_out, ct_to, w_to, sem):
    for c in start_all([(w_out, w_to), (ct, ct_to)], sem):
        c.wait()


def pick(info, x, ct, last, first, sem):
    count = x.shape[0]
    copies = [
        pltpu.make_async_copy(source.at[a : a + n], target.at[b : b + n], sem.at[i])
        for i, (source, target, a, b, n) in enumerate(
            (
                (x, last, count - WIDE, 0, WIDE),
                (ct, last, count - NEAR, WIDE, NEAR),
                (x, first, 0, 0, WIDE),
                (ct, first, 0, WIDE, NEAR),
            )
        )
    ]
    for c in copies:
        c.start()
    for c in copies:
        c.wait()


def pack(info, before, after, halo):
    rows = before.shape[0]
    halo[:rows, :] = before[...]
    halo[rows:, :] = after[...]


def upstream(info, own, other, w_out, x, wv, wg, full, pull, x_to, wv_to, wg_to, sem):
    count, half = own.shape
    copies = start_all([(x, x_to), (wv, wv_to), (wg, wg_to)], sem)
    mine, theirs = halves_at(info, half)
    full[:, pl.ds(mine, half)] = own[...]
    full[:, pl.ds(theirs, half)] = other[...]
    step = count // 2
    for c in range(0, count, step):
        pull[c : c + step, :] = dot(full[c : c + step, :], w_out[...], NT).astype(bf16)
    for c in copies:
        c.wait()


def front(info, own, other, halo_own, halo_other, wv, wg, w_out, norm, rstd, hid, sig, slope, ends, edge):
    count, half = own.shape
    channels = wv.shape[1]
    mine, theirs = halves_at(info, half)

    def normalize(to, a, b):
        a, b = a.astype(f32), b.astype(f32)
        width = 2 * half
        mean = (jnp.sum(a, 1, keepdims=True) + jnp.sum(b, 1, keepdims=True)) / width
        a, b = a - mean, b - mean
        var = jnp.sum(a * a, 1, keepdims=True) + jnp.sum(b * b, 1, keepdims=True)
        inverse = lax.rsqrt(var / width + epsilon)
        norm[to, pl.ds(mine, half)] = (a * inverse).astype(bf16)
        norm[to, pl.ds(theirs, half)] = (b * inverse).astype(bf16)
        return inverse

    chunk = 64

    def body(i, _):
        at = pl.multiple_of(i * chunk, chunk)
        inverse = normalize(
            pl.ds(pl.multiple_of(WIDE + at, WIDE), chunk),
            own[pl.ds(at, chunk), :],
            other[pl.ds(at, chunk), :],
        )
        rstd[pl.ds(at, chunk), :] = jnp.broadcast_to(inverse, (chunk, LANES))
        return 0

    lax.fori_loop(0, count // chunk, body, 0, unroll=2)
    for to, at in ((0, 0), (WIDE + count, WIDE + NEAR)):
        normalize(pl.ds(to, WIDE), halo_own[at : at + WIDE, :], halo_other[at : at + WIDE, :])
    for a, at in ((halo_own, mine), (halo_other, theirs)):
        edge[:NEAR, pl.ds(at, half)] = a[WIDE : WIDE + NEAR, :]
        edge[NEAR:, pl.ds(at, half)] = a[2 * WIDE + NEAR :, :]
    ends[...] = dot(edge[...], w_out[...], NT)

    tile = channels // 3
    rows = count + 2 * WIDE
    step = rows // 2
    for n in range(0, channels, tile):
        cols = slice(n, n + tile)
        for c in range(0, rows, step):
            value = dot(norm[c : c + step, :], wv[:, cols])
            s = sigmoid(dot(norm[c : c + step, :], wg[:, cols]))
            keep = row_mask(info, c - WIDE, step, info[1])
            vs = value * s * keep
            hid[c : c + step, cols] = vs.astype(bf16)
            low, high = max(c, WIDE), min(c + step, WIDE + count)
            part = slice(low - c, high - c)
            sig[low - WIDE : high - WIDE, cols] = (s * keep)[part].astype(bf16)
            slope[low - WIDE : high - WIDE, cols] = (vs * (1.0 - s))[part].astype(bf16)


def tap_sums(source, base, groups, taps):
    sums = [None] * groups
    for residue in range(8):
        mine = list(range(residue, len(taps), 8))
        shifted = [
            source[pl.ds(base + 8 * i + residue, 8), :] for i in range(groups + len(mine) - 1)
        ]
        for i, k in enumerate(mine):
            for g in range(groups):
                term = shifted[g + i] * taps[k]
                sums[g] = term if sums[g] is None else sums[g] + term
    return sums


def tap_rows(taps, cols, reverse=False):
    values = taps[:, cols].astype(f32)
    order = range(taps.shape[0])
    return [
        jnp.broadcast_to(values[k : k + 1, :], (8, LANES))
        for k in (reversed(order) if reverse else order)
    ]


def lane_tile(n):
    return pl.ds(pl.multiple_of(n * LANES, LANES), LANES)


def paired(first, second):
    lane = lax.broadcasted_iota(jnp.int32, (first.shape[0], LANES), 1)
    return jnp.where(
        lane < LANES // 2,
        jnp.sum(first, axis=1, keepdims=True),
        jnp.sum(second, axis=1, keepdims=True),
    )


def depthwise(info, hid, taps, conv, stats, scratch, total, square):
    rows = conv.shape[0]
    skip = WIDE - NEAR - (taps.shape[0] - 1) // 2
    groups = 20
    total[...] = jnp.zeros_like(total)
    square[...] = jnp.zeros_like(square)

    def tile(n, _):
        cols = lane_tile(n)
        scratch[: hid.shape[0], :] = hid[:, cols].astype(f32)
        weights = tap_rows(taps, cols)

        def body(i, _):
            base = pl.multiple_of(i * 8 * groups, 8)
            for g, value in enumerate(tap_sums(scratch, base + skip, groups, weights)):
                at = pl.ds(base + 8 * g, 8)
                conv[at, cols] = value
                total[at, :] += value
                square[at, :] += value * value
            return 0

        lax.fori_loop(0, rows // (8 * groups), body, 0)
        return 0

    lax.fori_loop(0, conv.shape[1] // LANES, tile, 0)
    stats[...] = paired(total[...], square[...])


def moments(first, second, width):
    mean = (first[:, :1] + second[:, :1]) / width
    half = LANES // 2
    square = (first[:, half : half + 1] + second[:, half : half + 1]) / width
    return mean, lax.rsqrt(square - mean * mean + epsilon)


def swish(info, conv, pull, ends, own, other, swished, dswish, stats):
    count, channels = pull.shape

    def part(at, g, rows):
        to = pl.ds(at, rows)
        mean, inverse = moments(own[to, :], other[to, :], 2 * channels)
        zhat = (conv[to, :] - mean) * inverse
        s = sigmoid(zhat)
        zs = zhat * s
        d = g * (s + zs * (1.0 - s))
        dswish[to, :] = d
        stats[to, :] = paired(d, d * zhat)
        return zs.astype(bf16)

    part(0, ends[:NEAR, :], NEAR)
    part(NEAR + count, ends[NEAR:, :], NEAR)
    step = 32

    def body(i, _):
        at = pl.multiple_of(i * step, step)
        rows = pl.ds(at, step)
        g = pull[rows, :].astype(f32)
        swished[rows, :] = part(pl.multiple_of(at + NEAR, NEAR), g, step)
        return 0

    lax.fori_loop(0, count // step, body, 0, unroll=2)


def out_terms(info, full, swished, *refs, rows):
    halves, product = refs[:-1], refs[-1]
    width = full.shape[1]
    cols = swished.shape[1] // 3
    step = width // 4
    for c in range(0, width, step):
        product[c : c + step, :] = dot(full[:, c : c + step], swished[...], TN).astype(bf16)
    for i in range(3):
        load = lambda at: product[at, i * cols : (i + 1) * cols]
        keep, send = (put_into(half) for half in halves[2 * i : 2 * i + 2])
        split_rows(info, i, i, width, rows, keep, send, load)


def back(info, dswish, conv, own, other, own2, other2, taps, sig, slope, norm, dconv, dvg, product, scratch, coef, *, third):
    rows, channels = dswish.shape
    count = sig.shape[0]
    width = 2 * channels
    mean, inverse = moments(own[...], other[...], width)
    half = LANES // 2
    shift = (own2[:, :1] + other2[:, :1]) / width
    cross = (own2[:, half : half + 1] + other2[:, half : half + 1]) / width
    inverse = inverse * row_mask(info, -NEAR, rows, info[2])
    tilt = inverse * inverse * cross
    coef[0] = jnp.broadcast_to(inverse, (rows, LANES))
    coef[1] = jnp.broadcast_to(tilt, (rows, LANES))
    coef[2] = jnp.broadcast_to(tilt * mean - inverse * shift, (rows, LANES))
    tiles = channels // LANES // 3
    groups = 16
    skip = NEAR - (taps.shape[0] - 1) // 2

    def tile(n, _):
        local = lane_tile(n)
        cols = lane_tile(third * tiles + n)
        d = (coef[0] * dswish[:, cols] - coef[1] * conv[:, cols] + coef[2]).astype(bf16)
        dconv[:, local] = d
        scratch[:rows, :] = d.astype(f32)
        weights = tap_rows(taps, cols, reverse=True)

        def body(i, _):
            base = pl.multiple_of(i * 8 * groups, 16)
            sums = tap_sums(scratch, base + skip, groups, weights)
            for g in range(0, groups, 2):
                at = pl.ds(base + 8 * g, 16)
                dh = jnp.concatenate(sums[g : g + 2], axis=0)
                dvg[at, local] = (dh * sig[at, cols]).astype(bf16)
                dvg[at, lane_tile(tiles + n)] = (dh * slope[at, cols]).astype(bf16)
            return 0

        lax.fori_loop(0, count // (8 * groups), body, 0)
        return 0

    lax.fori_loop(0, tiles, tile, 0)
    step = width // 4
    for c in range(0, width, step):
        r = dot(norm[WIDE : WIDE + count, c : c + step], dvg[...], TN)
        product[c : c + step, :] = r.astype(bf16)


def taps_sums(info, dconv, hid, out, scratch, total, *, third):
    rows, channels = dconv.shape
    count = rows - 2 * NEAR
    taps = total.shape[0]
    half = (taps - 1) // 2
    groups = 16
    tiles = channels // LANES

    def tile(n, _):
        local = lane_tile(n)
        cols = lane_tile(third * tiles + n)
        scratch[:rows, :] = dconv[:, local].astype(f32)
        total[...] = jnp.zeros_like(total)

        def body(i, _):
            base = pl.multiple_of(i * 8 * groups, 16)
            h = []
            for g in range(0, groups, 2):
                both = hid[pl.ds(pl.multiple_of(WIDE + base + 8 * g, 16), 16), cols].astype(f32)
                h += [both[:8], both[8:]]
            for residue in range(8):
                mine = list(range(residue, taps, 8))
                shifted = [
                    scratch[pl.ds(base + NEAR - half + 8 * g + residue, 8), :]
                    for g in range(groups + len(mine) - 1)
                ]
                for j, m in enumerate(mine):
                    term = shifted[j] * h[0]
                    for g in range(1, groups):
                        term = term + shifted[g + j] * h[g]
                    total[taps - 1 - m] += term
            return 0

        lax.fori_loop(0, count // (8 * groups), body, 0)
        out[:taps, local] = jnp.sum(total[...], axis=1)
        out[taps:, local] = jnp.zeros((out.shape[0] - taps, LANES), f32)
        return 0

    lax.fori_loop(0, tiles, tile, 0)


def add_taps(info, value, got, result):
    result[...] = value[...] + got[...]


def out_half(info, swished, w_out, result, *, own):
    half = result.shape[1]
    at = halves_at(info, half)[0 if own else 1]
    step = swished.shape[0] // 2
    for r in range(0, swished.shape[0], step):
        part = dot(swished[r : r + step, :], w_out[:, pl.ds(at, half)])
        result[r : r + step, :] = part.astype(result.dtype)


def norm_half(info, a, b, c, wv, wg, *results, own):
    half = results[0].shape[1]
    at = halves_at(info, half)[0 if own else 1]
    third = half // 3
    step = a.shape[0] // 2
    for n, result in enumerate(results):
        r = n * step
        total = None
        for i, dvg in enumerate((a, b, c)):
            cols = slice(i * third, (i + 1) * third)
            for j, w in enumerate((wv, wg)):
                part = dot(
                    dvg[r : r + step, j * third : (j + 1) * third], w[pl.ds(at, half), cols], NT
                )
                total = part if total is None else total + part
        result[...] = total.astype(result.dtype)


def norm_sums(info, mine0, mine1, got0, got1, norm, total, stats):
    count, half = total.shape
    at = halves_at(info, half)[0]
    step = 32
    for n, (mine, got) in enumerate(((mine0, got0), (mine1, got1))):
        start = n * count // 2

        def body(i, _):
            here = pl.multiple_of(i * step, step)
            rows, to = pl.ds(here, step), pl.ds(start + here, step)
            xhat = norm[pl.ds(WIDE + start + here, step), pl.ds(at, half)]
            d = mine[rows, :] + got[rows, :].astype(f32)
            total[to, :] = d
            stats[to, :] = paired(d, d * xhat.astype(f32))
            return 0

        lax.fori_loop(0, count // 2 // step, body, 0, unroll=2)


def written(result, buffer, sem, part):
    count, step = buffer.shape[0], buffer.shape[0] // sem.shape[0]
    copies = []
    for i in range(sem.shape[0]):
        rows = slice(i * step, (i + 1) * step)
        buffer[rows, :] = part(i * step, step)
        copies.append(pltpu.make_async_copy(buffer.at[rows], result.at[rows], sem.at[i]))
        copies[-1].start()
    for c in copies:
        c.wait()


def input_rows(info, ct, total, norm, rstd, own, other, result, buffer, sem):
    count, half = total.shape
    at = halves_at(info, half)[0]

    def part(first, step):
        rows = slice(first, first + step)
        xhat = norm[WIDE + first : WIDE + first + step, pl.ds(at, half)].astype(f32)
        sums = (own[rows, :] + other[rows, :]) / (2 * half)
        mean, cross = sums[:, :1], sums[:, LANES // 2 : LANES // 2 + 1]
        gradient = rstd[rows, :1] * (total[rows, :] - mean - xhat * cross)
        return (ct[rows, :].astype(f32) + gradient).astype(bf16)

    written(result, buffer, sem, part)


def output_rows(info, x, mine, got, result, buffer, sem):
    def part(first, step):
        rows = slice(first, first + step)
        return (x[rows, :].astype(f32) + mine[rows, :] + got[rows, :].astype(f32)).astype(bf16)

    written(result, buffer, sem, part)


def shards(inputs, lengths, cotangent, w_value, w_gate, kernel, w_out):
    x, ct = inputs[0], cotangent[0]
    count, channels = x.shape
    width = channels * lax.axis_size("tensor")
    core = lax.axis_index("tensor")
    peers = lax.axis_size("seq")
    every = every_bit()
    block = width >> len(every)
    taps = kernel.shape[0]
    info = jnp.stack(
        [lax.axis_index("seq") * count, lengths[0], jnp.int32(peers * count), core]
        + [(lax.axis_index(a) >> b) & 1 for a, b in every]
    ).astype(jnp.int32)

    up = [(i, i + 1) for i in range(peers - 1)]
    down = [(j, i) for i, j in up]
    x_other, ct_other = swap(x, "tensor"), swap(ct, "tensor")
    last, first, mark = run(
        pick,
        info,
        [x, ct],
        [((WIDE + NEAR, channels), bf16)] * 2,
        scratch=[pltpu.SemaphoreType.DMA((4,))],
        space=HBM,
    )
    before, after = lax.ppermute(last, "seq", up), lax.ppermute(first, "seq", down)
    ctv, wo, mark = run(
        prepare,
        info,
        [ct, w_out],
        [(ct.shape, bf16), (w_out.shape, bf16)],
        scratch=[pltpu.SemaphoreType.DMA((2,))],
        after=[mark],
        space=HBM,
    )
    halo, mark = run(
        pack, info, [before, after], [((2 * (WIDE + NEAR), channels), bf16)], after=[mark]
    )
    halo_other = swap(halo, "tensor")

    rows, ext = count + 2 * NEAR, count + 2 * WIDE
    full, pull, xv, wv, wg, mark = run(
        upstream,
        info,
        [ctv, ct_other, wo],
        [((count, width), bf16), ((count, channels), bf16)]
        + [(a.shape, bf16) for a in (x, w_value, w_gate)],
        scratch=[pltpu.SemaphoreType.DMA((3,))],
        after=[mark],
        far=[x, w_value, w_gate],
    )
    norm, rstd, hid, sig, slope, ends, _ = run(
        front,
        info,
        [xv, x_other, halo, halo_other, wv, wg, wo],
        [
            ((ext, width), bf16),
            ((count, LANES), f32),
            ((ext, channels), bf16),
            ((count, channels), bf16),
            ((count, channels), bf16),
            ((2 * NEAR, channels), f32),
        ],
        scratch=[pltpu.VMEM((2 * NEAR, width), bf16)],
        after=[mark],
    )
    row_sums = ((rows, LANES), f32)
    column = pltpu.VMEM((rows, LANES), f32)
    conv, stats, _ = run(
        depthwise,
        info,
        [hid, kernel],
        [((rows, channels), f32), row_sums],
        scratch=[pltpu.VMEM((ext + 16, LANES), f32), column, column],
    )
    stats_other = swap(stats, "tensor")
    swished, dswish, stats2, _ = run(
        swish,
        info,
        [conv, pull, ends, stats, stats_other],
        [((count, channels), bf16), ((rows, channels), f32), row_sums],
    )
    stats2_other = swap(stats2, "tensor")

    third = channels // 3
    *out_parts, mark = run(
        functools.partial(out_terms, rows=block),
        info,
        [full, swished],
        [((width // 2, third), bf16)] * 6,
        scratch=[pltpu.VMEM((width, channels), bf16)],
    )
    out_got = [send_bit(out_parts[2 * i + 1], i) for i in range(3)]

    def out_part(own, mark):
        return run(
            functools.partial(out_half, own=own),
            info,
            [swished, wo],
            [((count, channels), f32 if own else bf16)],
            after=[mark],
        )

    dconvs, dvgs, kept, got = [], [], [], []
    for i in range(3):
        dconv, dvg, product, mark = run(
            functools.partial(back, third=i),
            info,
            [dswish, conv, stats, stats_other, stats2, stats2_other, kernel, sig, slope, norm],
            [((rows, third), bf16), ((count, 2 * third), bf16), ((width, 2 * third), bf16)],
            scratch=[pltpu.VMEM((rows + 16, LANES), f32), pltpu.VMEM((3, rows, LANES), f32)],
            after=[mark],
        )
        if i == 0:
            out_theirs, mark = out_part(False, mark)
            out_other = swap(out_theirs, "tensor")
            out_mine, mark = out_part(True, mark)
        previous = (i + 2) % 3
        vkeep, okeep, send, mark = run(
            functools.partial(first_split, third=i, rows=block),
            info,
            [product, out_parts[2 * previous], out_got[previous]],
            [
                ((width // 2, 2 * third), bf16),
                ((width // 4, third), bf16),
                ((width // 2 + width // 8, 2 * third), bf16),
            ],
            after=[mark, *out_got],
        )
        dconvs.append(dconv)
        dvgs.append(dvg)
        kept.append((vkeep, okeep))
        got.append(send_bit(send, i))

    extra = (taps + 1) * 3 // 2

    def second(i, mark, *riding):
        vkeep, okeep, send, mark = run(
            functools.partial(second_split, third=i, rows=block),
            info,
            [*kept[i], got[i], *riding],
            [
                ((width // 4, 2 * third), bf16),
                ((width // 8, third), bf16),
                ((width // 4 + width // 16 + extra * len(riding), 2 * third), bf16),
            ],
            scratch=[pltpu.VMEM((width // 4, third), bf16)],
            after=[mark],
        )
        kept[i], got[i] = (vkeep, okeep), send_bit(send, (i + 1) % 3)
        return mark

    def third_step(i, mark, *riding):
        off, on = (riding, ()) if i == 1 else ((), riding)
        vkeep, okeep, send, *sums, mark = run(
            functools.partial(third_split, third=i, rows=block),
            info,
            [*kept[i], got[i], *riding],
            [
                ((width // 8, 2 * third), bf16),
                ((width // 8, third), bf16),
                ((width // 8 + extra * len(on), 2 * third), bf16),
            ]
            + [(r.shape, f32) for r in off],
            scratch=[pltpu.VMEM((width // 8, third), bf16)],
            after=[mark],
        )
        kept[i], got[i] = (vkeep, okeep), send_bit(send, (i + 2) % 3)
        return *sums, mark

    def last_step(i, mark, *riding):
        behind = (taps + 1) * len(riding)
        keep, send, mark = run(
            functools.partial(last_split, rows=block),
            info,
            [*kept[i], got[i], *riding],
            [((width // 16 + behind, 3 * third), bf16)] * 2,
            scratch=[pltpu.VMEM(r.shape, f32) for r in riding],
            after=[mark],
        )
        return *finish(keep, send, block, behind), mark

    def norm_part(own, mark):
        return run(
            functools.partial(norm_half, own=own),
            info,
            [*dvgs, wv, wg],
            [((count // 2, channels), f32 if own else bf16)] * 2,
            after=[mark],
        )

    def taps_part(i, mark):
        return run(
            functools.partial(taps_sums, third=i),
            info,
            [dconvs[i], hid],
            [((taps + 1, third), f32)],
            scratch=[pltpu.VMEM((rows + 16, LANES), f32), pltpu.VMEM((taps, 8, LANES), f32)],
            after=[mark],
        )

    def final(kernel, args, mark):
        return run(
            kernel,
            info,
            args,
            [((count, channels), bf16)],
            scratch=[pltpu.VMEM((count, channels), bf16), pltpu.SemaphoreType.DMA((4,))],
            after=[mark],
            to=HBM,
        )

    parts = []
    for i in range(3):
        part, mark = taps_part(i, mark)
        parts.append(part)
    taps_own = jnp.concatenate(parts, axis=1)
    *mine, mark = norm_part(True, mark)
    mark = second(0, mark)
    taps_sum, mark = run(
        add_taps, info, [taps_own, send_bit(taps_own, 0)], [(taps_own.shape, f32)], after=[mark]
    )
    *theirs, mark = norm_part(False, mark)
    theirs = [swap(t, "tensor") for t in theirs]
    mark = second(1, mark, taps_sum)
    dnorm, stats3, mark = run(
        norm_sums,
        info,
        [*mine, *theirs, norm],
        [((count, channels), f32), ((count, LANES), f32)],
        after=[mark],
    )
    stats3_other = swap(stats3, "tensor")
    mark = second(2, mark)
    output, mark = final(output_rows, [x, out_mine, out_other], mark)
    input_gradient, mark = final(
        input_rows, [ct, dnorm, norm, rstd, stats3, stats3_other], mark
    )
    (mark,) = third_step(0, mark)
    taps_sum, mark = third_step(1, mark, taps_sum)
    (mark,) = third_step(2, mark, taps_sum)
    total0, _, mark = last_step(0, mark)
    total1, _, mark = last_step(1, mark)
    total2, kernel_grad, mark = last_step(2, mark, taps_sum)
    totals = [total0, total1, total2]
    for bit in range(4, len(every)):
        kernel_grad = kernel_grad + send_bit(kernel_grad, bit)
    kernel_grad = kernel_grad[:taps]
    value_grad, gate_grad = (
        jnp.concatenate([t[:, j * third : (j + 1) * third] for t in totals], axis=1)
        for j in (0, 1)
    )
    out_grad = jnp.concatenate([totals[(i + 1) % 3][:, 2 * third :] for i in range(3)], axis=1).T
    return (
        output[None],
        input_gradient[None],
        value_grad,
        gate_grad,
        kernel_grad,
        out_grad,
    )


def solution(mesh):
    return jax.shard_map(
        shards,
        mesh=mesh,
        in_specs=(
            P("dp", "seq", "tensor"),
            P("dp"),
            P("dp", "seq", "tensor"),
            P(None, "tensor"),
            P(None, "tensor"),
            P(None, "tensor"),
            P("tensor", None),
        ),
        out_specs=(
            P("dp", "seq", "tensor"),
            P("dp", "seq", "tensor"),
            P(("seq", "dp"), "tensor"),
            P(("seq", "dp"), "tensor"),
            P(None, "tensor"),
            P("tensor", ("seq", "dp")),
        ),
        check_vma=False,
    )
```

```python
import functools

import jax
import jax.numpy as jnp
from jax import lax
from jax.experimental import pallas as pl
from jax.experimental.pallas import tpu as pltpu
from jax.sharding import PartitionSpec as P

epsilon = 1e-05
f32, bf16 = jnp.float32, jnp.bfloat16
LANES = 128
WIDE, NEAR = 32, 16
NN = (((1,), (0,)), ((), ()))
NT = (((1,), (1,)), ((), ()))
TN = (((0,), (0,)), ((), ()))
VMEM = pl.BlockSpec(memory_space=pltpu.VMEM)
SMEM = pl.BlockSpec(memory_space=pltpu.SMEM)
ANY = pl.BlockSpec(memory_space=pl.ANY)
HBM = pl.BlockSpec(memory_space=pltpu.HBM)


def dot(a, b, dims=NN):
    return lax.dot_general(a, b, dims, preferred_element_type=f32)


def run(kernel, info, args, outs, scratch=(), after=(), limit=8, space=VMEM, to=VMEM, far=()):
    near = len(args)

    def body(*refs):
        lead = 1 + near + len(far)
        rest = refs[lead + len(after) :]
        kernel(*refs[:lead], *rest[: len(outs)], *rest[len(outs) + 1 :])
        rest[len(outs)][...] = jnp.zeros((8, LANES), f32)

    args = [pltpu.with_memory_space_constraint(a, space.memory_space) for a in args]
    args += [pltpu.with_memory_space_constraint(a, pltpu.HBM) for a in far]
    *results, mark = pl.pallas_call(
        body,
        in_specs=[SMEM] + [space] * near + [HBM] * len(far) + [ANY] * len(after),
        out_specs=[to] * len(outs) + [VMEM],
        out_shape=[to.memory_space(shape, dtype) for shape, dtype in outs]
        + [pltpu.VMEM((8, LANES), f32)],
        scratch_shapes=list(scratch),
        compiler_params=pltpu.CompilerParams(vmem_limit_bytes=limit << 20),
        cost_estimate=pl.CostEstimate(flops=COST, bytes_accessed=COST, transcendentals=0),
        name=kernel.__name__ if hasattr(kernel, "__name__") else kernel.func.__name__,
    )(info, *args, *after)
    return *results, mark


COST = 1 << 10


def swap(value, axis, bit=0):
    size = lax.axis_size(axis)
    return lax.ppermute(value, axis, [(i, i ^ (1 << bit)) for i in range(size)])


def bits_of(axis):
    return [(axis, b) for b in range(lax.axis_size(axis).bit_length() - 1)]


def every_bit():
    return bits_of("dp") + bits_of("seq")


def split_rows(info, bit, place, total, rows, keep, send, load):
    run_length = rows << place
    for j in range(total // (2 * run_length)):
        for put, side in ((keep, info[4 + bit]), (send, 1 - info[4 + bit])):
            if run_length % 32:
                low, high = (
                    load(slice((2 * j + i) * run_length, (2 * j + i + 1) * run_length))
                    for i in (0, 1)
                )
                value = jnp.where(side == 0, low, high)
            else:
                at = pl.multiple_of((2 * j + side) * run_length, run_length)
                value = load(pl.ds(at, run_length))
            put(j * run_length, value)


def put_into(target):
    def put(at, value):
        target[at : at + value.shape[0], :] = value

    return put


def put_folded(target, first, half):
    columns = target.shape[1] // 2

    def put(at, value):
        length = value.shape[0]
        for low in range(0, length, min(length, half)):
            part = value[low : low + min(length, half)]
            side, row = divmod(at + low, half)
            to = slice(first + row, first + row + part.shape[0])
            target[to, side * columns : (side + 1) * columns] = part

    return put


def add(a, b):
    return (a.astype(f32) + b.astype(f32)).astype(bf16)


def first_split(info, product, okept, ogot, vkeep, okeep, send, *, third, rows):
    total = product.shape[0]
    split_rows(info, third, third, total, rows, put_into(vkeep), put_into(send), lambda at: product[at, :])
    before = (third + 2) % 3
    place = third - (before < third)
    fold = put_folded(send, total // 2, total // 8)
    load = lambda at: add(okept[at, :], ogot[at, :])
    split_rows(info, third, place, total // 2, rows, put_into(okeep), fold, load)


def unfold(got, first, rows, target):
    half = rows // 2
    columns = target.shape[1]
    target[:half, :] = got[first : first + half, :columns]
    target[half:, :] = got[first : first + half, columns:]


def ride(taps, send):
    rows, columns = taps.shape[0], send.shape[1]
    value = taps[...].astype(bf16)
    first = send.shape[0] - rows - rows // 2
    send[first : first + rows, :] = value[:, :columns]
    send[first + rows :, : columns // 2] = value[: rows // 2, columns:]
    send[first + rows :, columns // 2 :] = value[rows // 2 :, columns:]


def alight(taps, got, result):
    rows, columns = taps.shape[0], got.shape[1]
    first = got.shape[0] - rows - rows // 2
    value = taps[...].astype(bf16).astype(f32)
    half = rows // 2
    result[:, :columns] = value[:, :columns] + got[first : first + rows, :].astype(f32)
    result[:half, columns:] = value[:half, columns:] + got[
        first + rows :, : columns // 2
    ].astype(f32)
    result[half:, columns:] = value[half:, columns:] + got[
        first + rows :, columns // 2 :
    ].astype(f32)


def second_split(info, vkept, okept, got, *refs, third, rows):
    *taps, vkeep, okeep, send, flat = refs
    if taps:
        ride(taps[0], send)
    total = vkept.shape[0]
    bit = (third + 1) % 3
    left = [b for b in range(3) if b != third]
    load = lambda at: add(vkept[at, :], got[at, :])
    split_rows(info, bit, left.index(bit), total, rows, put_into(vkeep), put_into(send), load)
    unfold(got, total, total // 2, flat)
    fold = put_folded(send, total // 2, total // 8)
    load = lambda at: add(okept[at, :], flat[at, :])
    split_rows(info, bit, 0, total // 2, rows, put_into(okeep), fold, load)


def third_split(info, vkept, okept, got, *refs, third, rows):
    if third == 1:
        taps, vkeep, okeep, send, sums, flat = refs
        alight(taps, got, sums)
    elif third == 2:
        sums, vkeep, okeep, send, flat = refs
        ride(sums, send)
    else:
        vkeep, okeep, send, flat = refs
    total = vkept.shape[0]
    bit, place = ((third + 2) % 3, 0) if third else (3, 1)
    load = lambda at: add(vkept[at, :], got[at, :])
    split_rows(info, bit, place, total, rows, put_into(vkeep), put_into(send), load)
    unfold(got, total, total // 2, flat)
    if third:
        okeep[...] = add(okept[...], flat[...])
    else:
        fold = put_folded(send, total // 2, total // 8)
        load = lambda at: add(okept[at, :], flat[at, :])
        split_rows(info, bit, 0, total // 2, rows, put_into(okeep), fold, load)


def first_last_split(info, vkept, okept, got, keep, send, osum, flat, *, rows):
    total = vkept.shape[0]
    load = lambda at: add(vkept[at, :], got[at, :])
    split_rows(info, 2, 0, total, rows, put_into(keep), put_into(send), load)
    unfold(got, total, total // 2, flat)
    osum[...] = okept[...].astype(f32) + flat[...].astype(f32)


def last_split(info, vkept, okept, got, *refs, rows):
    keep, send = refs[len(refs) // 4 :][:2]
    total, columns = vkept.shape
    if len(refs) > 2:
        alight(refs[0], got, refs[3])
        keep[total // 2 :, :] = refs[3][...].astype(bf16)
        send[total // 2 :, :] = refs[3][...].astype(bf16)

    def put(target):
        def to(at, value):
            target[at : at + value.shape[0], : value.shape[1]] = value

        return to

    load = lambda at: add(vkept[at, :], got[at, :])
    split_rows(info, 3, 0, total, rows, put(keep), put(send), load)

    def side(target):
        def to(at, value):
            target[at : at + value.shape[0], columns:] = value

        return to

    split_rows(info, 3, 0, total, rows, side(keep), side(send), lambda at: okept[at, :])


def send_bit(value, bit):
    return swap(value, *every_bit()[bit])


def finish(value, rows):
    for bit in range(4, len(every_bit())):
        axis, place = every_bit()[bit]
        value = value.astype(bf16).reshape(-1, 2, rows, value.shape[1])
        mine = (lax.axis_index(axis) >> place) & 1
        keep, send = (
            lax.dynamic_index_in_dim(value, side, 1, keepdims=False) for side in (mine, 1 - mine)
        )
        shape = (-1, value.shape[-1])
        value = keep.reshape(shape).astype(f32) + send_bit(send.reshape(shape), bit).astype(f32)
    return value


def sigmoid(v):
    return 0.5 + 0.5 * jnp.tanh(0.5 * v)


def row_mask(info, first, rows, limit):
    place = info[0] + first + lax.broadcasted_iota(jnp.int32, (rows, 1), 0)
    return ((place >= 0) & (place < limit)).astype(f32)


def halves_at(info, half):
    return (
        pl.multiple_of(info[3] * half, half),
        pl.multiple_of((1 - info[3]) * half, half),
    )


def start_all(pairs, sem):
    copies = [pltpu.make_async_copy(a, b, sem.at[i]) for i, (a, b) in enumerate(pairs)]
    for c in copies:
        c.start()
    return copies


def prepare(info, ct, w_out, ct_to, w_to, sem):
    for c in start_all([(w_out, w_to), (ct, ct_to)], sem):
        c.wait()


def pick(info, x, ct, last, first, sem):
    count = x.shape[0]
    copies = [
        pltpu.make_async_copy(source.at[a : a + n], target.at[b : b + n], sem.at[i])
        for i, (source, target, a, b, n) in enumerate(
            (
                (x, last, count - WIDE, 0, WIDE),
                (ct, last, count - NEAR, WIDE, NEAR),
                (x, first, 0, 0, WIDE),
                (ct, first, 0, WIDE, NEAR),
            )
        )
    ]
    for c in copies:
        c.start()
    for c in copies:
        c.wait()


def pack(info, before, after, halo):
    rows = before.shape[0]
    halo[:rows, :] = before[...]
    halo[rows:, :] = after[...]


def upstream(info, own, other, w_out, x, wv, wg, full, pull, x_to, wv_to, wg_to, sem):
    count, half = own.shape
    copies = start_all([(x, x_to), (wv, wv_to), (wg, wg_to)], sem)
    mine, theirs = halves_at(info, half)
    full[:, pl.ds(mine, half)] = own[...]
    full[:, pl.ds(theirs, half)] = other[...]
    step = count // 2
    for c in range(0, count, step):
        pull[c : c + step, :] = dot(full[c : c + step, :], w_out[...], NT).astype(bf16)
    for c in copies:
        c.wait()


def front(info, own, other, halo_own, halo_other, wv, wg, w_out, norm, rstd, hid, sig, slope, ends, edge):
    count, half = own.shape
    channels = wv.shape[1]
    mine, theirs = halves_at(info, half)

    def normalize(to, a, b):
        a, b = a.astype(f32), b.astype(f32)
        width = 2 * half
        mean = (jnp.sum(a, 1, keepdims=True) + jnp.sum(b, 1, keepdims=True)) / width
        a, b = a - mean, b - mean
        var = jnp.sum(a * a, 1, keepdims=True) + jnp.sum(b * b, 1, keepdims=True)
        inverse = lax.rsqrt(var / width + epsilon)
        norm[to, pl.ds(mine, half)] = (a * inverse).astype(bf16)
        norm[to, pl.ds(theirs, half)] = (b * inverse).astype(bf16)
        return inverse

    chunk = 128

    def body(i, _):
        at = pl.multiple_of(i * chunk, chunk)
        inverse = normalize(
            pl.ds(pl.multiple_of(WIDE + at, WIDE), chunk),
            own[pl.ds(at, chunk), :],
            other[pl.ds(at, chunk), :],
        )
        rstd[pl.ds(at, chunk), :] = jnp.broadcast_to(inverse, (chunk, LANES))
        return 0

    lax.fori_loop(0, count // chunk, body, 0, unroll=2)
    for to, at in ((0, 0), (WIDE + count, WIDE + NEAR)):
        normalize(pl.ds(to, WIDE), halo_own[at : at + WIDE, :], halo_other[at : at + WIDE, :])
    for a, at in ((halo_own, mine), (halo_other, theirs)):
        edge[:NEAR, pl.ds(at, half)] = a[WIDE : WIDE + NEAR, :]
        edge[NEAR:, pl.ds(at, half)] = a[2 * WIDE + NEAR :, :]
    ends[...] = dot(edge[...], w_out[...], NT)

    tile = channels // 3
    rows = count + 2 * WIDE
    step = rows // 2
    for n in range(0, channels, tile):
        cols = slice(n, n + tile)
        for c in range(0, rows, step):
            value = dot(norm[c : c + step, :], wv[:, cols])
            s = sigmoid(dot(norm[c : c + step, :], wg[:, cols]))
            keep = row_mask(info, c - WIDE, step, info[1])
            vs = value * s * keep
            hid[c : c + step, cols] = vs.astype(bf16)
            low, high = max(c, WIDE), min(c + step, WIDE + count)
            part = slice(low - c, high - c)
            sig[low - WIDE : high - WIDE, cols] = (s * keep)[part].astype(bf16)
            slope[low - WIDE : high - WIDE, cols] = (vs * (1.0 - s))[part].astype(bf16)


def tap_sums(source, base, groups, taps):
    sums = [None] * groups
    for residue in range(8):
        mine = list(range(residue, len(taps), 8))
        shifted = [
            source[pl.ds(base + 8 * i + residue, 8), :] for i in range(groups + len(mine) - 1)
        ]
        for i, k in enumerate(mine):
            for g in range(groups):
                term = shifted[g + i] * taps[k]
                sums[g] = term if sums[g] is None else sums[g] + term
    return sums


def tap_rows(taps, cols, reverse=False):
    values = taps[:, cols].astype(f32)
    order = range(taps.shape[0])
    return [
        jnp.broadcast_to(values[k : k + 1, :], (8, LANES))
        for k in (reversed(order) if reverse else order)
    ]


def lane_tile(n):
    return pl.ds(pl.multiple_of(n * LANES, LANES), LANES)


def paired(first, second):
    lane = lax.broadcasted_iota(jnp.int32, (first.shape[0], LANES), 1)
    return jnp.where(
        lane < LANES // 2,
        jnp.sum(first, axis=1, keepdims=True),
        jnp.sum(second, axis=1, keepdims=True),
    )


def depthwise(info, hid, taps, conv, stats, scratch, total, square):
    rows = conv.shape[0]
    skip = WIDE - NEAR - (taps.shape[0] - 1) // 2
    groups = 20
    total[...] = jnp.zeros_like(total)
    square[...] = jnp.zeros_like(square)

    def tile(n, _):
        cols = lane_tile(n)
        scratch[: hid.shape[0], :] = hid[:, cols].astype(f32)
        weights = tap_rows(taps, cols)

        def body(i, _):
            base = pl.multiple_of(i * 8 * groups, 8)
            for g, value in enumerate(tap_sums(scratch, base + skip, groups, weights)):
                at = pl.ds(base + 8 * g, 8)
                conv[at, cols] = value
                total[at, :] += value
                square[at, :] += value * value
            return 0

        lax.fori_loop(0, rows // (8 * groups), body, 0)
        return 0

    lax.fori_loop(0, conv.shape[1] // LANES, tile, 0)
    stats[...] = paired(total[...], square[...])


def moments(first, second, width):
    mean = (first[:, :1] + second[:, :1]) / width
    half = LANES // 2
    square = (first[:, half : half + 1] + second[:, half : half + 1]) / width
    return mean, lax.rsqrt(square - mean * mean + epsilon)


def swish(info, conv, pull, ends, own, other, swished, dswish, stats):
    count, channels = pull.shape

    def part(at, g, rows):
        to = pl.ds(at, rows)
        mean, inverse = moments(own[to, :], other[to, :], 2 * channels)
        zhat = (conv[to, :] - mean) * inverse
        s = sigmoid(zhat)
        zs = zhat * s
        d = g * (s + zs * (1.0 - s))
        dswish[to, :] = d
        stats[to, :] = paired(d, d * zhat)
        return zs.astype(bf16)

    part(0, ends[:NEAR, :], NEAR)
    part(NEAR + count, ends[NEAR:, :], NEAR)
    step = 64

    def body(i, _):
        at = pl.multiple_of(i * step, step)
        rows = pl.ds(at, step)
        g = pull[rows, :].astype(f32)
        swished[rows, :] = part(pl.multiple_of(at + NEAR, NEAR), g, step)
        return 0

    lax.fori_loop(0, count // step, body, 0, unroll=2)


def out_terms(info, full, swished, *refs, rows):
    halves, product = refs[:-1], refs[-1]
    width = full.shape[1]
    cols = swished.shape[1] // 3
    step = width // 4
    for c in range(0, width, step):
        product[c : c + step, :] = dot(full[:, c : c + step], swished[...], TN).astype(bf16)
    for i in range(3):
        load = lambda at: product[at, i * cols : (i + 1) * cols]
        keep, send = (put_into(half) for half in halves[2 * i : 2 * i + 2])
        split_rows(info, i, i, width, rows, keep, send, load)


def slopes(info, own, other, own2, other2, coef, width):
    rows = own.shape[0]
    mean, inverse = moments(own[...], other[...], width)
    half = LANES // 2
    shift = (own2[:, :1] + other2[:, :1]) / width
    cross = (own2[:, half : half + 1] + other2[:, half : half + 1]) / width
    inverse = inverse * row_mask(info, -NEAR, rows, info[2])
    tilt = inverse * inverse * cross
    coef[0] = jnp.broadcast_to(inverse, (rows, LANES))
    coef[1] = jnp.broadcast_to(tilt, (rows, LANES))
    coef[2] = jnp.broadcast_to(tilt * mean - inverse * shift, (rows, LANES))


def back(info, dswish, conv, taps, sig, slope, norm, *refs, third):
    rows, channels = dswish.shape
    count = sig.shape[0]
    width = 2 * channels
    if third == 0:
        *sums, dconv, dvg, product, coef, scratch = refs
        slopes(info, *sums, coef, width)
    else:
        coef, dconv, dvg, product, scratch = refs
    tiles = channels // LANES // 3
    groups = 16
    skip = NEAR - (taps.shape[0] - 1) // 2

    def tile(n, _):
        local = lane_tile(n)
        cols = lane_tile(third * tiles + n)
        d = (coef[0] * dswish[:, cols] - coef[1] * conv[:, cols] + coef[2]).astype(bf16)
        dconv[:, local] = d
        scratch[:rows, :] = d.astype(f32)
        weights = tap_rows(taps, cols, reverse=True)

        def body(i, _):
            base = pl.multiple_of(i * 8 * groups, 16)
            sums = tap_sums(scratch, base + skip, groups, weights)
            for g in range(0, groups, 2):
                at = pl.ds(base + 8 * g, 16)
                dh = jnp.concatenate(sums[g : g + 2], axis=0)
                dvg[at, local] = (dh * sig[at, cols]).astype(bf16)
                dvg[at, lane_tile(tiles + n)] = (dh * slope[at, cols]).astype(bf16)
            return 0

        lax.fori_loop(0, count // (8 * groups), body, 0)
        return 0

    lax.fori_loop(0, tiles, tile, 0)
    step = width // 4
    for c in range(0, width, step):
        r = dot(norm[WIDE : WIDE + count, c : c + step], dvg[...], TN)
        product[c : c + step, :] = r.astype(bf16)


def taps_sums(info, dconv, hid, out, scratch, total, *, third):
    rows, channels = dconv.shape
    count = rows - 2 * NEAR
    taps = total.shape[0]
    half = (taps - 1) // 2
    groups = 16
    tiles = channels // LANES

    def tile(n, _):
        local = lane_tile(n)
        cols = lane_tile(third * tiles + n)
        scratch[:rows, :] = dconv[:, local].astype(f32)
        total[...] = jnp.zeros_like(total)

        def body(i, _):
            base = pl.multiple_of(i * 8 * groups, 16)
            h = []
            for g in range(0, groups, 2):
                both = hid[pl.ds(pl.multiple_of(WIDE + base + 8 * g, 16), 16), cols].astype(f32)
                h += [both[:8], both[8:]]
            for residue in range(8):
                mine = list(range(residue, taps, 8))
                shifted = [
                    scratch[pl.ds(base + NEAR - half + 8 * g + residue, 8), :]
                    for g in range(groups + len(mine) - 1)
                ]
                for j, m in enumerate(mine):
                    term = shifted[j] * h[0]
                    for g in range(1, groups):
                        term = term + shifted[g + j] * h[g]
                    total[taps - 1 - m] += term
            return 0

        lax.fori_loop(0, count // (8 * groups), body, 0)
        out[:taps, local] = jnp.sum(total[...], axis=1)
        out[taps:, local] = jnp.zeros((out.shape[0] - taps, LANES), f32)
        return 0

    lax.fori_loop(0, tiles, tile, 0)


def add_taps(info, value, got, result):
    result[...] = value[...] + got[...]


def out_half(info, swished, w_out, result, *, own):
    half = result.shape[1]
    at = halves_at(info, half)[0 if own else 1]
    step = swished.shape[0] // 2
    for r in range(0, swished.shape[0], step):
        part = dot(swished[r : r + step, :], w_out[:, pl.ds(at, half)])
        result[r : r + step, :] = part.astype(result.dtype)


def norm_half(info, a, b, c, wv, wg, *results, own):
    half = results[0].shape[1]
    at = halves_at(info, half)[0 if own else 1]
    third = half // 3
    step = a.shape[0] // 2
    for n, result in enumerate(results):
        r = n * step
        total = None
        for i, dvg in enumerate((a, b, c)):
            cols = slice(i * third, (i + 1) * third)
            for j, w in enumerate((wv, wg)):
                part = dot(
                    dvg[r : r + step, j * third : (j + 1) * third], w[pl.ds(at, half), cols], NT
                )
                total = part if total is None else total + part
        result[...] = total.astype(result.dtype)


def norm_sums(info, mine0, mine1, got0, got1, norm, total, stats):
    count, half = total.shape
    at = halves_at(info, half)[0]
    step = 32
    for n, (mine, got) in enumerate(((mine0, got0), (mine1, got1))):
        start = n * count // 2

        def body(i, _):
            here = pl.multiple_of(i * step, step)
            rows, to = pl.ds(here, step), pl.ds(start + here, step)
            xhat = norm[pl.ds(WIDE + start + here, step), pl.ds(at, half)]
            d = mine[rows, :] + got[rows, :].astype(f32)
            total[to, :] = d
            stats[to, :] = paired(d, d * xhat.astype(f32))
            return 0

        lax.fori_loop(0, count // 2 // step, body, 0, unroll=2)


def written(result, buffer, sem, part):
    count, step = buffer.shape[0], buffer.shape[0] // sem.shape[0]
    copies = []
    for i in range(sem.shape[0]):
        rows = slice(i * step, (i + 1) * step)
        buffer[rows, :] = part(i * step, step)
        copies.append(pltpu.make_async_copy(buffer.at[rows], result.at[rows], sem.at[i]))
        copies[-1].start()
    for c in copies:
        c.wait()


def input_rows(info, ct, total, norm, rstd, own, other, result, buffer, sem):
    count, half = total.shape
    at = halves_at(info, half)[0]

    def part(first, step):
        rows = slice(first, first + step)
        xhat = norm[WIDE + first : WIDE + first + step, pl.ds(at, half)].astype(f32)
        sums = (own[rows, :] + other[rows, :]) / (2 * half)
        mean, cross = sums[:, :1], sums[:, LANES // 2 : LANES // 2 + 1]
        gradient = rstd[rows, :1] * (total[rows, :] - mean - xhat * cross)
        return (ct[rows, :].astype(f32) + gradient).astype(bf16)

    written(result, buffer, sem, part)


def output_rows(info, x, mine, got, result, buffer, sem):
    def part(first, step):
        rows = slice(first, first + step)
        return (x[rows, :].astype(f32) + mine[rows, :] + got[rows, :].astype(f32)).astype(bf16)

    written(result, buffer, sem, part)


def shards(inputs, lengths, cotangent, w_value, w_gate, kernel, w_out):
    x, ct = inputs[0], cotangent[0]
    count, channels = x.shape
    width = channels * lax.axis_size("tensor")
    core = lax.axis_index("tensor")
    peers = lax.axis_size("seq")
    every = every_bit()
    block = width >> len(every)
    taps = kernel.shape[0]
    info = jnp.stack(
        [lax.axis_index("seq") * count, lengths[0], jnp.int32(peers * count), core]
        + [(lax.axis_index(a) >> b) & 1 for a, b in every]
    ).astype(jnp.int32)

    up = [(i, i + 1) for i in range(peers - 1)]
    down = [(j, i) for i, j in up]
    x_other, ct_other = swap(x, "tensor"), swap(ct, "tensor")
    last, first, mark = run(
        pick,
        info,
        [x, ct],
        [((WIDE + NEAR, channels), bf16)] * 2,
        scratch=[pltpu.SemaphoreType.DMA((4,))],
        space=HBM,
    )
    before, after = lax.ppermute(last, "seq", up), lax.ppermute(first, "seq", down)
    ctv, wo, mark = run(
        prepare,
        info,
        [ct, w_out],
        [(ct.shape, bf16), (w_out.shape, bf16)],
        scratch=[pltpu.SemaphoreType.DMA((2,))],
        after=[mark],
        space=HBM,
    )
    halo, mark = run(
        pack, info, [before, after], [((2 * (WIDE + NEAR), channels), bf16)], after=[mark]
    )
    halo_other = swap(halo, "tensor")

    rows, ext = count + 2 * NEAR, count + 2 * WIDE
    full, pull, xv, wv, wg, mark = run(
        upstream,
        info,
        [ctv, ct_other, wo],
        [((count, width), bf16), ((count, channels), bf16)]
        + [(a.shape, bf16) for a in (x, w_value, w_gate)],
        scratch=[pltpu.SemaphoreType.DMA((3,))],
        after=[mark],
        far=[x, w_value, w_gate],
    )
    norm, rstd, hid, sig, slope, ends, _ = run(
        front,
        info,
        [xv, x_other, halo, halo_other, wv, wg, wo],
        [
            ((ext, width), bf16),
            ((count, LANES), f32),
            ((ext, channels), bf16),
            ((count, channels), bf16),
            ((count, channels), bf16),
            ((2 * NEAR, channels), f32),
        ],
        scratch=[pltpu.VMEM((2 * NEAR, width), bf16)],
        after=[mark],
    )
    row_sums = ((rows, LANES), f32)
    column = pltpu.VMEM((rows, LANES), f32)
    conv, stats, _ = run(
        depthwise,
        info,
        [hid, kernel],
        [((rows, channels), f32), row_sums],
        scratch=[pltpu.VMEM((ext + 16, LANES), f32), column, column],
    )
    stats_other = swap(stats, "tensor")
    swished, dswish, stats2, _ = run(
        swish,
        info,
        [conv, pull, ends, stats, stats_other],
        [((count, channels), bf16), ((rows, channels), f32), row_sums],
    )
    stats2_other = swap(stats2, "tensor")

    third = channels // 3
    *out_parts, mark = run(
        functools.partial(out_terms, rows=block),
        info,
        [full, swished],
        [((width // 2, third), bf16)] * 6,
        scratch=[pltpu.VMEM((width, channels), bf16)],
    )
    out_got = [send_bit(out_parts[2 * i + 1], i) for i in range(3)]

    def out_part(own, mark):
        return run(
            functools.partial(out_half, own=own),
            info,
            [swished, wo],
            [((count, channels), f32 if own else bf16)],
            after=[mark],
        )

    dconvs, dvgs, kept, got = [], [], [], []
    sums = [stats, stats_other, stats2, stats2_other]
    for i in range(3):
        dconv, dvg, product, *coef, mark = run(
            functools.partial(back, third=i),
            info,
            [dswish, conv, kernel, sig, slope, norm, *sums],
            [((rows, third), bf16), ((count, 2 * third), bf16), ((width, 2 * third), bf16)]
            + [((3, rows, LANES), f32)] * (i == 0),
            scratch=[pltpu.VMEM((rows + 16, LANES), f32)],
            after=[mark],
        )
        if i == 0:
            sums = coef
        if i == 0:
            out_theirs, mark = out_part(False, mark)
            out_other = swap(out_theirs, "tensor")
            out_mine, mark = out_part(True, mark)
        previous = (i + 2) % 3
        vkeep, okeep, send, mark = run(
            functools.partial(first_split, third=i, rows=block),
            info,
            [product, out_parts[2 * previous], out_got[previous]],
            [
                ((width // 2, 2 * third), bf16),
                ((width // 4, third), bf16),
                ((width // 2 + width // 8, 2 * third), bf16),
            ],
            after=[mark, *out_got],
        )
        dconvs.append(dconv)
        dvgs.append(dvg)
        kept.append((vkeep, okeep))
        got.append(send_bit(send, i))

    extra = (taps + 1) * 3 // 2

    def second(i, mark, *riding):
        vkeep, okeep, send, mark = run(
            functools.partial(second_split, third=i, rows=block),
            info,
            [*kept[i], got[i], *riding],
            [
                ((width // 4, 2 * third), bf16),
                ((width // 8, third), bf16),
                ((width // 4 + width // 16 + extra * len(riding), 2 * third), bf16),
            ],
            scratch=[pltpu.VMEM((width // 4, third), bf16)],
            after=[mark],
        )
        kept[i], got[i] = (vkeep, okeep), send_bit(send, (i + 1) % 3)
        return mark

    def third_step(i, mark, *riding):
        off, on = (riding, ()) if i == 1 else ((), riding)
        vkeep, okeep, send, *sums, mark = run(
            functools.partial(third_split, third=i, rows=block),
            info,
            [*kept[i], got[i], *riding],
            [
                ((width // 8, 2 * third), bf16),
                ((width // 8 if i else width // 16, third), bf16),
                ((width // 8 + (extra * len(on) if i else width // 32), 2 * third), bf16),
            ]
            + [(r.shape, f32) for r in off],
            scratch=[pltpu.VMEM((width // 8, third), bf16)],
            after=[mark],
        )
        kept[i], got[i] = (vkeep, okeep), send_bit(send, (i + 2) % 3 if i else 3)
        return *sums, mark

    def last_step(i, mark, *riding):
        behind = (taps + 1) * len(riding)
        if i == 0:
            keep, send, osum, mark = run(
                functools.partial(first_last_split, rows=block),
                info,
                [*kept[0], got[0]],
                [((width // 16, 2 * third), bf16)] * 2 + [((width // 16, third), f32)],
                scratch=[pltpu.VMEM((width // 16, third), bf16)],
                after=[mark],
            )
            return keep.astype(f32) + send_bit(send, 2).astype(f32), osum, mark
        keep, send, mark = run(
            functools.partial(last_split, rows=block),
            info,
            [*kept[i], got[i], *riding],
            [((width // 16 + behind, 3 * third), bf16)] * 2,
            scratch=[pltpu.VMEM(r.shape, f32) for r in riding],
            after=[mark],
        )
        value = keep.astype(f32) + send_bit(send, 3).astype(f32)
        return value[: width // 16], value[width // 16 :], mark

    def norm_part(own, mark):
        return run(
            functools.partial(norm_half, own=own),
            info,
            [*dvgs, wv, wg],
            [((count // 2, channels), f32 if own else bf16)] * 2,
            after=[mark],
        )

    def taps_part(i, mark):
        return run(
            functools.partial(taps_sums, third=i),
            info,
            [dconvs[i], hid],
            [((taps + 1, third), f32)],
            scratch=[pltpu.VMEM((rows + 16, LANES), f32), pltpu.VMEM((taps, 8, LANES), f32)],
            after=[mark],
        )

    def final(kernel, args, mark):
        return run(
            kernel,
            info,
            args,
            [((count, channels), bf16)],
            scratch=[pltpu.VMEM((count, channels), bf16), pltpu.SemaphoreType.DMA((4,))],
            after=[mark],
            to=HBM,
        )

    parts = []
    for i in range(3):
        part, mark = taps_part(i, mark)
        parts.append(part)
    taps_own = jnp.concatenate(parts, axis=1)
    *mine, mark = norm_part(True, mark)
    mark = second(0, mark)
    taps_sum, mark = run(
        add_taps, info, [taps_own, send_bit(taps_own, 0)], [(taps_own.shape, f32)], after=[mark]
    )
    *theirs, mark = norm_part(False, mark)
    theirs = [swap(t, "tensor") for t in theirs]
    mark = second(1, mark, taps_sum)
    dnorm, stats3, mark = run(
        norm_sums,
        info,
        [*mine, *theirs, norm],
        [((count, channels), f32), ((count, LANES), f32)],
        after=[mark],
    )
    stats3_other = swap(stats3, "tensor")
    mark = second(2, mark)
    output, mark = final(output_rows, [x, out_mine, out_other], mark)
    input_gradient, mark = final(
        input_rows, [ct, dnorm, norm, rstd, stats3, stats3_other], mark
    )
    (mark,) = third_step(0, mark)
    taps_sum, mark = third_step(1, mark, taps_sum)
    (mark,) = third_step(2, mark, taps_sum)
    total0, out2, mark = last_step(0, mark)
    total1, _, mark = last_step(1, mark)
    total2, kernel_grad, mark = last_step(2, mark, taps_sum)
    totals = [finish(t, block) for t in (total0, total1, total2)]
    value_grad, gate_grad = (
        jnp.concatenate([t[:, j * third : (j + 1) * third] for t in totals], axis=1)
        for j in (0, 1)
    )
    out_grad = jnp.concatenate(
        [totals[1][:, 2 * third :], totals[2][:, 2 * third :], finish(out2, block)], axis=1
    ).T
    for bit in range(4, len(every)):
        kernel_grad = kernel_grad + send_bit(kernel_grad, bit)
    kernel_grad = kernel_grad[:taps]
    return (
        output[None],
        input_gradient[None],
        value_grad,
        gate_grad,
        kernel_grad,
        out_grad,
    )


def solution(mesh):
    return jax.shard_map(
        shards,
        mesh=mesh,
        in_specs=(
            P("dp", "seq", "tensor"),
            P("dp"),
            P("dp", "seq", "tensor"),
            P(None, "tensor"),
            P(None, "tensor"),
            P(None, "tensor"),
            P("tensor", None),
        ),
        out_specs=(
            P("dp", "seq", "tensor"),
            P("dp", "seq", "tensor"),
            P(("seq", "dp"), "tensor"),
            P(("seq", "dp"), "tensor"),
            P(None, "tensor"),
            P("tensor", ("seq", "dp")),
        ),
        check_vma=False,
    )
```

```python
import functools

import jax
import jax.numpy as jnp
from jax import lax
from jax.experimental import pallas as pl
from jax.experimental.pallas import tpu as pltpu
from jax.sharding import PartitionSpec as P

epsilon = 1e-05
f32, bf16 = jnp.float32, jnp.bfloat16
LANES = 128
WIDE, NEAR = 32, 16
NN = (((1,), (0,)), ((), ()))
NT = (((1,), (1,)), ((), ()))
TN = (((0,), (0,)), ((), ()))
VMEM = pl.BlockSpec(memory_space=pltpu.VMEM)
SMEM = pl.BlockSpec(memory_space=pltpu.SMEM)
ANY = pl.BlockSpec(memory_space=pl.ANY)
HBM = pl.BlockSpec(memory_space=pltpu.HBM)


def dot(a, b, dims=NN):
    return lax.dot_general(a, b, dims, preferred_element_type=f32)


def run(kernel, info, args, outs, scratch=(), after=(), limit=8, space=VMEM, to=VMEM, far=()):
    near = len(args)

    def body(*refs):
        lead = 1 + near + len(far)
        rest = refs[lead + len(after) :]
        kernel(*refs[:lead], *rest[: len(outs)], *rest[len(outs) + 1 :])
        rest[len(outs)][...] = jnp.zeros((8, LANES), f32)

    args = [pltpu.with_memory_space_constraint(a, space.memory_space) for a in args]
    args += [pltpu.with_memory_space_constraint(a, pltpu.HBM) for a in far]
    *results, mark = pl.pallas_call(
        body,
        in_specs=[SMEM] + [space] * near + [HBM] * len(far) + [ANY] * len(after),
        out_specs=[to] * len(outs) + [VMEM],
        out_shape=[to.memory_space(shape, dtype) for shape, dtype in outs]
        + [pltpu.VMEM((8, LANES), f32)],
        scratch_shapes=list(scratch),
        compiler_params=pltpu.CompilerParams(vmem_limit_bytes=limit << 20),
        cost_estimate=pl.CostEstimate(flops=COST, bytes_accessed=COST, transcendentals=0),
        name=kernel.__name__ if hasattr(kernel, "__name__") else kernel.func.__name__,
    )(info, *args, *after)
    return *results, mark


COST = 1 << 10


def swap(value, axis, bit=0):
    size = lax.axis_size(axis)
    return lax.ppermute(value, axis, [(i, i ^ (1 << bit)) for i in range(size)])


def bits_of(axis):
    return [(axis, b) for b in range(lax.axis_size(axis).bit_length() - 1)]


def every_bit():
    return bits_of("dp") + bits_of("seq")


def split_rows(info, bit, place, total, rows, keep, send, load):
    run_length = rows << place
    for j in range(total // (2 * run_length)):
        for put, side in ((keep, info[4 + bit]), (send, 1 - info[4 + bit])):
            if run_length % 32:
                low, high = (
                    load(slice((2 * j + i) * run_length, (2 * j + i + 1) * run_length))
                    for i in (0, 1)
                )
                value = jnp.where(side == 0, low, high)
            else:
                at = pl.multiple_of((2 * j + side) * run_length, run_length)
                value = load(pl.ds(at, run_length))
            put(j * run_length, value)


def put_into(target):
    def put(at, value):
        target[at : at + value.shape[0], :] = value

    return put


def put_folded(target, first, half):
    columns = target.shape[1] // 2

    def put(at, value):
        length = value.shape[0]
        for low in range(0, length, min(length, half)):
            part = value[low : low + min(length, half)]
            side, row = divmod(at + low, half)
            to = slice(first + row, first + row + part.shape[0])
            target[to, side * columns : (side + 1) * columns] = part

    return put


def add(a, b):
    return (a.astype(f32) + b.astype(f32)).astype(bf16)


def first_split(info, product, okept, ogot, vkeep, okeep, send, *, third, rows):
    total = product.shape[0]
    split_rows(info, third, third, total, rows, put_into(vkeep), put_into(send), lambda at: product[at, :])
    before = (third + 2) % 3
    place = third - (before < third)
    fold = put_folded(send, total // 2, total // 8)
    load = lambda at: add(okept[at, :], ogot[at, :])
    split_rows(info, third, place, total // 2, rows, put_into(okeep), fold, load)


def unfold(got, first, rows, target):
    half = rows // 2
    columns = target.shape[1]
    target[:half, :] = got[first : first + half, :columns]
    target[half:, :] = got[first : first + half, columns:]


def ride(taps, send):
    rows, columns = taps.shape[0], send.shape[1]
    value = taps[...].astype(bf16)
    first = send.shape[0] - rows - rows // 2
    send[first : first + rows, :] = value[:, :columns]
    send[first + rows :, : columns // 2] = value[: rows // 2, columns:]
    send[first + rows :, columns // 2 :] = value[rows // 2 :, columns:]


def alight(taps, got, result):
    rows, columns = taps.shape[0], got.shape[1]
    first = got.shape[0] - rows - rows // 2
    value = taps[...].astype(bf16).astype(f32)
    half = rows // 2
    result[:, :columns] = value[:, :columns] + got[first : first + rows, :].astype(f32)
    result[:half, columns:] = value[:half, columns:] + got[
        first + rows :, : columns // 2
    ].astype(f32)
    result[half:, columns:] = value[half:, columns:] + got[
        first + rows :, columns // 2 :
    ].astype(f32)


def second_split(info, vkept, okept, got, *refs, third, rows):
    *taps, vkeep, okeep, send, flat = refs
    if taps:
        ride(taps[0], send)
    total = vkept.shape[0]
    bit = (third + 1) % 3
    left = [b for b in range(3) if b != third]
    load = lambda at: add(vkept[at, :], got[at, :])
    split_rows(info, bit, left.index(bit), total, rows, put_into(vkeep), put_into(send), load)
    unfold(got, total, total // 2, flat)
    fold = put_folded(send, total // 2, total // 8)
    load = lambda at: add(okept[at, :], flat[at, :])
    split_rows(info, bit, 0, total // 2, rows, put_into(okeep), fold, load)


def third_split(info, vkept, okept, got, *refs, third, rows):
    if third == 1:
        taps, vkeep, okeep, send, sums, flat = refs
        alight(taps, got, sums)
    elif third == 2:
        sums, vkeep, okeep, send, flat = refs
        ride(sums, send)
    else:
        vkeep, okeep, send, flat = refs
    total = vkept.shape[0]
    bit, place = ((third + 2) % 3, 0) if third else (3, 1)
    load = lambda at: add(vkept[at, :], got[at, :])
    split_rows(info, bit, place, total, rows, put_into(vkeep), put_into(send), load)
    unfold(got, total, total // 2, flat)
    if third:
        okeep[...] = add(okept[...], flat[...])
    else:
        fold = put_folded(send, total // 2, total // 8)
        load = lambda at: add(okept[at, :], flat[at, :])
        split_rows(info, bit, 0, total // 2, rows, put_into(okeep), fold, load)


def first_last_split(info, vkept, okept, got, keep, send, osum, flat, *, rows):
    total = vkept.shape[0]
    load = lambda at: add(vkept[at, :], got[at, :])
    split_rows(info, 2, 0, total, rows, put_into(keep), put_into(send), load)
    unfold(got, total, total // 2, flat)
    osum[...] = okept[...].astype(f32) + flat[...].astype(f32)


def last_split(info, vkept, okept, got, *refs, rows):
    keep, send = refs[len(refs) // 4 :][:2]
    total, columns = vkept.shape
    if len(refs) > 2:
        alight(refs[0], got, refs[3])
        keep[total // 2 :, :] = refs[3][...].astype(bf16)
        send[total // 2 :, :] = refs[3][...].astype(bf16)

    def put(target):
        def to(at, value):
            target[at : at + value.shape[0], : value.shape[1]] = value

        return to

    load = lambda at: add(vkept[at, :], got[at, :])
    split_rows(info, 3, 0, total, rows, put(keep), put(send), load)

    def side(target):
        def to(at, value):
            target[at : at + value.shape[0], columns:] = value

        return to

    split_rows(info, 3, 0, total, rows, side(keep), side(send), lambda at: okept[at, :])


def send_bit(value, bit):
    return swap(value, *every_bit()[bit])


def finish(value, rows):
    for bit in range(4, len(every_bit())):
        axis, place = every_bit()[bit]
        value = value.astype(bf16).reshape(-1, 2, rows, value.shape[1])
        mine = (lax.axis_index(axis) >> place) & 1
        keep, send = (
            lax.dynamic_index_in_dim(value, side, 1, keepdims=False) for side in (mine, 1 - mine)
        )
        shape = (-1, value.shape[-1])
        value = keep.reshape(shape).astype(f32) + send_bit(send.reshape(shape), bit).astype(f32)
    return value


def sigmoid(v):
    return 0.5 + 0.5 * jnp.tanh(0.5 * v)


def row_mask(info, first, rows, limit):
    place = info[0] + first + lax.broadcasted_iota(jnp.int32, (rows, 1), 0)
    return ((place >= 0) & (place < limit)).astype(f32)


def halves_at(info, half):
    return (
        pl.multiple_of(info[3] * half, half),
        pl.multiple_of((1 - info[3]) * half, half),
    )


def start_all(pairs, sem):
    copies = [pltpu.make_async_copy(a, b, sem.at[i]) for i, (a, b) in enumerate(pairs)]
    for c in copies:
        c.start()
    return copies


def prepare(info, ct, w_out, ct_to, w_to, sem):
    for c in start_all([(w_out, w_to), (ct, ct_to)], sem):
        c.wait()


def pick(info, x, ct, last, first, sem):
    count = x.shape[0]
    copies = [
        pltpu.make_async_copy(source.at[a : a + n], target.at[b : b + n], sem.at[i])
        for i, (source, target, a, b, n) in enumerate(
            (
                (x, last, count - WIDE, 0, WIDE),
                (ct, last, count - NEAR, WIDE, NEAR),
                (x, first, 0, 0, WIDE),
                (ct, first, 0, WIDE, NEAR),
            )
        )
    ]
    for c in copies:
        c.start()
    for c in copies:
        c.wait()


def pack(info, before, after, halo):
    rows = before.shape[0]
    halo[:rows, :] = before[...]
    halo[rows:, :] = after[...]


def upstream(info, own, other, w_out, x, wv, wg, full, pull, x_to, wv_to, wg_to, sem):
    count, half = own.shape
    copies = start_all([(x, x_to), (wv, wv_to), (wg, wg_to)], sem)
    mine, theirs = halves_at(info, half)
    full[:, pl.ds(mine, half)] = own[...]
    full[:, pl.ds(theirs, half)] = other[...]
    step = count // 2
    for c in range(0, count, step):
        pull[c : c + step, :] = dot(full[c : c + step, :], w_out[...], NT).astype(bf16)
    for c in copies:
        c.wait()


def upstream_ends(info, halo_own, halo_other, w_out, ends, edge):
    half = halo_own.shape[1]
    mine, theirs = halves_at(info, half)
    for a, at in ((halo_own, mine), (halo_other, theirs)):
        edge[:NEAR, pl.ds(at, half)] = a[WIDE : WIDE + NEAR, :]
        edge[NEAR:, pl.ds(at, half)] = a[2 * WIDE + NEAR :, :]
    ends[...] = dot(edge[...], w_out[...], NT)


def front(info, own, other, halo_own, halo_other, wv, wg, norm, rstd, hid, sig, slope):
    count, half = own.shape
    channels = wv.shape[1]
    mine, theirs = halves_at(info, half)

    def normalize(to, a, b):
        a, b = a.astype(f32), b.astype(f32)
        width = 2 * half
        mean = (jnp.sum(a, 1, keepdims=True) + jnp.sum(b, 1, keepdims=True)) / width
        a, b = a - mean, b - mean
        var = jnp.sum(a * a, 1, keepdims=True) + jnp.sum(b * b, 1, keepdims=True)
        inverse = lax.rsqrt(var / width + epsilon)
        norm[to, pl.ds(mine, half)] = (a * inverse).astype(bf16)
        norm[to, pl.ds(theirs, half)] = (b * inverse).astype(bf16)
        return inverse

    chunk = 128

    def body(i, _):
        at = pl.multiple_of(i * chunk, chunk)
        inverse = normalize(
            pl.ds(pl.multiple_of(WIDE + at, WIDE), chunk),
            own[pl.ds(at, chunk), :],
            other[pl.ds(at, chunk), :],
        )
        rstd[pl.ds(at, chunk), :] = jnp.broadcast_to(inverse, (chunk, LANES))
        return 0

    lax.fori_loop(0, count // chunk, body, 0, unroll=2)
    for to, at in ((0, 0), (WIDE + count, WIDE + NEAR)):
        normalize(pl.ds(to, WIDE), halo_own[at : at + WIDE, :], halo_other[at : at + WIDE, :])
    tile = channels // 3
    rows = count + 2 * WIDE
    step = rows // 2
    for n in range(0, channels, tile):
        cols = slice(n, n + tile)
        for c in range(0, rows, step):
            value = dot(norm[c : c + step, :], wv[:, cols])
            s = sigmoid(dot(norm[c : c + step, :], wg[:, cols]))
            keep = row_mask(info, c - WIDE, step, info[1])
            vs = value * s * keep
            hid[c : c + step, cols] = vs.astype(bf16)
            low, high = max(c, WIDE), min(c + step, WIDE + count)
            part = slice(low - c, high - c)
            sig[low - WIDE : high - WIDE, cols] = (s * keep)[part].astype(bf16)
            slope[low - WIDE : high - WIDE, cols] = (vs * (1.0 - s))[part].astype(bf16)


def tap_sums(source, base, groups, taps):
    sums = [None] * groups
    for residue in range(8):
        mine = list(range(residue, len(taps), 8))
        shifted = [
            source[pl.ds(base + 8 * i + residue, 8), :] for i in range(groups + len(mine) - 1)
        ]
        for i, k in enumerate(mine):
            for g in range(groups):
                term = shifted[g + i] * taps[k]
                sums[g] = term if sums[g] is None else sums[g] + term
    return sums


def tap_rows(taps, cols, reverse=False):
    values = taps[:, cols].astype(f32)
    order = range(taps.shape[0])
    return [
        jnp.broadcast_to(values[k : k + 1, :], (8, LANES))
        for k in (reversed(order) if reverse else order)
    ]


def lane_tile(n):
    return pl.ds(pl.multiple_of(n * LANES, LANES), LANES)


def paired(first, second):
    lane = lax.broadcasted_iota(jnp.int32, (first.shape[0], LANES), 1)
    return jnp.where(
        lane < LANES // 2,
        jnp.sum(first, axis=1, keepdims=True),
        jnp.sum(second, axis=1, keepdims=True),
    )


def depthwise(info, hid, taps, conv, stats, scratch, total, square):
    rows = conv.shape[0]
    skip = WIDE - NEAR - (taps.shape[0] - 1) // 2
    groups = 20
    total[...] = jnp.zeros_like(total)
    square[...] = jnp.zeros_like(square)

    def tile(n, _):
        cols = lane_tile(n)
        scratch[: hid.shape[0], :] = hid[:, cols].astype(f32)
        weights = tap_rows(taps, cols)

        def body(i, _):
            base = pl.multiple_of(i * 8 * groups, 8)
            for g, value in enumerate(tap_sums(scratch, base + skip, groups, weights)):
                at = pl.ds(base + 8 * g, 8)
                conv[at, cols] = value
                total[at, :] += value
                square[at, :] += value * value
            return 0

        lax.fori_loop(0, rows // (8 * groups), body, 0)
        return 0

    lax.fori_loop(0, conv.shape[1] // LANES, tile, 0)
    stats[...] = paired(total[...], square[...])


def moments(first, second, width):
    mean = (first[:, :1] + second[:, :1]) / width
    half = LANES // 2
    square = (first[:, half : half + 1] + second[:, half : half + 1]) / width
    return mean, lax.rsqrt(square - mean * mean + epsilon)


def swish(info, conv, pull, ends, own, other, swished, dswish, stats):
    count, channels = pull.shape

    def part(at, g, rows):
        to = pl.ds(at, rows)
        mean, inverse = moments(own[to, :], other[to, :], 2 * channels)
        zhat = (conv[to, :] - mean) * inverse
        s = sigmoid(zhat)
        zs = zhat * s
        d = g * (s + zs * (1.0 - s))
        dswish[to, :] = d
        stats[to, :] = paired(d, d * zhat)
        return zs.astype(bf16)

    part(0, ends[:NEAR, :], NEAR)
    part(NEAR + count, ends[NEAR:, :], NEAR)
    step = 64

    def body(i, _):
        at = pl.multiple_of(i * step, step)
        rows = pl.ds(at, step)
        g = pull[rows, :].astype(f32)
        swished[rows, :] = part(pl.multiple_of(at + NEAR, NEAR), g, step)
        return 0

    lax.fori_loop(0, count // step, body, 0, unroll=2)


def out_terms(info, full, swished, *refs, rows):
    halves, product = refs[:-1], refs[-1]
    width = full.shape[1]
    cols = swished.shape[1] // 3
    step = width // 4
    for c in range(0, width, step):
        product[c : c + step, :] = dot(full[:, c : c + step], swished[...], TN).astype(bf16)
    for i in range(3):
        load = lambda at: product[at, i * cols : (i + 1) * cols]
        keep, send = (put_into(half) for half in halves[2 * i : 2 * i + 2])
        split_rows(info, i, i, width, rows, keep, send, load)


def slopes(info, own, other, own2, other2, coef, width):
    rows = own.shape[0]
    mean, inverse = moments(own[...], other[...], width)
    half = LANES // 2
    shift = (own2[:, :1] + other2[:, :1]) / width
    cross = (own2[:, half : half + 1] + other2[:, half : half + 1]) / width
    inverse = inverse * row_mask(info, -NEAR, rows, info[2])
    tilt = inverse * inverse * cross
    coef[0] = jnp.broadcast_to(inverse, (rows, LANES))
    coef[1] = jnp.broadcast_to(tilt, (rows, LANES))
    coef[2] = jnp.broadcast_to(tilt * mean - inverse * shift, (rows, LANES))


def back(info, dswish, conv, taps, sig, slope, norm, *refs, third):
    rows, channels = dswish.shape
    count = sig.shape[0]
    width = 2 * channels
    if third == 0:
        *sums, dconv, dvg, product, coef, scratch = refs
        slopes(info, *sums, coef, width)
    else:
        coef, dconv, dvg, product, scratch = refs
    tiles = channels // LANES // 3
    groups = 16
    skip = NEAR - (taps.shape[0] - 1) // 2

    def tile(n, _):
        local = lane_tile(n)
        cols = lane_tile(third * tiles + n)
        d = (coef[0] * dswish[:, cols] - coef[1] * conv[:, cols] + coef[2]).astype(bf16)
        dconv[:, local] = d
        scratch[:rows, :] = d.astype(f32)
        weights = tap_rows(taps, cols, reverse=True)

        def body(i, _):
            base = pl.multiple_of(i * 8 * groups, 16)
            sums = tap_sums(scratch, base + skip, groups, weights)
            for g in range(0, groups, 2):
                at = pl.ds(base + 8 * g, 16)
                dh = jnp.concatenate(sums[g : g + 2], axis=0)
                dvg[at, local] = (dh * sig[at, cols]).astype(bf16)
                dvg[at, lane_tile(tiles + n)] = (dh * slope[at, cols]).astype(bf16)
            return 0

        lax.fori_loop(0, count // (8 * groups), body, 0)
        return 0

    lax.fori_loop(0, tiles, tile, 0)
    step = width // 4
    for c in range(0, width, step):
        r = dot(norm[WIDE : WIDE + count, c : c + step], dvg[...], TN)
        product[c : c + step, :] = r.astype(bf16)


def taps_sums(info, dconv, hid, out, scratch, total, *, third):
    rows, channels = dconv.shape
    count = rows - 2 * NEAR
    taps = total.shape[0]
    half = (taps - 1) // 2
    groups = 16
    tiles = channels // LANES

    def tile(n, _):
        local = lane_tile(n)
        cols = lane_tile(third * tiles + n)
        scratch[:rows, :] = dconv[:, local].astype(f32)
        total[...] = jnp.zeros_like(total)

        def body(i, _):
            base = pl.multiple_of(i * 8 * groups, 16)
            h = []
            for g in range(0, groups, 2):
                both = hid[pl.ds(pl.multiple_of(WIDE + base + 8 * g, 16), 16), cols].astype(f32)
                h += [both[:8], both[8:]]
            for residue in range(8):
                mine = list(range(residue, taps, 8))
                shifted = [
                    scratch[pl.ds(base + NEAR - half + 8 * g + residue, 8), :]
                    for g in range(groups + len(mine) - 1)
                ]
                for j, m in enumerate(mine):
                    term = shifted[j] * h[0]
                    for g in range(1, groups):
                        term = term + shifted[g + j] * h[g]
                    total[taps - 1 - m] += term
            return 0

        lax.fori_loop(0, count // (8 * groups), body, 0)
        out[:taps, local] = jnp.sum(total[...], axis=1)
        out[taps:, local] = jnp.zeros((out.shape[0] - taps, LANES), f32)
        return 0

    lax.fori_loop(0, tiles, tile, 0)


def add_taps(info, value, got, result):
    result[...] = value[...] + got[...]


def out_half(info, swished, w_out, result, *, own):
    half = result.shape[1]
    at = halves_at(info, half)[0 if own else 1]
    step = swished.shape[0] // 2
    for r in range(0, swished.shape[0], step):
        part = dot(swished[r : r + step, :], w_out[:, pl.ds(at, half)])
        result[r : r + step, :] = part.astype(result.dtype)


def norm_half(info, a, b, c, wv, wg, *results, own):
    half = results[0].shape[1]
    at = halves_at(info, half)[0 if own else 1]
    third = half // 3
    step = a.shape[0] // 2
    for n, result in enumerate(results):
        r = n * step
        total = None
        for i, dvg in enumerate((a, b, c)):
            cols = slice(i * third, (i + 1) * third)
            for j, w in enumerate((wv, wg)):
                part = dot(
                    dvg[r : r + step, j * third : (j + 1) * third], w[pl.ds(at, half), cols], NT
                )
                total = part if total is None else total + part
        result[...] = total.astype(result.dtype)


def norm_sums(info, mine0, mine1, got0, got1, norm, total, stats):
    count, half = total.shape
    at = halves_at(info, half)[0]
    step = 32
    for n, (mine, got) in enumerate(((mine0, got0), (mine1, got1))):
        start = n * count // 2

        def body(i, _):
            here = pl.multiple_of(i * step, step)
            rows, to = pl.ds(here, step), pl.ds(start + here, step)
            xhat = norm[pl.ds(WIDE + start + here, step), pl.ds(at, half)]
            d = mine[rows, :] + got[rows, :].astype(f32)
            total[to, :] = d
            stats[to, :] = paired(d, d * xhat.astype(f32))
            return 0

        lax.fori_loop(0, count // 2 // step, body, 0, unroll=2)


def written(result, buffer, sem, part):
    count, step = buffer.shape[0], buffer.shape[0] // sem.shape[0]
    copies = []
    for i in range(sem.shape[0]):
        rows = slice(i * step, (i + 1) * step)
        buffer[rows, :] = part(i * step, step)
        copies.append(pltpu.make_async_copy(buffer.at[rows], result.at[rows], sem.at[i]))
        copies[-1].start()
    for c in copies:
        c.wait()


def input_rows(info, ct, total, norm, rstd, own, other, result, buffer, sem):
    count, half = total.shape
    at = halves_at(info, half)[0]

    def part(first, step):
        rows = slice(first, first + step)
        xhat = norm[WIDE + first : WIDE + first + step, pl.ds(at, half)].astype(f32)
        sums = (own[rows, :] + other[rows, :]) / (2 * half)
        mean, cross = sums[:, :1], sums[:, LANES // 2 : LANES // 2 + 1]
        gradient = rstd[rows, :1] * (total[rows, :] - mean - xhat * cross)
        return (ct[rows, :].astype(f32) + gradient).astype(bf16)

    written(result, buffer, sem, part)


def output_rows(info, x, mine, got, result, buffer, sem):
    def part(first, step):
        rows = slice(first, first + step)
        return (x[rows, :].astype(f32) + mine[rows, :] + got[rows, :].astype(f32)).astype(bf16)

    written(result, buffer, sem, part)


def shards(inputs, lengths, cotangent, w_value, w_gate, kernel, w_out):
    x, ct = inputs[0], cotangent[0]
    count, channels = x.shape
    width = channels * lax.axis_size("tensor")
    core = lax.axis_index("tensor")
    peers = lax.axis_size("seq")
    every = every_bit()
    block = width >> len(every)
    taps = kernel.shape[0]
    info = jnp.stack(
        [lax.axis_index("seq") * count, lengths[0], jnp.int32(peers * count), core]
        + [(lax.axis_index(a) >> b) & 1 for a, b in every]
    ).astype(jnp.int32)

    up = [(i, i + 1) for i in range(peers - 1)]
    down = [(j, i) for i, j in up]
    x_other, ct_other = swap(x, "tensor"), swap(ct, "tensor")
    last, first, mark = run(
        pick,
        info,
        [x, ct],
        [((WIDE + NEAR, channels), bf16)] * 2,
        scratch=[pltpu.SemaphoreType.DMA((4,))],
        space=HBM,
    )
    before, after = lax.ppermute(last, "seq", up), lax.ppermute(first, "seq", down)
    ctv, wo, mark = run(
        prepare,
        info,
        [ct, w_out],
        [(ct.shape, bf16), (w_out.shape, bf16)],
        scratch=[pltpu.SemaphoreType.DMA((2,))],
        after=[mark],
        space=HBM,
    )
    halo, mark = run(
        pack, info, [before, after], [((2 * (WIDE + NEAR), channels), bf16)], after=[mark]
    )
    halo_other = swap(halo, "tensor")

    rows, ext = count + 2 * NEAR, count + 2 * WIDE
    full, pull, xv, wv, wg, mark = run(
        upstream,
        info,
        [ctv, ct_other, wo],
        [((count, width), bf16), ((count, channels), bf16)]
        + [(a.shape, bf16) for a in (x, w_value, w_gate)],
        scratch=[pltpu.SemaphoreType.DMA((3,))],
        after=[mark],
        far=[x, w_value, w_gate],
    )
    norm, rstd, hid, sig, slope, _ = run(
        front,
        info,
        [xv, x_other, halo, halo_other, wv, wg],
        [
            ((ext, width), bf16),
            ((count, LANES), f32),
            ((ext, channels), bf16),
            ((count, channels), bf16),
            ((count, channels), bf16),
        ],
        after=[mark],
    )
    row_sums = ((rows, LANES), f32)
    column = pltpu.VMEM((rows, LANES), f32)
    conv, stats, mark = run(
        depthwise,
        info,
        [hid, kernel],
        [((rows, channels), f32), row_sums],
        scratch=[pltpu.VMEM((ext + 16, LANES), f32), column, column],
    )
    stats_other = swap(stats, "tensor")
    ends, mark = run(
        upstream_ends,
        info,
        [halo, halo_other, wo],
        [((2 * NEAR, channels), f32)],
        scratch=[pltpu.VMEM((2 * NEAR, width), bf16)],
        after=[mark],
    )
    swished, dswish, stats2, _ = run(
        swish,
        info,
        [conv, pull, ends, stats, stats_other],
        [((count, channels), bf16), ((rows, channels), f32), row_sums],
    )
    stats2_other = swap(stats2, "tensor")

    third = channels // 3
    *out_parts, mark = run(
        functools.partial(out_terms, rows=block),
        info,
        [full, swished],
        [((width // 2, third), bf16)] * 6,
        scratch=[pltpu.VMEM((width, channels), bf16)],
    )
    out_got = [send_bit(out_parts[2 * i + 1], i) for i in range(3)]

    def out_part(own, mark):
        return run(
            functools.partial(out_half, own=own),
            info,
            [swished, wo],
            [((count, channels), f32 if own else bf16)],
            after=[mark],
        )

    dconvs, dvgs, kept, got = [], [], [], []
    sums = [stats, stats_other, stats2, stats2_other]
    for i in range(3):
        dconv, dvg, product, *coef, mark = run(
            functools.partial(back, third=i),
            info,
            [dswish, conv, kernel, sig, slope, norm, *sums],
            [((rows, third), bf16), ((count, 2 * third), bf16), ((width, 2 * third), bf16)]
            + [((3, rows, LANES), f32)] * (i == 0),
            scratch=[pltpu.VMEM((rows + 16, LANES), f32)],
            after=[mark],
        )
        if i == 0:
            sums = coef
        if i == 0:
            out_theirs, mark = out_part(False, mark)
            out_other = swap(out_theirs, "tensor")
            out_mine, mark = out_part(True, mark)
        previous = (i + 2) % 3
        vkeep, okeep, send, mark = run(
            functools.partial(first_split, third=i, rows=block),
            info,
            [product, out_parts[2 * previous], out_got[previous]],
            [
                ((width // 2, 2 * third), bf16),
                ((width // 4, third), bf16),
                ((width // 2 + width // 8, 2 * third), bf16),
            ],
            after=[mark, *out_got],
        )
        dconvs.append(dconv)
        dvgs.append(dvg)
        kept.append((vkeep, okeep))
        got.append(send_bit(send, i))

    extra = (taps + 1) * 3 // 2

    def second(i, mark, *riding):
        vkeep, okeep, send, mark = run(
            functools.partial(second_split, third=i, rows=block),
            info,
            [*kept[i], got[i], *riding],
            [
                ((width // 4, 2 * third), bf16),
                ((width // 8, third), bf16),
                ((width // 4 + width // 16 + extra * len(riding), 2 * third), bf16),
            ],
            scratch=[pltpu.VMEM((width // 4, third), bf16)],
            after=[mark],
        )
        kept[i], got[i] = (vkeep, okeep), send_bit(send, (i + 1) % 3)
        return mark

    def third_step(i, mark, *riding):
        off, on = (riding, ()) if i == 1 else ((), riding)
        vkeep, okeep, send, *sums, mark = run(
            functools.partial(third_split, third=i, rows=block),
            info,
            [*kept[i], got[i], *riding],
            [
                ((width // 8, 2 * third), bf16),
                ((width // 8 if i else width // 16, third), bf16),
                ((width // 8 + (extra * len(on) if i else width // 32), 2 * third), bf16),
            ]
            + [(r.shape, f32) for r in off],
            scratch=[pltpu.VMEM((width // 8, third), bf16)],
            after=[mark],
        )
        kept[i], got[i] = (vkeep, okeep), send_bit(send, (i + 2) % 3 if i else 3)
        return *sums, mark

    def last_step(i, mark, *riding):
        behind = (taps + 1) * len(riding)
        if i == 0:
            keep, send, osum, mark = run(
                functools.partial(first_last_split, rows=block),
                info,
                [*kept[0], got[0]],
                [((width // 16, 2 * third), bf16)] * 2 + [((width // 16, third), f32)],
                scratch=[pltpu.VMEM((width // 16, third), bf16)],
                after=[mark],
            )
            return keep.astype(f32) + send_bit(send, 2).astype(f32), osum, mark
        keep, send, mark = run(
            functools.partial(last_split, rows=block),
            info,
            [*kept[i], got[i], *riding],
            [((width // 16 + behind, 3 * third), bf16)] * 2,
            scratch=[pltpu.VMEM(r.shape, f32) for r in riding],
            after=[mark],
        )
        value = keep.astype(f32) + send_bit(send, 3).astype(f32)
        return value[: width // 16], value[width // 16 :], mark

    def norm_part(own, mark):
        return run(
            functools.partial(norm_half, own=own),
            info,
            [*dvgs, wv, wg],
            [((count // 2, channels), f32 if own else bf16)] * 2,
            after=[mark],
        )

    def taps_part(i, mark):
        return run(
            functools.partial(taps_sums, third=i),
            info,
            [dconvs[i], hid],
            [((taps + 1, third), f32)],
            scratch=[pltpu.VMEM((rows + 16, LANES), f32), pltpu.VMEM((taps, 8, LANES), f32)],
            after=[mark],
        )

    def final(kernel, args, mark):
        return run(
            kernel,
            info,
            args,
            [((count, channels), bf16)],
            scratch=[pltpu.VMEM((count, channels), bf16), pltpu.SemaphoreType.DMA((4,))],
            after=[mark],
            to=HBM,
        )

    parts = []
    for i in range(3):
        part, mark = taps_part(i, mark)
        parts.append(part)
    taps_own = jnp.concatenate(parts, axis=1)
    *mine, mark = norm_part(True, mark)
    mark = second(0, mark)
    taps_sum, mark = run(
        add_taps, info, [taps_own, send_bit(taps_own, 0)], [(taps_own.shape, f32)], after=[mark]
    )
    *theirs, mark = norm_part(False, mark)
    theirs = [swap(t, "tensor") for t in theirs]
    mark = second(1, mark, taps_sum)
    dnorm, stats3, mark = run(
        norm_sums,
        info,
        [*mine, *theirs, norm],
        [((count, channels), f32), ((count, LANES), f32)],
        after=[mark],
    )
    stats3_other = swap(stats3, "tensor")
    mark = second(2, mark)
    output, mark = final(output_rows, [x, out_mine, out_other], mark)
    input_gradient, mark = final(
        input_rows, [ct, dnorm, norm, rstd, stats3, stats3_other], mark
    )
    (mark,) = third_step(0, mark)
    taps_sum, mark = third_step(1, mark, taps_sum)
    (mark,) = third_step(2, mark, taps_sum)
    total0, out2, mark = last_step(0, mark)
    total1, _, mark = last_step(1, mark)
    total2, kernel_grad, mark = last_step(2, mark, taps_sum)
    totals = [finish(t, block) for t in (total0, total1, total2)]
    value_grad, gate_grad = (
        jnp.concatenate([t[:, j * third : (j + 1) * third] for t in totals], axis=1)
        for j in (0, 1)
    )
    out_grad = jnp.concatenate(
        [totals[1][:, 2 * third :], totals[2][:, 2 * third :], finish(out2, block)], axis=1
    ).T
    for bit in range(4, len(every)):
        kernel_grad = kernel_grad + send_bit(kernel_grad, bit)
    kernel_grad = kernel_grad[:taps]
    return (
        output[None],
        input_gradient[None],
        value_grad,
        gate_grad,
        kernel_grad,
        out_grad,
    )


def solution(mesh):
    return jax.shard_map(
        shards,
        mesh=mesh,
        in_specs=(
            P("dp", "seq", "tensor"),
            P("dp"),
            P("dp", "seq", "tensor"),
            P(None, "tensor"),
            P(None, "tensor"),
            P(None, "tensor"),
            P("tensor", None),
        ),
        out_specs=(
            P("dp", "seq", "tensor"),
            P("dp", "seq", "tensor"),
            P(("seq", "dp"), "tensor"),
            P(("seq", "dp"), "tensor"),
            P(None, "tensor"),
            P("tensor", ("seq", "dp")),
        ),
        check_vma=False,
    )
```

```python
import functools

import jax
import jax.numpy as jnp
from jax import lax
from jax.experimental import pallas as pl
from jax.experimental.pallas import tpu as pltpu
from jax.sharding import PartitionSpec as P

epsilon = 1e-05
f32, bf16 = jnp.float32, jnp.bfloat16
LANES = 128
WIDE, NEAR = 32, 16
NN = (((1,), (0,)), ((), ()))
NT = (((1,), (1,)), ((), ()))
TN = (((0,), (0,)), ((), ()))
VMEM = pl.BlockSpec(memory_space=pltpu.VMEM)
SMEM = pl.BlockSpec(memory_space=pltpu.SMEM)
ANY = pl.BlockSpec(memory_space=pl.ANY)
HBM = pl.BlockSpec(memory_space=pltpu.HBM)


def dot(a, b, dims=NN):
    return lax.dot_general(a, b, dims, preferred_element_type=f32)


def run(kernel, info, args, outs, scratch=(), after=(), limit=8, space=VMEM, to=VMEM, far=()):
    near = len(args)

    def body(*refs):
        lead = 1 + near + len(far)
        rest = refs[lead + len(after) :]
        kernel(*refs[:lead], *rest[: len(outs)], *rest[len(outs) + 1 :])
        rest[len(outs)][...] = jnp.zeros((8, LANES), f32)

    args = [pltpu.with_memory_space_constraint(a, space.memory_space) for a in args]
    args += [pltpu.with_memory_space_constraint(a, pltpu.HBM) for a in far]
    *results, mark = pl.pallas_call(
        body,
        in_specs=[SMEM] + [space] * near + [HBM] * len(far) + [ANY] * len(after),
        out_specs=[to] * len(outs) + [VMEM],
        out_shape=[to.memory_space(shape, dtype) for shape, dtype in outs]
        + [pltpu.VMEM((8, LANES), f32)],
        scratch_shapes=list(scratch),
        compiler_params=pltpu.CompilerParams(vmem_limit_bytes=limit << 20),
        cost_estimate=pl.CostEstimate(flops=COST, bytes_accessed=COST, transcendentals=0),
        name=kernel.__name__ if hasattr(kernel, "__name__") else kernel.func.__name__,
    )(info, *args, *after)
    return *results, mark


COST = 1 << 10


def swap(value, axis, bit=0):
    size = lax.axis_size(axis)
    return lax.ppermute(value, axis, [(i, i ^ (1 << bit)) for i in range(size)])


def bits_of(axis):
    return [(axis, b) for b in range(lax.axis_size(axis).bit_length() - 1)]


def every_bit():
    return bits_of("dp") + bits_of("seq")


def split_rows(info, bit, place, total, rows, keep, send, load):
    run_length = rows << place
    for j in range(total // (2 * run_length)):
        for put, side in ((keep, info[4 + bit]), (send, 1 - info[4 + bit])):
            if run_length % 32:
                low, high = (
                    load(slice((2 * j + i) * run_length, (2 * j + i + 1) * run_length))
                    for i in (0, 1)
                )
                value = jnp.where(side == 0, low, high)
            else:
                at = pl.multiple_of((2 * j + side) * run_length, run_length)
                value = load(pl.ds(at, run_length))
            put(j * run_length, value)


def put_into(target):
    def put(at, value):
        target[at : at + value.shape[0], :] = value

    return put


def put_folded(target, first, half):
    columns = target.shape[1] // 2

    def put(at, value):
        length = value.shape[0]
        for low in range(0, length, min(length, half)):
            part = value[low : low + min(length, half)]
            side, row = divmod(at + low, half)
            to = slice(first + row, first + row + part.shape[0])
            target[to, side * columns : (side + 1) * columns] = part

    return put


def add(a, b):
    return (a.astype(f32) + b.astype(f32)).astype(bf16)


def first_split(info, product, okept, ogot, vkeep, okeep, send, *, third, rows):
    total = product.shape[0]
    split_rows(info, third, third, total, rows, put_into(vkeep), put_into(send), lambda at: product[at, :])
    before = (third + 2) % 3
    place = third - (before < third)
    fold = put_folded(send, total // 2, total // 8)
    load = lambda at: add(okept[at, :], ogot[at, :])
    split_rows(info, third, place, total // 2, rows, put_into(okeep), fold, load)


def unfold(got, first, rows, target):
    half = rows // 2
    columns = target.shape[1]
    target[:half, :] = got[first : first + half, :columns]
    target[half:, :] = got[first : first + half, columns:]


def ride(taps, send):
    rows, columns = taps.shape[0], send.shape[1]
    value = taps[...].astype(bf16)
    first = send.shape[0] - rows - rows // 2
    send[first : first + rows, :] = value[:, :columns]
    send[first + rows :, : columns // 2] = value[: rows // 2, columns:]
    send[first + rows :, columns // 2 :] = value[rows // 2 :, columns:]


def alight(taps, got, result):
    rows, columns = taps.shape[0], got.shape[1]
    first = got.shape[0] - rows - rows // 2
    value = taps[...].astype(bf16).astype(f32)
    half = rows // 2
    result[:, :columns] = value[:, :columns] + got[first : first + rows, :].astype(f32)
    result[:half, columns:] = value[:half, columns:] + got[
        first + rows :, : columns // 2
    ].astype(f32)
    result[half:, columns:] = value[half:, columns:] + got[
        first + rows :, columns // 2 :
    ].astype(f32)


def second_split(info, vkept, okept, got, *refs, third, rows):
    *taps, vkeep, okeep, send, flat = refs
    if taps:
        ride(taps[0], send)
    total = vkept.shape[0]
    bit = (third + 1) % 3
    left = [b for b in range(3) if b != third]
    load = lambda at: add(vkept[at, :], got[at, :])
    split_rows(info, bit, left.index(bit), total, rows, put_into(vkeep), put_into(send), load)
    unfold(got, total, total // 2, flat)
    fold = put_folded(send, total // 2, total // 8)
    load = lambda at: add(okept[at, :], flat[at, :])
    split_rows(info, bit, 0, total // 2, rows, put_into(okeep), fold, load)


def third_split(info, vkept, okept, got, *refs, third, rows):
    if third == 1:
        taps, vkeep, okeep, send, sums, flat = refs
        alight(taps, got, sums)
    elif third == 2:
        sums, vkeep, okeep, send, flat = refs
        ride(sums, send)
    else:
        vkeep, okeep, send, flat = refs
    total = vkept.shape[0]
    bit, place = ((third + 2) % 3, 0) if third else (3, 1)
    load = lambda at: add(vkept[at, :], got[at, :])
    split_rows(info, bit, place, total, rows, put_into(vkeep), put_into(send), load)
    unfold(got, total, total // 2, flat)
    if third:
        okeep[...] = add(okept[...], flat[...])
    else:
        fold = put_folded(send, total // 2, total // 8)
        load = lambda at: add(okept[at, :], flat[at, :])
        split_rows(info, bit, 0, total // 2, rows, put_into(okeep), fold, load)


def first_last_split(info, vkept, okept, got, keep, send, osum, flat, *, rows):
    total = vkept.shape[0]
    load = lambda at: add(vkept[at, :], got[at, :])
    split_rows(info, 2, 0, total, rows, put_into(keep), put_into(send), load)
    unfold(got, total, total // 2, flat)
    osum[...] = okept[...].astype(f32) + flat[...].astype(f32)


def last_split(info, vkept, okept, got, *refs, rows):
    keep, send = refs[len(refs) // 4 :][:2]
    total, columns = vkept.shape
    if len(refs) > 2:
        alight(refs[0], got, refs[3])
        keep[total // 2 :, :] = refs[3][...].astype(bf16)
        send[total // 2 :, :] = refs[3][...].astype(bf16)

    def put(target):
        def to(at, value):
            target[at : at + value.shape[0], : value.shape[1]] = value

        return to

    load = lambda at: add(vkept[at, :], got[at, :])
    split_rows(info, 3, 0, total, rows, put(keep), put(send), load)

    def side(target):
        def to(at, value):
            target[at : at + value.shape[0], columns:] = value

        return to

    split_rows(info, 3, 0, total, rows, side(keep), side(send), lambda at: okept[at, :])


def send_bit(value, bit):
    return swap(value, *every_bit()[bit])


def finish(value, rows):
    for bit in range(4, len(every_bit())):
        axis, place = every_bit()[bit]
        value = value.astype(bf16).reshape(-1, 2, rows, value.shape[1])
        mine = (lax.axis_index(axis) >> place) & 1
        keep, send = (
            lax.dynamic_index_in_dim(value, side, 1, keepdims=False) for side in (mine, 1 - mine)
        )
        shape = (-1, value.shape[-1])
        value = keep.reshape(shape).astype(f32) + send_bit(send.reshape(shape), bit).astype(f32)
    return value


def sigmoid(v):
    return 0.5 + 0.5 * jnp.tanh(0.5 * v)


def row_mask(info, first, rows, limit):
    place = info[0] + first + lax.broadcasted_iota(jnp.int32, (rows, 1), 0)
    return ((place >= 0) & (place < limit)).astype(f32)


def halves_at(info, half):
    return (
        pl.multiple_of(info[3] * half, half),
        pl.multiple_of((1 - info[3]) * half, half),
    )


def start_all(pairs, sem):
    copies = [pltpu.make_async_copy(a, b, sem.at[i]) for i, (a, b) in enumerate(pairs)]
    for c in copies:
        c.start()
    return copies


def prepare(info, ct, w_out, ct_to, w_to, sem):
    for c in start_all([(w_out, w_to), (ct, ct_to)], sem):
        c.wait()


def pick(info, x, ct, last, first, sem):
    count = x.shape[0]
    copies = [
        pltpu.make_async_copy(source.at[a : a + n], target.at[b : b + n], sem.at[i])
        for i, (source, target, a, b, n) in enumerate(
            (
                (x, last, count - WIDE, 0, WIDE),
                (ct, last, count - NEAR, WIDE, NEAR),
                (x, first, 0, 0, WIDE),
                (ct, first, 0, WIDE, NEAR),
            )
        )
    ]
    for c in copies:
        c.start()
    for c in copies:
        c.wait()


def pack(info, before, after, halo):
    rows = before.shape[0]
    halo[:rows, :] = before[...]
    halo[rows:, :] = after[...]


def upstream(info, own, other, w_out, x, wv, wg, full, pull, x_to, wv_to, wg_to, sem):
    count, half = own.shape
    copies = start_all([(x, x_to), (wv, wv_to), (wg, wg_to)], sem)
    mine, theirs = halves_at(info, half)
    full[:, pl.ds(mine, half)] = own[...]
    full[:, pl.ds(theirs, half)] = other[...]
    step = count // 2
    for c in range(0, count, step):
        pull[c : c + step, :] = dot(full[c : c + step, :], w_out[...], NT).astype(bf16)
    for c in copies:
        c.wait()


def upstream_ends(info, halo_own, halo_other, w_out, ends, edge):
    half = halo_own.shape[1]
    mine, theirs = halves_at(info, half)
    for a, at in ((halo_own, mine), (halo_other, theirs)):
        edge[:NEAR, pl.ds(at, half)] = a[WIDE : WIDE + NEAR, :]
        edge[NEAR:, pl.ds(at, half)] = a[2 * WIDE + NEAR :, :]
    ends[...] = dot(edge[...], w_out[...], NT)


def front(info, own, other, halo_own, halo_other, wv, wg, norm, rstd, hid, sig, slope):
    count, half = own.shape
    channels = wv.shape[1]
    mine, theirs = halves_at(info, half)

    def normalize(to, a, b):
        a, b = a.astype(f32), b.astype(f32)
        width = 2 * half
        mean = (jnp.sum(a, 1, keepdims=True) + jnp.sum(b, 1, keepdims=True)) / width
        a, b = a - mean, b - mean
        var = jnp.sum(a * a, 1, keepdims=True) + jnp.sum(b * b, 1, keepdims=True)
        inverse = lax.rsqrt(var / width + epsilon)
        norm[to, pl.ds(mine, half)] = (a * inverse).astype(bf16)
        norm[to, pl.ds(theirs, half)] = (b * inverse).astype(bf16)
        return inverse

    chunk = 128

    def body(i, _):
        at = pl.multiple_of(i * chunk, chunk)
        inverse = normalize(
            pl.ds(pl.multiple_of(WIDE + at, WIDE), chunk),
            own[pl.ds(at, chunk), :],
            other[pl.ds(at, chunk), :],
        )
        rstd[pl.ds(at, chunk), :] = jnp.broadcast_to(inverse, (chunk, LANES))
        return 0

    lax.fori_loop(0, count // chunk, body, 0, unroll=2)
    for to, at in ((0, 0), (WIDE + count, WIDE + NEAR)):
        normalize(pl.ds(to, WIDE), halo_own[at : at + WIDE, :], halo_other[at : at + WIDE, :])
    tile = channels // 3
    rows = count + 2 * WIDE
    step = rows // 2
    for n in range(0, channels, tile):
        cols = slice(n, n + tile)
        for c in range(0, rows, step):
            value = dot(norm[c : c + step, :], wv[:, cols])
            s = sigmoid(dot(norm[c : c + step, :], wg[:, cols]))
            keep = row_mask(info, c - WIDE, step, info[1])
            vs = value * s * keep
            hid[c : c + step, cols] = vs.astype(bf16)
            low, high = max(c, WIDE), min(c + step, WIDE + count)
            part = slice(low - c, high - c)
            sig[low - WIDE : high - WIDE, cols] = (s * keep)[part].astype(bf16)
            slope[low - WIDE : high - WIDE, cols] = (vs * (1.0 - s))[part].astype(bf16)


def tap_sums(source, base, groups, taps):
    sums = [None] * groups
    for residue in range(8):
        mine = list(range(residue, len(taps), 8))
        shifted = [
            source[pl.ds(base + 8 * i + residue, 8), :] for i in range(groups + len(mine) - 1)
        ]
        for i, k in enumerate(mine):
            for g in range(groups):
                term = shifted[g + i] * taps[k]
                sums[g] = term if sums[g] is None else sums[g] + term
    return sums


def tap_rows(taps, cols, reverse=False):
    values = taps[:, cols].astype(f32)
    order = range(taps.shape[0])
    return [
        jnp.broadcast_to(values[k : k + 1, :], (8, LANES))
        for k in (reversed(order) if reverse else order)
    ]


def lane_tile(n):
    return pl.ds(pl.multiple_of(n * LANES, LANES), LANES)


def paired(first, second):
    lane = lax.broadcasted_iota(jnp.int32, (first.shape[0], LANES), 1)
    return jnp.where(
        lane < LANES // 2,
        jnp.sum(first, axis=1, keepdims=True),
        jnp.sum(second, axis=1, keepdims=True),
    )


def depthwise(info, hid, taps, conv, stats, scratch, total, square):
    rows = conv.shape[0]
    skip = WIDE - NEAR - (taps.shape[0] - 1) // 2
    groups = 20
    total[...] = jnp.zeros_like(total)
    square[...] = jnp.zeros_like(square)

    def tile(n, _):
        cols = lane_tile(n)
        scratch[: hid.shape[0], :] = hid[:, cols].astype(f32)
        weights = tap_rows(taps, cols)

        def body(i, _):
            base = pl.multiple_of(i * 8 * groups, 8)
            for g, value in enumerate(tap_sums(scratch, base + skip, groups, weights)):
                at = pl.ds(base + 8 * g, 8)
                conv[at, cols] = value
                total[at, :] += value
                square[at, :] += value * value
            return 0

        lax.fori_loop(0, rows // (8 * groups), body, 0)
        return 0

    lax.fori_loop(0, conv.shape[1] // LANES, tile, 0)
    stats[...] = paired(total[...], square[...])


def moments(first, second, width):
    mean = (first[:, :1] + second[:, :1]) / width
    half = LANES // 2
    square = (first[:, half : half + 1] + second[:, half : half + 1]) / width
    return mean, lax.rsqrt(jnp.maximum(square - mean * mean, 0.0) + epsilon)


def swish(info, conv, pull, ends, own, other, swished, dswish, stats):
    count, channels = pull.shape

    def part(at, g, rows):
        to = pl.ds(at, rows)
        mean, inverse = moments(own[to, :], other[to, :], 2 * channels)
        zhat = (conv[to, :] - mean) * inverse
        s = sigmoid(zhat)
        zs = zhat * s
        d = g * (s + zs * (1.0 - s))
        dswish[to, :] = d
        stats[to, :] = paired(d, d * zhat)
        return zs.astype(bf16)

    part(0, ends[:NEAR, :], NEAR)
    part(NEAR + count, ends[NEAR:, :], NEAR)
    step = 64

    def body(i, _):
        at = pl.multiple_of(i * step, step)
        rows = pl.ds(at, step)
        g = pull[rows, :].astype(f32)
        swished[rows, :] = part(pl.multiple_of(at + NEAR, NEAR), g, step)
        return 0

    lax.fori_loop(0, count // step, body, 0, unroll=2)


def out_terms(info, full, swished, *refs, rows):
    halves, product = refs[:-1], refs[-1]
    width = full.shape[1]
    cols = swished.shape[1] // 3
    step = width // 4
    for c in range(0, width, step):
        product[c : c + step, :] = dot(full[:, c : c + step], swished[...], TN).astype(bf16)
    for i in range(3):
        load = lambda at: product[at, i * cols : (i + 1) * cols]
        keep, send = (put_into(half) for half in halves[2 * i : 2 * i + 2])
        split_rows(info, i, i, width, rows, keep, send, load)


def slopes(info, own, other, own2, other2, coef, width):
    rows = own.shape[0]
    mean, inverse = moments(own[...], other[...], width)
    half = LANES // 2
    shift = (own2[:, :1] + other2[:, :1]) / width
    cross = (own2[:, half : half + 1] + other2[:, half : half + 1]) / width
    inverse = inverse * row_mask(info, -NEAR, rows, info[2])
    tilt = inverse * inverse * cross
    coef[0] = jnp.broadcast_to(inverse, (rows, LANES))
    coef[1] = jnp.broadcast_to(tilt, (rows, LANES))
    coef[2] = jnp.broadcast_to(tilt * mean - inverse * shift, (rows, LANES))


def back(info, dswish, conv, taps, sig, slope, norm, *refs, third):
    rows, channels = dswish.shape
    count = sig.shape[0]
    width = 2 * channels
    if third == 0:
        *sums, dconv, dvg, product, coef, scratch = refs
        slopes(info, *sums, coef, width)
    else:
        coef, dconv, dvg, product, scratch = refs
    tiles = channels // LANES // 3
    groups = 16
    skip = NEAR - (taps.shape[0] - 1) // 2

    def tile(n, _):
        local = lane_tile(n)
        cols = lane_tile(third * tiles + n)
        d = (coef[0] * dswish[:, cols] - coef[1] * conv[:, cols] + coef[2]).astype(bf16)
        dconv[:, local] = d
        scratch[:rows, :] = d.astype(f32)
        weights = tap_rows(taps, cols, reverse=True)

        def body(i, _):
            base = pl.multiple_of(i * 8 * groups, 16)
            sums = tap_sums(scratch, base + skip, groups, weights)
            for g in range(0, groups, 2):
                at = pl.ds(base + 8 * g, 16)
                dh = jnp.concatenate(sums[g : g + 2], axis=0)
                dvg[at, local] = (dh * sig[at, cols]).astype(bf16)
                dvg[at, lane_tile(tiles + n)] = (dh * slope[at, cols]).astype(bf16)
            return 0

        lax.fori_loop(0, count // (8 * groups), body, 0)
        return 0

    lax.fori_loop(0, tiles, tile, 0)
    step = width // 4
    for c in range(0, width, step):
        r = dot(norm[WIDE : WIDE + count, c : c + step], dvg[...], TN)
        product[c : c + step, :] = r.astype(bf16)


def taps_sums(info, dconv, hid, out, scratch, total, *, third):
    rows, channels = dconv.shape
    count = rows - 2 * NEAR
    taps = total.shape[0]
    half = (taps - 1) // 2
    groups = 16
    tiles = channels // LANES

    def tile(n, _):
        local = lane_tile(n)
        cols = lane_tile(third * tiles + n)
        scratch[:rows, :] = dconv[:, local].astype(f32)
        total[...] = jnp.zeros_like(total)

        def body(i, _):
            base = pl.multiple_of(i * 8 * groups, 16)
            h = []
            for g in range(0, groups, 2):
                both = hid[pl.ds(pl.multiple_of(WIDE + base + 8 * g, 16), 16), cols].astype(f32)
                h += [both[:8], both[8:]]
            for residue in range(8):
                mine = list(range(residue, taps, 8))
                shifted = [
                    scratch[pl.ds(base + NEAR - half + 8 * g + residue, 8), :]
                    for g in range(groups + len(mine) - 1)
                ]
                for j, m in enumerate(mine):
                    term = shifted[j] * h[0]
                    for g in range(1, groups):
                        term = term + shifted[g + j] * h[g]
                    total[taps - 1 - m] += term
            return 0

        lax.fori_loop(0, count // (8 * groups), body, 0)
        out[:taps, local] = jnp.sum(total[...], axis=1)
        out[taps:, local] = jnp.zeros((out.shape[0] - taps, LANES), f32)
        return 0

    lax.fori_loop(0, tiles, tile, 0)


def add_taps(info, value, got, result):
    result[...] = value[...] + got[...]


def out_half(info, swished, w_out, result, *, own):
    half = result.shape[1]
    at = halves_at(info, half)[0 if own else 1]
    step = swished.shape[0] // 2
    for r in range(0, swished.shape[0], step):
        part = dot(swished[r : r + step, :], w_out[:, pl.ds(at, half)])
        result[r : r + step, :] = part.astype(result.dtype)


def norm_half(info, a, b, c, wv, wg, *results, own):
    half = results[0].shape[1]
    at = halves_at(info, half)[0 if own else 1]
    third = half // 3
    step = a.shape[0] // 2
    for n, result in enumerate(results):
        r = n * step
        total = None
        for i, dvg in enumerate((a, b, c)):
            cols = slice(i * third, (i + 1) * third)
            for j, w in enumerate((wv, wg)):
                part = dot(
                    dvg[r : r + step, j * third : (j + 1) * third], w[pl.ds(at, half), cols], NT
                )
                total = part if total is None else total + part
        result[...] = total.astype(result.dtype)


def norm_sums(info, mine0, mine1, got0, got1, norm, total, stats):
    count, half = total.shape
    at = halves_at(info, half)[0]
    step = 32
    for n, (mine, got) in enumerate(((mine0, got0), (mine1, got1))):
        start = n * count // 2

        def body(i, _):
            here = pl.multiple_of(i * step, step)
            rows, to = pl.ds(here, step), pl.ds(start + here, step)
            xhat = norm[pl.ds(WIDE + start + here, step), pl.ds(at, half)]
            d = mine[rows, :] + got[rows, :].astype(f32)
            total[to, :] = d
            stats[to, :] = paired(d, d * xhat.astype(f32))
            return 0

        lax.fori_loop(0, count // 2 // step, body, 0, unroll=2)


def written(result, buffer, sem, part):
    count, step = buffer.shape[0], buffer.shape[0] // sem.shape[0]
    copies = []
    for i in range(sem.shape[0]):
        rows = slice(i * step, (i + 1) * step)
        buffer[rows, :] = part(i * step, step)
        copies.append(pltpu.make_async_copy(buffer.at[rows], result.at[rows], sem.at[i]))
        copies[-1].start()
    for c in copies:
        c.wait()


def input_rows(info, ct, total, norm, rstd, own, other, result, buffer, sem):
    count, half = total.shape
    at = halves_at(info, half)[0]

    def part(first, step):
        rows = slice(first, first + step)
        xhat = norm[WIDE + first : WIDE + first + step, pl.ds(at, half)].astype(f32)
        sums = (own[rows, :] + other[rows, :]) / (2 * half)
        mean, cross = sums[:, :1], sums[:, LANES // 2 : LANES // 2 + 1]
        gradient = rstd[rows, :1] * (total[rows, :] - mean - xhat * cross)
        return (ct[rows, :].astype(f32) + gradient).astype(bf16)

    written(result, buffer, sem, part)


def output_rows(info, x, mine, got, result, buffer, sem):
    def part(first, step):
        rows = slice(first, first + step)
        return (x[rows, :].astype(f32) + mine[rows, :] + got[rows, :].astype(f32)).astype(bf16)

    written(result, buffer, sem, part)


def shards(inputs, lengths, cotangent, w_value, w_gate, kernel, w_out):
    x, ct = inputs[0], cotangent[0]
    count, channels = x.shape
    width = channels * lax.axis_size("tensor")
    core = lax.axis_index("tensor")
    peers = lax.axis_size("seq")
    every = every_bit()
    block = width >> len(every)
    taps = kernel.shape[0]
    info = jnp.stack(
        [lax.axis_index("seq") * count, lengths[0], jnp.int32(peers * count), core]
        + [(lax.axis_index(a) >> b) & 1 for a, b in every]
    ).astype(jnp.int32)

    up = [(i, i + 1) for i in range(peers - 1)]
    down = [(j, i) for i, j in up]
    x_other, ct_other = swap(x, "tensor"), swap(ct, "tensor")
    last, first, mark = run(
        pick,
        info,
        [x, ct],
        [((WIDE + NEAR, channels), bf16)] * 2,
        scratch=[pltpu.SemaphoreType.DMA((4,))],
        space=HBM,
    )
    before, after = lax.ppermute(last, "seq", up), lax.ppermute(first, "seq", down)
    ctv, wo, mark = run(
        prepare,
        info,
        [ct, w_out],
        [(ct.shape, bf16), (w_out.shape, bf16)],
        scratch=[pltpu.SemaphoreType.DMA((2,))],
        after=[mark],
        space=HBM,
    )
    halo, mark = run(
        pack, info, [before, after], [((2 * (WIDE + NEAR), channels), bf16)], after=[mark]
    )
    halo_other = swap(halo, "tensor")

    rows, ext = count + 2 * NEAR, count + 2 * WIDE
    full, pull, xv, wv, wg, mark = run(
        upstream,
        info,
        [ctv, ct_other, wo],
        [((count, width), bf16), ((count, channels), bf16)]
        + [(a.shape, bf16) for a in (x, w_value, w_gate)],
        scratch=[pltpu.SemaphoreType.DMA((3,))],
        after=[mark],
        far=[x, w_value, w_gate],
    )
    norm, rstd, hid, sig, slope, _ = run(
        front,
        info,
        [xv, x_other, halo, halo_other, wv, wg],
        [
            ((ext, width), bf16),
            ((count, LANES), f32),
            ((ext, channels), bf16),
            ((count, channels), bf16),
            ((count, channels), bf16),
        ],
        after=[mark],
    )
    row_sums = ((rows, LANES), f32)
    column = pltpu.VMEM((rows, LANES), f32)
    conv, stats, mark = run(
        depthwise,
        info,
        [hid, kernel],
        [((rows, channels), f32), row_sums],
        scratch=[pltpu.VMEM((ext + 16, LANES), f32), column, column],
    )
    stats_other = swap(stats, "tensor")
    ends, mark = run(
        upstream_ends,
        info,
        [halo, halo_other, wo],
        [((2 * NEAR, channels), f32)],
        scratch=[pltpu.VMEM((2 * NEAR, width), bf16)],
        after=[mark],
    )
    swished, dswish, stats2, _ = run(
        swish,
        info,
        [conv, pull, ends, stats, stats_other],
        [((count, channels), bf16), ((rows, channels), f32), row_sums],
    )
    stats2_other = swap(stats2, "tensor")

    third = channels // 3
    *out_parts, mark = run(
        functools.partial(out_terms, rows=block),
        info,
        [full, swished],
        [((width // 2, third), bf16)] * 6,
        scratch=[pltpu.VMEM((width, channels), bf16)],
    )
    out_got = [send_bit(out_parts[2 * i + 1], i) for i in range(3)]

    def out_part(own, mark):
        return run(
            functools.partial(out_half, own=own),
            info,
            [swished, wo],
            [((count, channels), f32 if own else bf16)],
            after=[mark],
        )

    dconvs, dvgs, kept, got = [], [], [], []
    sums = [stats, stats_other, stats2, stats2_other]
    for i in range(3):
        dconv, dvg, product, *coef, mark = run(
            functools.partial(back, third=i),
            info,
            [dswish, conv, kernel, sig, slope, norm, *sums],
            [((rows, third), bf16), ((count, 2 * third), bf16), ((width, 2 * third), bf16)]
            + [((3, rows, LANES), f32)] * (i == 0),
            scratch=[pltpu.VMEM((rows + 16, LANES), f32)],
            after=[mark],
        )
        if i == 0:
            sums = coef
        if i == 0:
            out_theirs, mark = out_part(False, mark)
            out_other = swap(out_theirs, "tensor")
            out_mine, mark = out_part(True, mark)
        previous = (i + 2) % 3
        vkeep, okeep, send, mark = run(
            functools.partial(first_split, third=i, rows=block),
            info,
            [product, out_parts[2 * previous], out_got[previous]],
            [
                ((width // 2, 2 * third), bf16),
                ((width // 4, third), bf16),
                ((width // 2 + width // 8, 2 * third), bf16),
            ],
            after=[mark, *out_got],
        )
        dconvs.append(dconv)
        dvgs.append(dvg)
        kept.append((vkeep, okeep))
        got.append(send_bit(send, i))

    extra = (taps + 1) * 3 // 2

    def second(i, mark, *riding):
        vkeep, okeep, send, mark = run(
            functools.partial(second_split, third=i, rows=block),
            info,
            [*kept[i], got[i], *riding],
            [
                ((width // 4, 2 * third), bf16),
                ((width // 8, third), bf16),
                ((width // 4 + width // 16 + extra * len(riding), 2 * third), bf16),
            ],
            scratch=[pltpu.VMEM((width // 4, third), bf16)],
            after=[mark],
        )
        kept[i], got[i] = (vkeep, okeep), send_bit(send, (i + 1) % 3)
        return mark

    def third_step(i, mark, *riding):
        off, on = (riding, ()) if i == 1 else ((), riding)
        vkeep, okeep, send, *sums, mark = run(
            functools.partial(third_split, third=i, rows=block),
            info,
            [*kept[i], got[i], *riding],
            [
                ((width // 8, 2 * third), bf16),
                ((width // 8 if i else width // 16, third), bf16),
                ((width // 8 + (extra * len(on) if i else width // 32), 2 * third), bf16),
            ]
            + [(r.shape, f32) for r in off],
            scratch=[pltpu.VMEM((width // 8, third), bf16)],
            after=[mark],
        )
        kept[i], got[i] = (vkeep, okeep), send_bit(send, (i + 2) % 3 if i else 3)
        return *sums, mark

    def last_step(i, mark, *riding):
        behind = (taps + 1) * len(riding)
        if i == 0:
            keep, send, osum, mark = run(
                functools.partial(first_last_split, rows=block),
                info,
                [*kept[0], got[0]],
                [((width // 16, 2 * third), bf16)] * 2 + [((width // 16, third), f32)],
                scratch=[pltpu.VMEM((width // 16, third), bf16)],
                after=[mark],
            )
            return keep.astype(f32) + send_bit(send, 2).astype(f32), osum, mark
        keep, send, mark = run(
            functools.partial(last_split, rows=block),
            info,
            [*kept[i], got[i], *riding],
            [((width // 16 + behind, 3 * third), bf16)] * 2,
            scratch=[pltpu.VMEM(r.shape, f32) for r in riding],
            after=[mark],
        )
        value = keep.astype(f32) + send_bit(send, 3).astype(f32)
        return value[: width // 16], value[width // 16 :], mark

    def norm_part(own, mark):
        return run(
            functools.partial(norm_half, own=own),
            info,
            [*dvgs, wv, wg],
            [((count // 2, channels), f32 if own else bf16)] * 2,
            after=[mark],
        )

    def taps_part(i, mark):
        return run(
            functools.partial(taps_sums, third=i),
            info,
            [dconvs[i], hid],
            [((taps + 1, third), f32)],
            scratch=[pltpu.VMEM((rows + 16, LANES), f32), pltpu.VMEM((taps, 8, LANES), f32)],
            after=[mark],
        )

    def final(kernel, args, mark):
        return run(
            kernel,
            info,
            args,
            [((count, channels), bf16)],
            scratch=[pltpu.VMEM((count, channels), bf16), pltpu.SemaphoreType.DMA((4,))],
            after=[mark],
            to=HBM,
        )

    parts = []
    for i in range(3):
        part, mark = taps_part(i, mark)
        parts.append(part)
    taps_own = jnp.concatenate(parts, axis=1)
    *mine, mark = norm_part(True, mark)
    mark = second(0, mark)
    taps_sum, mark = run(
        add_taps, info, [taps_own, send_bit(taps_own, 0)], [(taps_own.shape, f32)], after=[mark]
    )
    *theirs, mark = norm_part(False, mark)
    theirs = [swap(t, "tensor") for t in theirs]
    mark = second(1, mark, taps_sum)
    dnorm, stats3, mark = run(
        norm_sums,
        info,
        [*mine, *theirs, norm],
        [((count, channels), f32), ((count, LANES), f32)],
        after=[mark],
    )
    stats3_other = swap(stats3, "tensor")
    mark = second(2, mark)
    output, mark = final(output_rows, [x, out_mine, out_other], mark)
    input_gradient, mark = final(
        input_rows, [ct, dnorm, norm, rstd, stats3, stats3_other], mark
    )
    (mark,) = third_step(0, mark)
    taps_sum, mark = third_step(1, mark, taps_sum)
    (mark,) = third_step(2, mark, taps_sum)
    total0, out2, mark = last_step(0, mark)
    total1, _, mark = last_step(1, mark)
    total2, kernel_grad, mark = last_step(2, mark, taps_sum)
    totals = [finish(t, block) for t in (total0, total1, total2)]
    value_grad, gate_grad = (
        jnp.concatenate([t[:, j * third : (j + 1) * third] for t in totals], axis=1)
        for j in (0, 1)
    )
    out_grad = jnp.concatenate(
        [totals[1][:, 2 * third :], totals[2][:, 2 * third :], finish(out2, block)], axis=1
    ).T
    for bit in range(4, len(every)):
        kernel_grad = kernel_grad + send_bit(kernel_grad, bit)
    kernel_grad = kernel_grad[:taps]
    return (
        output[None],
        input_gradient[None],
        value_grad,
        gate_grad,
        kernel_grad,
        out_grad,
    )


def solution(mesh):
    return jax.shard_map(
        shards,
        mesh=mesh,
        in_specs=(
            P("dp", "seq", "tensor"),
            P("dp"),
            P("dp", "seq", "tensor"),
            P(None, "tensor"),
            P(None, "tensor"),
            P(None, "tensor"),
            P("tensor", None),
        ),
        out_specs=(
            P("dp", "seq", "tensor"),
            P("dp", "seq", "tensor"),
            P(("seq", "dp"), "tensor"),
            P(("seq", "dp"), "tensor"),
            P(None, "tensor"),
            P("tensor", ("seq", "dp")),
        ),
        check_vma=False,
    )
```
